32 devices in a mesh: section: 2 (over x), dp: 4 (over z), tensor: 4 (over y, core).
Axes of the slice: x: 2, y: 2, z: 4, core: 2. Of those that a mesh axis runs over, the one named last changes fastest.
Arguments:
- section_input: bfloat16 [2, 8192, 640], P(None, ('dp', 'tensor')), may hold values from -6 to 6
- cotangent: bfloat16 [2, 8192, 640], P(None, ('dp', 'tensor')), may hold values from -6 to 6
- segments: int32 [2, 8192], P(None, 'dp'), may hold values from 0 to 23, as said below
- query_weight: bfloat16 [2, 640, 1024], P('section', 'dp', 'tensor'), may hold values from -0.25 to 0.25
- key_weight: bfloat16 [2, 640, 256], P('section', 'dp'), may hold values from -0.25 to 0.25
- value_weight: bfloat16 [2, 640, 256], P('section', 'dp'), may hold values from -0.25 to 0.25
- output_weight: bfloat16 [2, 640, 1024], P('section', 'dp', 'tensor'), may hold values from -0.1875 to 0.1875
- gate_weight: bfloat16 [2, 640, 2048], P('section', 'dp', 'tensor'), may hold values from -0.25 to 0.25
- up_weight: bfloat16 [2, 640, 2048], P('section', 'dp', 'tensor'), may hold values from -0.25 to 0.25
- down_weight: bfloat16 [2, 640, 2048], P('section', 'dp', 'tensor'), may hold values from -0.125 to 0.125
- norm_gains: bfloat16 [2, 640, 4], P('section', 'dp'), may hold values from 0.5 to 1.5
- head_gains: bfloat16 [2, 256, 2], P('section', 'dp'), may hold values from 0.5 to 1.5
Outputs:
- section_output: float32 [2, 2, 8192, 640], P('section', None, ('dp', 'tensor'))
- input_grads: float32 [2, 2, 8192, 640], P('section', None, ('dp', 'tensor'))
- query_grad: float32 [2, 640, 1024], P('section', 'dp', 'tensor')
- key_grad: float32 [2, 640, 256], P('section', 'dp')
- value_grad: float32 [2, 640, 256], P('section', 'dp')
- output_grad: float32 [2, 640, 1024], P('section', 'dp', 'tensor')
- gate_grad: float32 [2, 640, 2048], P('section', 'dp', 'tensor')
- up_grad: float32 [2, 640, 2048], P('section', 'dp', 'tensor')
- down_grad: float32 [2, 640, 2048], P('section', 'dp', 'tensor')
- norm_gains_grad: float32 [2, 640, 4], P('section', 'dp')
- head_gains_grad: float32 [2, 256, 2], P('section', 'dp')
The draws below stay inside these ranges and needn't reach their ends.
Inputs may be any that keep to these rules, and one draw needn't show every extreme that they name: `segments`: segment numbers never fall along a micro-batch's tokens, every sequence of 2048 tokens begins with a new one, and no segment crosses from one sequence to the next.
All inputs are finite; a program needn't handle non-finite values.
Results may differ from the reference program's by a relative error of at most 0.029.
Values may be sent and summed in bfloat16 or wider, within the bound.
No kernel may reach another device: no remote copies, remote signals or barrier semaphores. Data moves between devices by JAX's collectives and lax.ppermute only.
A program may use at most 256 MiB of HBM per device.

```python
import jax
import jax.numpy as jnp
from jax import lax

D = 640
HQ = 4
HD = 256
FF = 2048
WIN = 512
LEN = 2048
M = 2
TOKENS = 8192


def draw_segments(key, part):
    key = jax.random.fold_in(key, 7)
    count = TOKENS // LEN
    head_key, tail_key = jax.random.split(key)
    heading = jax.random.randint(head_key, (M, count, 1), LEN // 10, LEN // 5 + 1)
    trailing = jax.random.randint(tail_key, (M, count, 1), LEN // 10, LEN // 5 + 1)
    places = jnp.arange(LEN, dtype=jnp.int32)[None, None, :]
    local = (places >= heading).astype(jnp.int32) + (places >= LEN - trailing).astype(jnp.int32)
    base = 3 * jnp.arange(M * count, dtype=jnp.int32).reshape(M, count, 1)
    return (base + local).reshape(M, count * LEN)


def steps_of(own_key, dims, cuts, low, high):
    factor_of, own = 1.0, jax.random.fold_in(own_key, 6)
    for axis_at, blocks in cuts:
        steps = jnp.exp(jax.random.uniform(jax.random.fold_in(own, axis_at), (blocks,), jnp.float32, low / len(cuts), high / len(cuts)))
        factor_of = factor_of * jnp.repeat(steps, dims[axis_at] // blocks).reshape([-1 if axis == axis_at else 1 for axis in range(len(dims))])
    return factor_of


def normal_values(rng, shape, width, limit, pieces=(), kind=jnp.bfloat16):
    entries = width * jax.random.normal(rng, shape, jnp.float32)
    if pieces:
        entries = entries * steps_of(rng, shape, pieces, -0.22, 0.18)
    return jnp.clip(entries, -limit, limit).astype(kind)


def setup_inputs(seed: int = 0) -> dict:
    key_list = jax.random.split(jax.random.key(seed), 13)
    return {
        "section_input": normal_values(key_list[0], (M, TOKENS, D), 1.0, 6.0, ((1, 16),)),
        "cotangent": normal_values(key_list[1], (M, TOKENS, D), 1.0, 6.0, ((1, 16),)),
        "segments": draw_segments(jax.random.fold_in(key_list[12], 71), 0),
        "query_weight": normal_values(key_list[3], (2, D, HQ * HD), D ** -0.5, 0.25, ((0, 2), (1, 4), (2, 4))),
        "key_weight": normal_values(key_list[4], (2, D, HD), D ** -0.5, 0.25, ((0, 2), (1, 4))),
        "value_weight": normal_values(key_list[5], (2, D, HD), D ** -0.5, 0.25, ((0, 2), (1, 4))),
        "output_weight": normal_values(key_list[6], (2, D, HQ * HD), (HQ * HD) ** -0.5, 0.1875, ((0, 2), (1, 4), (2, 4))),
        "gate_weight": normal_values(key_list[7], (2, D, FF), D ** -0.5, 0.25, ((0, 2), (1, 4), (2, 4))),
        "up_weight": normal_values(key_list[8], (2, D, FF), D ** -0.5, 0.25, ((0, 2), (1, 4), (2, 4))),
        "down_weight": normal_values(key_list[9], (2, D, FF), FF ** -0.5, 0.125, ((0, 2), (1, 4), (2, 4))),
        "norm_gains": jnp.clip(1.0 + 0.1 * jax.random.normal(key_list[10], (2, D, 4), jnp.float32), 0.5, 1.5).astype(jnp.bfloat16),
        "head_gains": jnp.clip(1.0 + 0.1 * jax.random.normal(key_list[11], (2, HD, 2), jnp.float32), 0.5, 1.5).astype(jnp.bfloat16),
    }


@jax.custom_vjp
def low(v):
    return lax.optimization_barrier(v.astype(jnp.bfloat16)).astype(jnp.float32)

@jax.custom_vjp
def low_back(v):
    return v

def low_keep(v):
    return (low(v), None)

def low_pass(kept, grad):
    return (grad,)

def back_keep(v):
    return (v, None)

def back_low(kept, grad):
    return (low(grad),)
low.defvjp(low_keep, low_pass)
low_back.defvjp(back_keep, back_low)

def highest(left, right):
    return jnp.dot(left, right, precision=lax.Precision.HIGHEST)

def rms_norm(values, gain):
    return values * lax.rsqrt(lax.optimization_barrier(jnp.mean(values * values, axis=-1, keepdims=True)) + 1e-06) * gain

def gelu_tanh(values):
    return 0.5 * values * (1.0 + jnp.tanh(0.7978845608028654 * (values + 0.044715 * values * values * values)))

def rotate(values, cosine, sine):
    half = values.shape[-1] // 2
    first_half = values[..., :half]
    second_half = values[..., half:]
    return jnp.concatenate([first_half * cosine - second_half * sine, second_half * cosine + first_half * sine], axis=-1)

def positions_of(segments):
    count = segments.shape[0]
    places = jnp.arange(count, dtype=jnp.int32)
    before = jnp.concatenate([segments[:1] - 1, segments[:-1]])
    starts = lax.cummax(jnp.where(segments != before, places, 0), axis=0)
    return places - starts

def rotary_tables(segments):
    half = HD // 2
    inverse = jnp.exp(-jnp.log(10000.0) * jnp.arange(half, dtype=jnp.float32) / half)
    angle = positions_of(segments).astype(jnp.float32)[:, None] * inverse[None, :]
    return (jnp.cos(angle), jnp.sin(angle))

def window_mask(query_segments, key_segments):
    query_place = jnp.arange(WIN, dtype=jnp.int32)[:, None] + WIN
    key_place = jnp.arange(2 * WIN, dtype=jnp.int32)[None, :]
    inside = (key_place <= query_place) & (query_place - key_place < WIN)
    return inside & (query_segments[:, None] == key_segments[None, :])

def attend(queries, key_rows, value_rows, segments):
    rows = queries.shape[0]
    pad_keys = jnp.concatenate([jnp.zeros((WIN, HD), jnp.float32), key_rows])
    pad_values = jnp.concatenate([jnp.zeros((WIN, HD), jnp.float32), value_rows])
    pad_segments = jnp.concatenate([jnp.full((WIN,), -1, jnp.int32), segments])

    def one_block(block):
        start = (block * WIN).astype(jnp.int32)
        query_block = lax.dynamic_slice_in_dim(queries, start, WIN, 0)
        key_block = lax.dynamic_slice_in_dim(pad_keys, start, 2 * WIN, 0)
        value_block = lax.dynamic_slice_in_dim(pad_values, start, 2 * WIN, 0)
        allowed = window_mask(lax.dynamic_slice_in_dim(segments, start, WIN, 0), lax.dynamic_slice_in_dim(pad_segments, start, 2 * WIN, 0))
        scores = low_back(jnp.einsum('qhd,kd->hqk', query_block, key_block, precision=lax.Precision.HIGHEST) * 0.0625)
        scores = jnp.where(allowed[None], scores, -1e+30)
        largest = lax.optimization_barrier(jnp.max(scores, axis=-1, keepdims=True))
        raised = jnp.exp(scores - largest)
        probs = raised / lax.optimization_barrier(jnp.sum(raised, axis=-1, keepdims=True))
        mixed = jnp.einsum('hqk,kd->qhd', low(probs), value_block, precision=lax.Precision.HIGHEST)
        return low(low_back(mixed))
    blocks = lax.map(jax.checkpoint(one_block), jnp.arange(rows // WIN, dtype=jnp.int32))
    return blocks.reshape(rows, HQ * HD)

def layer(layer_in, weights, segments):
    query_w, key_w, value_w, output_w, gate_w, up_w, down_w, gains, head_gains = weights
    rows = layer_in.shape[0]
    cosine, sine = rotary_tables(segments)
    normed = low(rms_norm(layer_in, gains[:, 0]))
    query_raw = low_back(highest(normed, query_w)).reshape(rows, HQ, HD)
    key_raw = low_back(highest(normed, key_w))
    value_rows = low(low_back(highest(normed, value_w)))
    queries = low(rotate(rms_norm(query_raw, head_gains[:, 0]), cosine[:, None, :], sine[:, None, :]))
    key_rows = low(rotate(rms_norm(key_raw, head_gains[:, 1]), cosine, sine))
    mixed = attend(queries, key_rows, value_rows, segments)
    branch = low_back(highest(mixed, output_w.T))
    middle = layer_in + rms_norm(branch, gains[:, 1])
    normed_two = low(rms_norm(middle, gains[:, 2]))
    gate = low_back(highest(normed_two, gate_w))
    upward = low_back(highest(normed_two, up_w))
    hidden = low(gelu_tanh(gate) * upward)
    branch_two = low_back(highest(hidden, down_w.T))
    return middle + rms_norm(branch_two, gains[:, 3])

def reference(section_input, cotangent, segments, query_weight, key_weight, value_weight, output_weight, gate_weight, up_weight, down_weight, norm_gains, head_gains):
    params = tuple((weight.astype(jnp.float32) for weight in (query_weight, key_weight, value_weight, output_weight, gate_weight, up_weight, down_weight, norm_gains, head_gains)))
    inputs = section_input.astype(jnp.float32)
    probe = jnp.zeros_like(inputs)

    def forward(inputs, probe, params):
        first_params = tuple((weight[0] for weight in params))
        second_params = tuple((weight[1] for weight in params))
        firsts = []
        seconds = []
        for micro in range(M):
            first_out = layer(inputs[micro], first_params, segments[micro])
            second_in = low(low_back(first_out)) + probe[micro]
            firsts.append(first_out)
            seconds.append(layer(second_in, second_params, segments[micro]))
        return (jnp.stack(firsts), jnp.stack(seconds))
    (first_outs, second_outs), pullback = jax.vjp(forward, inputs, probe, params)
    grad_inputs, grad_probe, grad_params = pullback((jnp.zeros_like(first_outs), cotangent.astype(jnp.float32)))
    return (jnp.stack([first_outs, second_outs]), jnp.stack([grad_inputs, grad_probe]), grad_params[0], grad_params[1], grad_params[2], grad_params[3], grad_params[4], grad_params[5], grad_params[6], grad_params[7], grad_params[8])
```

```python
import jax
import jax.numpy as jnp
from jax import lax
from jax.experimental import pallas as pl
from jax.experimental.pallas import tpu as pltpu
from jax.sharding import PartitionSpec as P

HD = 256
HALF = HD // 2
WIN = 512
BLK = 256
EPS = 1e-06
F32 = jnp.float32
BF16 = jnp.bfloat16
LIMIT = 50 * 1024 * 1024


def nn(a, b):
    return lax.dot_general(a, b, (((1,), (0,)), ((), ())), preferred_element_type=F32)


def nt(a, b):
    return lax.dot_general(a, b, (((1,), (1,)), ((), ())), preferred_element_type=F32)


def tn(a, b):
    return lax.dot_general(a, b, (((0,), (0,)), ((), ())), preferred_element_type=F32)


def rms(values, gain):
    return values * lax.rsqrt(jnp.mean(values * values, axis=-1, keepdims=True) + EPS) * gain


def rms_back(grad, values, gain):
    scale = lax.rsqrt(jnp.mean(values * values, axis=-1, keepdims=True) + EPS)
    unit = values * scale
    scaled = grad * gain
    inner = jnp.mean(scaled * unit, axis=-1, keepdims=True)
    return scale * (scaled - unit * inner), jnp.sum(grad * unit, axis=0, keepdims=True)


def rot(values, cosine, sine):
    a, b = values[:, :HALF], values[:, HALF:]
    return jnp.concatenate([a * cosine - b * sine, b * cosine + a * sine], axis=-1)


def rot_back(grad, cosine, sine):
    a, b = grad[:, :HALF], grad[:, HALF:]
    return jnp.concatenate([a * cosine + b * sine, b * cosine - a * sine], axis=-1)


GELU_A = 0.7978845608028654
GELU_B = 0.044715


def triangle():
    row = lax.broadcasted_iota(jnp.int32, (BLK, BLK), 0)
    column = lax.broadcasted_iota(jnp.int32, (BLK, BLK), 1)
    return column <= row


def tiles(block):
    rows = slice(block * BLK, (block + 1) * BLK)
    other = slice((1 - block) * BLK, (2 - block) * BLK)
    return rows, other, block == 1


def masks(block, lower, seg_col, seg_own, seg_prev):
    rows, other, own = tiles(block)
    mine = seg_col[rows, :]
    diagonal = mine == jnp.where(lower, seg_own[:, rows], seg_prev[:, rows])
    rest = mine == (seg_own if own else seg_prev)[:, other]
    return diagonal, rest


def prep_kernel(x, gains, heads, kvw, cosine, sine, normed, kraw, kv):
    rows = rms(x[...], gains[0:1, :]).astype(BF16)
    normed[...] = rows
    raw = nn(rows, kvw[:, :HD])
    kraw[...] = raw
    kv[:, :HD] = rot(rms(raw, heads[1:2, :]), cosine[...], sine[...]).astype(BF16)
    kv[:, HD:] = nn(rows, kvw[:, HD : 2 * HD]).astype(BF16)


def attend_kernel(
    x, normed, gains, heads, qo, own, prev, cosine, sine, seg_col, seg_own, seg_prev,
    qraw, q, mixed, lse, branch, middle, normed_two,
):
    step = pl.program_id(0)
    raw = nn(normed[...], qo[0, 0])
    qraw[0] = raw
    turned = rot(rms(raw, heads[0:1, :]), cosine[...], sine[...]).astype(BF16)
    q[0] = turned * jnp.asarray(0.0625, BF16)
    lower = triangle()
    for block in range(2):
        rows, other, is_own = tiles(block)
        diagonal, rest = masks(block, lower, seg_col[...], seg_own[...], seg_prev[...])
        query = q[0, rows, :]
        far = own if is_own else prev
        near_scores = jnp.where(
            lower, nt(query, own[rows, :HD]), nt(query, prev[rows, :HD])
        )
        near_scores = jnp.where(diagonal, near_scores, -1e30)
        far_scores = jnp.where(rest, nt(query, far[other, :HD]), -1e30)
        largest = jnp.maximum(
            jnp.max(near_scores, axis=-1, keepdims=True),
            jnp.max(far_scores, axis=-1, keepdims=True),
        )
        near = jnp.exp(near_scores - largest)
        rest_p = jnp.exp(far_scores - largest)
        total = jnp.sum(near, axis=-1, keepdims=True) + jnp.sum(rest_p, axis=-1, keepdims=True)
        inverse = 1.0 / total
        near = near * inverse
        rest_p = (rest_p * inverse).astype(BF16)
        near_own = jnp.where(lower, near, 0.0).astype(BF16)
        near_prev = jnp.where(lower, 0.0, near).astype(BF16)
        mixed[0, rows, :] = (
            nn(near_own, own[rows, HD:]) + nn(near_prev, prev[rows, HD:]) + nn(rest_p, far[other, HD:])
        ).astype(BF16)
        lse[0, rows, :] = largest + jnp.log(total)
    part = nt(mixed[0], qo[0, 1])

    @pl.when(step == 0)
    def _():
        branch[...] = part

    @pl.when(step > 0)
    def _():
        branch[...] += part

    @pl.when(step == pl.num_programs(0) - 1)
    def _():
        mid = x[...] + rms(branch[...], gains[1:2, :])
        middle[...] = mid
        normed_two[...] = rms(mid, gains[2:3, :]).astype(BF16)


def feed_kernel(normed_two, ff, middle, gains, gate_out, up_out, branch_two, out):
    step = pl.program_id(0)
    rows = normed_two[...]
    gate = nn(rows, ff[0, 0])
    upward = nn(rows, ff[0, 1])
    gate_out[0] = gate.astype(BF16)
    up_out[0] = upward.astype(BF16)
    wave = jnp.tanh(GELU_A * (gate + GELU_B * gate * gate * gate))
    hidden = (0.5 * gate * (1.0 + wave) * upward).astype(BF16)
    part = nt(hidden, ff[0, 2])

    @pl.when(step == 0)
    def _():
        branch_two[...] = part

    @pl.when(step > 0)
    def _():
        branch_two[...] += part

    @pl.when(step == pl.num_programs(0) - 1)
    def _():
        out[...] = middle[...] + rms(branch_two[...], gains[3:4, :])


def feed_back_kernel(
    grad, branch_two, middle, branch, normed_two, gains, gate_in, up_in, ff,
    send, keep, grad_middle, grad_branch, gain_grads, incoming, incoming_t, rows_t, total,
):
    step = pl.program_id(0)

    @pl.when(step == 0)
    def _():
        values, gain = rms_back(grad[...], branch_two[...], gains[3:4, :])
        incoming[...] = values.astype(BF16)
        incoming_t[...] = values.T.astype(BF16)
        rows_t[...] = normed_two[...].T
        gain_grads[2:3, :] = gain
        gain_grads[3:4, :] = jnp.zeros_like(gain)

    gate = gate_in[0].astype(F32)
    upward = up_in[0].astype(F32)
    square = gate * gate
    wave = jnp.tanh(GELU_A * gate * (1.0 + GELU_B * square))
    bell = 0.5 * (1.0 + wave)
    active = gate * bell
    slope = bell + 0.5 * gate * (1.0 - wave * wave) * (GELU_A * (1.0 + 3.0 * GELU_B * square))
    grad_hidden = nn(incoming[...], ff[0, 2])
    grad_up = (grad_hidden * active).astype(BF16)
    grad_gate = (grad_hidden * upward * slope).astype(BF16)
    hidden = (active * upward).astype(BF16)

    def store(place):
        place[0, 0] = nn(rows_t[...], grad_gate).astype(BF16)
        place[0, 1] = nn(rows_t[...], grad_up).astype(BF16)
        place[0, 2] = nn(incoming_t[...], hidden).astype(BF16)

    @pl.when(step < 2)
    def _():
        store(send)

    @pl.when(step >= 2)
    def _():
        store(keep)

    part = nt(grad_gate, ff[0, 0]) + nt(grad_up, ff[0, 1])

    @pl.when(step == 0)
    def _():
        total[...] = part

    @pl.when(step > 0)
    def _():
        total[...] += part

    @pl.when(step == pl.num_programs(0) - 1)
    def _():
        from_norm, gain = rms_back(total[...], middle[...], gains[2:3, :])
        gain_grads[1:2, :] = gain
        mid = grad[...] + from_norm
        grad_middle[...] = mid
        values, gain = rms_back(mid, branch[...], gains[1:2, :])
        gain_grads[0:1, :] = gain
        grad_branch[...] = values.astype(BF16)


def attend_back_kernel(
    grad_branch, normed, heads, qo, q, qraw, mixed, lse, own, prev, cosine, sine,
    seg_col, seg_own, seg_prev,
    send, keep, kv_own, kv_prev, grad_normed, head_grad, grad_t, rows_t, prev_sum, grad_q,
):
    step = pl.program_id(0)

    @pl.when(step == 0)
    def _():
        grad_t[...] = grad_branch[...].T
        rows_t[...] = normed[...].T
        kv_own[...] = jnp.zeros_like(kv_own)
        prev_sum[...] = jnp.zeros_like(prev_sum)
        grad_normed[...] = jnp.zeros_like(grad_normed)
        head_grad[...] = jnp.zeros_like(head_grad)

    grad_mixed = nn(grad_branch[...], qo[0, 1]).astype(BF16)
    lower = triangle()
    for block in range(2):
        rows, other, is_own = tiles(block)
        diagonal, rest = masks(block, lower, seg_col[...], seg_own[...], seg_prev[...])
        query = q[0, rows, :]
        incoming = grad_mixed[rows, :]
        far = own if is_own else prev
        far_sum = kv_own if is_own else prev_sum
        log_total = lse[0, rows, :]
        near_scores = jnp.where(
            lower, nt(query, own[rows, :HD]), nt(query, prev[rows, :HD])
        )
        near = jnp.exp(jnp.where(diagonal, near_scores, -1e30) - log_total)
        rest_p = jnp.exp(jnp.where(rest, nt(query, far[other, :HD]), -1e30) - log_total)
        near_grad = jnp.where(
            lower, nt(incoming, own[rows, HD:]), nt(incoming, prev[rows, HD:])
        )
        rest_grad = nt(incoming, far[other, HD:])
        inner = jnp.sum(near * near_grad, axis=-1, keepdims=True) + jnp.sum(
            rest_p * rest_grad, axis=-1, keepdims=True
        )
        near_score = near * (near_grad - inner)
        rest_score = (rest_p * (rest_grad - inner)).astype(BF16)
        score_own = jnp.where(lower, near_score, 0.0).astype(BF16)
        score_prev = jnp.where(lower, 0.0, near_score).astype(BF16)
        near_own = jnp.where(lower, near, 0.0).astype(BF16)
        near_prev = jnp.where(lower, 0.0, near).astype(BF16)
        rest_p = rest_p.astype(BF16)
        grad_q[rows, :] = 0.0625 * (
            nn(score_own, own[rows, :HD])
            + nn(score_prev, prev[rows, :HD])
            + nn(rest_score, far[other, :HD])
        )
        kv_own[rows, :HD] += tn(score_own, query)
        prev_sum[rows, :HD] += tn(score_prev, query)
        far_sum[other, :HD] += tn(rest_score, query)
        kv_own[rows, HD:] += tn(near_own, incoming)
        prev_sum[rows, HD:] += tn(near_prev, incoming)
        far_sum[other, HD:] += tn(rest_p, incoming)
    values, gain = rms_back(
        rot_back(grad_q[...], cosine[...], sine[...]), qraw[0], heads[0:1, :]
    )
    head_grad[0:1, :] += gain
    grad_raw = values.astype(BF16)
    grad_normed[...] += nt(grad_raw, qo[0, 0])

    def store(place):
        place[0, 0] = nn(rows_t[...], grad_raw).astype(BF16)
        place[0, 1] = nn(grad_t[...], mixed[0]).astype(BF16)

    @pl.when(step < 2)
    def _():
        store(send)

    @pl.when(step >= 2)
    def _():
        store(keep)

    @pl.when(step == pl.num_programs(0) - 1)
    def _():
        kv_prev[...] = prev_sum[...].astype(BF16)


def finish_kernel(
    kv_own, kv_next, kraw, normed, kvw, heads, gains, x, grad_normed, grad_middle, cosine, sine,
    kv_grad, grad_x, gain_grad, head_grad,
):
    total = kv_own[...] + kv_next[...].astype(F32)
    values, gain = rms_back(
        rot_back(total[:, :HD], cosine[...], sine[...]), kraw[...], heads[1:2, :]
    )
    head_grad[...] = gain
    grad_key = values.astype(BF16)
    grad_value = total[:, HD:].astype(BF16)
    rows = normed[...]
    kv_grad[:, :HD] = tn(rows, grad_key).astype(BF16)
    kv_grad[:, HD:] = tn(rows, grad_value).astype(BF16)
    from_all = grad_normed[...] + nt(grad_key, kvw[:, :HD]) + nt(grad_value, kvw[:, HD : 2 * HD])
    from_norm, gain = rms_back(from_all, x[...], gains[0:1, :])
    gain_grad[...] = gain
    grad_x[...] = grad_middle[...] + from_norm


def whole(shape):
    zeros = (0,) * len(shape)
    return pl.BlockSpec(shape, lambda *at: zeros)


def slot(shape):
    zeros = (0,) * (len(shape) - 1)
    return pl.BlockSpec((1,) + tuple(shape[1:]), lambda at: (at,) + zeros)


def early(shape):
    zeros = (0,) * (len(shape) - 1)
    return pl.BlockSpec((1,) + tuple(shape[1:]), lambda at: (jnp.minimum(at, 1),) + zeros)


def late(shape):
    zeros = (0,) * (len(shape) - 1)
    return pl.BlockSpec((1,) + tuple(shape[1:]), lambda at: (jnp.maximum(at - 2, 0),) + zeros)


def run(kernel, grid, ins, outs, scratch=(), macs=0):
    arrays = [a for a, _ in ins]
    moved = sum(a.size * a.dtype.itemsize for a in arrays)
    return pl.pallas_call(
        kernel,
        grid=grid,
        in_specs=[spec(a.shape) for a, spec in ins],
        out_specs=[spec(shape) for shape, _, spec in outs],
        out_shape=[jax.ShapeDtypeStruct(shape, kind) for shape, kind, _ in outs],
        scratch_shapes=list(scratch),
        compiler_params=pltpu.CompilerParams(vmem_limit_bytes=LIMIT),
        cost_estimate=pl.CostEstimate(
            flops=2 * macs, bytes_accessed=2 * moved, transcendentals=0
        ),
    )(*arrays)


def forward_layer(x, w, common):
    cosine, sine, seg_col, seg_own, seg_prev = common
    qo, kvw, ff, gains, heads = w
    rows, width = x.shape
    slots, units = ff.shape[0], ff.shape[3]
    normed, kraw, kv = run(
        prep_kernel, (1,),
        [(x, whole), (gains, whole), (heads, whole), (kvw, whole), (cosine, whole), (sine, whole)],
        [((rows, width), BF16, whole), ((rows, HD), F32, whole), ((rows, 2 * HD), BF16, whole)],
        macs=rows * width * 2 * HD,
    )
    count = lax.axis_size("tensor")
    prev = lax.ppermute(kv, "tensor", [(i, i + 1) for i in range(count - 1)])
    qraw, q, mixed, lse, branch, middle, normed_two = run(
        attend_kernel, (slots,),
        [(x, whole), (normed, whole), (gains, whole), (heads, whole), (qo, slot), (kv, whole),
         (prev, whole), (cosine, whole), (sine, whole), (seg_col, whole), (seg_own, whole),
         (seg_prev, whole)],
        [((slots, rows, HD), F32, slot), ((slots, rows, HD), BF16, slot),
         ((slots, rows, HD), BF16, slot), ((slots, rows, 1), F32, slot),
         ((rows, width), F32, whole), ((rows, width), F32, whole), ((rows, width), BF16, whole)],
        macs=slots * rows * HD * (2 * width + 3 * WIN),
    )
    gate, upward, branch_two, out = run(
        feed_kernel, (slots,),
        [(normed_two, whole), (ff, slot), (middle, whole), (gains, whole)],
        [((slots, rows, units), BF16, slot), ((slots, rows, units), BF16, slot),
         ((rows, width), F32, whole), ((rows, width), F32, whole)],
        macs=slots * rows * width * units * 3,
    )
    kept = (x, normed, kraw, kv, prev, qraw, q, mixed, lse, branch, middle, normed_two, gate,
            upward, branch_two)
    return out, kept


def backward_layer(grad, w, kept, common):
    cosine, sine, seg_col, seg_own, seg_prev = common
    qo, kvw, ff, gains, heads = w
    (x, normed, kraw, kv, prev, qraw, q, mixed, lse, branch, middle, normed_two, gate, upward,
     branch_two) = kept
    rows, width = x.shape
    slots, units = ff.shape[0], ff.shape[3]
    half = slots // 2
    ff_send, ff_keep, grad_middle, grad_branch, gain_three = run(
        feed_back_kernel, (slots,),
        [(grad, whole), (branch_two, whole), (middle, whole), (branch, whole),
         (normed_two, whole), (gains, whole), (gate, slot), (upward, slot), (ff, slot)],
        [((half, 3, width, units), BF16, early), ((half, 3, width, units), BF16, late),
         ((rows, width), F32, whole), ((rows, width), BF16, whole), ((4, width), F32, whole)],
        [pltpu.VMEM((rows, width), BF16), pltpu.VMEM((width, rows), BF16),
         pltpu.VMEM((width, rows), BF16), pltpu.VMEM((rows, width), F32)],
        macs=slots * rows * width * units * 6,
    )
    qo_send, qo_keep, kv_own, kv_prev, grad_normed, head_query = run(
        attend_back_kernel, (slots,),
        [(grad_branch, whole), (normed, whole), (heads, whole), (qo, slot), (q, slot),
         (qraw, slot), (mixed, slot), (lse, slot), (kv, whole), (prev, whole), (cosine, whole),
         (sine, whole), (seg_col, whole), (seg_own, whole), (seg_prev, whole)],
        [((half, 2, width, HD), BF16, early), ((half, 2, width, HD), BF16, late),
         ((rows, 2 * HD), F32, whole), ((rows, 2 * HD), BF16, whole), ((rows, width), F32, whole),
         ((1, HD), F32, whole)],
        [pltpu.VMEM((width, rows), BF16), pltpu.VMEM((width, rows), BF16),
         pltpu.VMEM((rows, 2 * HD), F32), pltpu.VMEM((rows, HD), F32)],
        macs=slots * rows * HD * (4 * width + 8 * WIN),
    )
    count = lax.axis_size("tensor")
    kv_next = lax.ppermute(kv_prev, "tensor", [(i + 1, i) for i in range(count - 1)])
    kv_grad, grad_x, gain_one, head_key = run(
        finish_kernel, (1,),
        [(kv_own, whole), (kv_next, whole), (kraw, whole), (normed, whole), (kvw, whole),
         (heads, whole), (gains, whole), (x, whole), (grad_normed, whole), (grad_middle, whole),
         (cosine, whole), (sine, whole)],
        [((width, 2 * HD), BF16, whole), ((rows, width), F32, whole), ((1, width), F32, whole),
         ((1, HD), F32, whole)],
        macs=rows * width * 4 * HD,
    )
    gain_rows = jnp.concatenate([gain_one, gain_three[:3]], axis=0)
    head_rows = jnp.concatenate([head_query, head_key], axis=0)
    return grad_x, (ff_send, ff_keep), (qo_send, qo_keep), kv_grad, gain_rows, head_rows


def tensor_pairs(bit):
    return [(i, i ^ bit) for i in range(lax.axis_size("tensor"))]


def rows_over_dp(part):
    count = lax.axis_size("dp")
    if count > 4:
        return lax.all_gather(part, "dp", axis=1, tiled=True)
    me = lax.axis_index("dp")
    rows = part.shape[1]
    full = jnp.zeros((part.shape[0], count * rows, part.shape[2]), part.dtype)
    pieces = [part] + [
        lax.ppermute(part, "dp", [(i, (i + shift) % count) for i in range(count)])
        for shift in range(1, count)
    ]
    for shift, piece in enumerate(pieces):
        full = lax.dynamic_update_slice_in_dim(full, piece, (me + count - shift) % count * rows, 1)
    return full


def slots_over_tensor(part):
    across = lax.ppermute(part, "tensor", tensor_pairs(2))
    beside = lax.ppermute(part, "tensor", tensor_pairs(1))
    corner = lax.ppermute(across, "tensor", tensor_pairs(1))
    return jnp.stack([beside, corner, part, across])


def add(left, right):
    return (left.astype(F32) + right.astype(F32)).astype(BF16)


def summed_over_dp(full):
    count = lax.axis_size("dp")
    if count > 4:
        return lax.psum_scatter(full, "dp", scatter_dimension=1, tiled=True).astype(F32)
    me = lax.axis_index("dp")
    rows = full.shape[1] // count

    def rows_of(owner):
        return lax.dynamic_slice_in_dim(full, owner % count * rows, rows, 1)

    total = rows_of(me).astype(F32)
    for shift in range(1, count):
        total += lax.ppermute(
            rows_of(me + shift), "dp", [(i, (i + shift) % count) for i in range(count)]
        ).astype(F32)
    return total


def to_section(part, layer):
    return part + lax.ppermute(part.astype(BF16), "section", [(1 - layer, layer)]).astype(F32)


def reduce_slots(sends, layer):
    send, keep = sends
    arrived = lax.ppermute(send, "tensor", tensor_pairs(1))
    across = add(keep[1], arrived[1])
    mine = add(keep[0], arrived[0])
    mine = add(mine, lax.ppermute(across, "tensor", tensor_pairs(2)))
    return to_section(summed_over_dp(mine), layer)


def reduce_shared(kv_grad, gain_rows, head_rows, layer):
    count = lax.axis_size("dp")
    width = kv_grad.shape[0]
    per_head = HD // count
    head_cols = head_rows.T.reshape(count, per_head, 2)
    head_cols = jnp.pad(head_cols, ((0, 0), (0, width // count - per_head), (0, 0)))
    small = jnp.concatenate([gain_rows.T, head_cols.reshape(width, 2)], axis=1)
    small = jnp.pad(small, ((0, 0), (0, 122))).astype(BF16)
    part = summed_over_dp(jnp.concatenate([kv_grad, small], axis=1)[None])[0]
    for bit in (1, 2):
        part = part + lax.ppermute(part.astype(BF16), "tensor", tensor_pairs(bit)).astype(F32)
    return to_section(part, layer)


def body(
    section_input, cotangent, segments, query_weight, key_weight, value_weight, output_weight,
    gate_weight, up_weight, down_weight, norm_gains, head_gains,
):
    section = lax.axis_index("section")
    place = lax.axis_index("tensor")
    first = section == 0
    rows = section_input.shape[1]
    per_head = head_gains.shape[1]
    local = norm_gains.shape[1]

    small = jnp.concatenate(
        [norm_gains[0], jnp.pad(head_gains[0], ((0, local - per_head), (0, 0)))], axis=1
    )
    small = jnp.pad(small, ((0, 0), (0, 122)))
    shared = jnp.concatenate([key_weight[0], value_weight[0], small], axis=1)[None]
    pairs = jnp.stack([query_weight[0], output_weight[0]])
    feeds = jnp.stack([gate_weight[0], up_weight[0], down_weight[0]])

    def both(part):
        other = lax.ppermute(part, "section", [(0, 1), (1, 0)])
        return jnp.where(first, part, other), jnp.where(first, other, part)

    shared_l, pairs_l, feeds_l = both(shared), both(pairs), both(feeds)
    weights = []
    for layer in range(2):
        common_w = rows_over_dp(shared_l[layer])[0]
        qo = slots_over_tensor(rows_over_dp(pairs_l[layer]))
        ff = slots_over_tensor(rows_over_dp(feeds_l[layer]))
        gains = common_w[:, 2 * HD : 2 * HD + 4].astype(F32).T
        count = lax.axis_size("dp")
        heads = common_w[:, 2 * HD + 4 : 2 * HD + 6].reshape(count, local, 2)[:, :per_head]
        heads = heads.reshape(HD, 2).astype(F32).T
        weights.append((qo, common_w, ff, gains, heads))

    own_segments = lax.dynamic_index_in_dim(segments, section, 0, keepdims=False)
    length = own_segments.shape[0]
    places = jnp.arange(length, dtype=jnp.int32)
    before = jnp.concatenate([own_segments[:1] - 1, own_segments[:-1]])
    starts = lax.cummax(jnp.where(own_segments != before, places, 0), axis=0)
    positions = lax.dynamic_slice_in_dim(places - starts, place * rows, rows, 0)
    inverse = jnp.exp(-jnp.log(10000.0) * jnp.arange(HALF, dtype=F32) / HALF)
    angle = positions.astype(F32)[:, None] * inverse[None, :]
    here = lax.dynamic_slice_in_dim(own_segments, place * rows, rows, 0)
    padded = jnp.concatenate([jnp.full((rows,), -1, jnp.int32), own_segments])
    prior = lax.dynamic_slice_in_dim(padded, place * rows, rows, 0)
    common = (jnp.cos(angle), jnp.sin(angle), here[:, None], here[None, :], prior[None, :])

    x0 = lax.dynamic_index_in_dim(section_input, section, 0, keepdims=False).astype(F32)
    grad = lax.dynamic_index_in_dim(cotangent, section, 0, keepdims=False).astype(F32)
    out0, kept0 = forward_layer(x0, weights[0], common)
    out1, kept1 = forward_layer(out0.astype(BF16).astype(F32), weights[1], common)
    grad1, ff1, qo1, kv1, gains1, heads1 = backward_layer(grad, weights[1], kept1, common)
    grad0, ff0, qo0, kv0, gains0, heads0 = backward_layer(
        grad1.astype(BF16).astype(F32), weights[0], kept0, common
    )

    def placed(layer_zero, layer_one):
        up = lax.ppermute(layer_one.astype(BF16), "section", [(0, 1)]).astype(F32)
        down = lax.ppermute(layer_zero.astype(BF16), "section", [(1, 0)]).astype(F32)
        return jnp.stack(
            [jnp.where(first, layer_zero, up), jnp.where(first, down, layer_one)]
        )[None]

    def owned(zero, one):
        return jnp.where(first, zero, one)

    feed = owned(reduce_slots(ff0, 0), reduce_slots(ff1, 1))
    pair = owned(reduce_slots(qo0, 0), reduce_slots(qo1, 1))
    rest = owned(
        reduce_shared(kv0, gains0, heads0, 0), reduce_shared(kv1, gains1, heads1, 1)
    )
    return (
        placed(out0, out1),
        placed(grad0, grad1),
        pair[:1],
        rest[None, :, :HD],
        rest[None, :, HD : 2 * HD],
        pair[1:],
        feed[:1],
        feed[1:2],
        feed[2:],
        rest[None, :, 2 * HD : 2 * HD + 4],
        rest[None, :per_head, 2 * HD + 4 : 2 * HD + 6],
    )


def solution(mesh):
    return jax.shard_map(
        body,
        mesh=mesh,
        in_specs=(
            P(None, ("dp", "tensor"), None),
            P(None, ("dp", "tensor"), None),
            P(None, "dp"),
            P("section", "dp", "tensor"),
            P("section", "dp", None),
            P("section", "dp", None),
            P("section", "dp", "tensor"),
            P("section", "dp", "tensor"),
            P("section", "dp", "tensor"),
            P("section", "dp", "tensor"),
            P("section", "dp", None),
            P("section", "dp", None),
        ),
        out_specs=(
            P("section", None, ("dp", "tensor"), None),
            P("section", None, ("dp", "tensor"), None),
            P("section", "dp", "tensor"),
            P("section", "dp", None),
            P("section", "dp", None),
            P("section", "dp", "tensor"),
            P("section", "dp", "tensor"),
            P("section", "dp", "tensor"),
            P("section", "dp", "tensor"),
            P("section", "dp", None),
            P("section", "dp", None),
        ),
        check_vma=False,
    )
```

```python
import functools

import jax
import jax.numpy as jnp
from jax import lax
from jax.experimental import pallas as pl
from jax.experimental.pallas import tpu as pltpu
from jax.sharding import PartitionSpec as P

HD = 256
HALF = HD // 2
WIN = 512
BLK = 256
EPS = 1e-06
F32 = jnp.float32
BF16 = jnp.bfloat16
LIMIT = 50 * 1024 * 1024


def nn(a, b):
    return lax.dot_general(a, b, (((1,), (0,)), ((), ())), preferred_element_type=F32)


def nt(a, b):
    return lax.dot_general(a, b, (((1,), (1,)), ((), ())), preferred_element_type=F32)


def tn(a, b):
    return lax.dot_general(a, b, (((0,), (0,)), ((), ())), preferred_element_type=F32)


def rms(values, gain):
    return values * lax.rsqrt(jnp.mean(values * values, axis=-1, keepdims=True) + EPS) * gain


def rms_back(grad, values, gain):
    scale = lax.rsqrt(jnp.mean(values * values, axis=-1, keepdims=True) + EPS)
    unit = values * scale
    scaled = grad * gain
    inner = jnp.mean(scaled * unit, axis=-1, keepdims=True)
    return scale * (scaled - unit * inner), jnp.sum(grad * unit, axis=0, keepdims=True)


def rot(values, cosine, sine):
    a, b = values[:, :HALF], values[:, HALF:]
    return jnp.concatenate([a * cosine - b * sine, b * cosine + a * sine], axis=-1)


def rot_back(grad, cosine, sine):
    a, b = grad[:, :HALF], grad[:, HALF:]
    return jnp.concatenate([a * cosine + b * sine, b * cosine - a * sine], axis=-1)


GELU_A = 0.7978845608028654
GELU_B = 0.044715


def triangle():
    row = lax.broadcasted_iota(jnp.int32, (BLK, BLK), 0)
    column = lax.broadcasted_iota(jnp.int32, (BLK, BLK), 1)
    return column <= row


def tiles(block):
    rows = slice(block * BLK, (block + 1) * BLK)
    other = slice((1 - block) * BLK, (2 - block) * BLK)
    return rows, other, block == 1


def masks(block, lower, seg_col, seg_own, seg_prev):
    rows, other, own = tiles(block)
    mine = seg_col[rows, :]
    diagonal = mine == jnp.where(lower, seg_own[:, rows], seg_prev[:, rows])
    rest = mine == (seg_own if own else seg_prev)[:, other]
    return diagonal, rest


def stream(step, choice, own, other, held, arrived):
    def fetch(index):
        for wanted, slots in ((1, own), (0, other)):

            @pl.when(choice[0] == wanted)
            def _(slots=slots):
                for part, ref in enumerate(slots[index]):
                    pltpu.make_async_copy(
                        ref, held.at[index % 2, part], arrived.at[index % 2, part]
                    ).start()

    @pl.when(step == 0)
    def _():
        fetch(0)

    for index in range(1, len(own)):

        @pl.when(step == index - 1)
        def _(index=index):
            fetch(index)

    now = lax.rem(step, 2)
    for part, ref in enumerate(own[0]):
        pltpu.make_async_copy(ref, held.at[now, part], arrived.at[now, part]).wait()
    return now


def assemble_kernel(cuts, place, *refs):
    count = (len(refs) - len(cuts) - 1)
    pieces, outs, done = refs[:count], refs[count:-1], refs[-1]
    copies = []
    for shift, piece in enumerate(pieces):
        owner = lax.rem(place[0] + count - shift, count)
        for cut, (start, rows) in enumerate(cuts):
            at = pl.ds(pl.multiple_of(owner * rows, rows), rows)
            lead = (slice(None),) * (len(piece.shape) - 2)
            copies.append(
                pltpu.make_async_copy(
                    piece.at[lead + (pl.ds(start, rows),)],
                    outs[cut].at[lead + (at,)],
                    done.at[shift, cut],
                )
            )
    for copy in copies:
        copy.start()
    for copy in copies:
        copy.wait()


def prep_kernel(x, gains, heads, kvw, cosine, sine, normed, kraw, kv):
    rows = rms(x[...], gains[0:1, :]).astype(BF16)
    normed[...] = rows
    raw = nn(rows, kvw[:, :HD])
    kraw[...] = raw
    kv[:, :HD] = rot(rms(raw, heads[1:2, :]), cosine[...], sine[...]).astype(BF16)
    kv[:, HD:] = nn(rows, kvw[:, HD : 2 * HD]).astype(BF16)


def attend_kernel(
    choice, x, normed, gains, heads, own, prev, cosine, sine, seg_col, seg_own, seg_prev,
    qo_a, qo_b, qo_c, qo_d, qraw, q, mixed, lse, branch, middle, normed_two, held, arrived,
):
    step = pl.program_id(0)
    slots = [[qo_a], [qo_b], [qo_c], [qo_d]]
    now = stream(step, choice, slots, slots, held, arrived)
    raw = nn(normed[...], held[now, 0, :, :HD])
    qraw[0] = raw
    turned = rot(rms(raw, heads[0:1, :]), cosine[...], sine[...]).astype(BF16)
    q[0] = turned * jnp.asarray(0.0625, BF16)
    lower = triangle()
    for block in range(2):
        rows, other, is_own = tiles(block)
        diagonal, rest = masks(block, lower, seg_col[...], seg_own[...], seg_prev[...])
        query = q[0, rows, :]
        far = own if is_own else prev
        near_scores = jnp.where(
            lower, nt(query, own[rows, :HD]), nt(query, prev[rows, :HD])
        )
        near_scores = jnp.where(diagonal, near_scores, -1e30)
        far_scores = jnp.where(rest, nt(query, far[other, :HD]), -1e30)
        largest = jnp.maximum(
            jnp.max(near_scores, axis=-1, keepdims=True),
            jnp.max(far_scores, axis=-1, keepdims=True),
        )
        near = jnp.exp(near_scores - largest)
        rest_p = jnp.exp(far_scores - largest)
        total = jnp.sum(near, axis=-1, keepdims=True) + jnp.sum(rest_p, axis=-1, keepdims=True)
        inverse = 1.0 / total
        near = near * inverse
        rest_p = (rest_p * inverse).astype(BF16)
        near_own = jnp.where(lower, near, 0.0).astype(BF16)
        near_prev = jnp.where(lower, 0.0, near).astype(BF16)
        mixed[0, rows, :] = (
            nn(near_own, own[rows, HD:]) + nn(near_prev, prev[rows, HD:]) + nn(rest_p, far[other, HD:])
        ).astype(BF16)
        lse[0, rows, :] = largest + jnp.log(total)
    part = nt(mixed[0], held[now, 0, :, HD:])

    @pl.when(step == 0)
    def _():
        branch[...] = part

    @pl.when(step > 0)
    def _():
        branch[...] += part

    @pl.when(step == pl.num_programs(0) - 1)
    def _():
        mid = x[...] + rms(branch[...], gains[1:2, :])
        middle[...] = mid
        normed_two[...] = rms(mid, gains[2:3, :]).astype(BF16)


def slots_of(refs):
    halves = [[refs[at], refs[at + 1]] for at in range(0, len(refs), 2)]
    return halves[: len(halves) // 2], halves[len(halves) // 2 :]


def feed_kernel(choice, normed_two, middle, gains, *refs):
    own, other = slots_of(refs[:16])
    gate_out, up_out, branch_two, out, held, arrived = refs[16:]
    step = pl.program_id(0)
    now = stream(step, choice, own, other, held, arrived)
    rows = normed_two[...]
    part = 0.0
    for half in range(2):
        gate = nn(rows, held[now, half, 0])
        upward = nn(rows, held[now, half, 1])
        gate_out[0, half] = gate.astype(BF16)
        up_out[0, half] = upward.astype(BF16)
        wave = jnp.tanh(GELU_A * (gate + GELU_B * gate * gate * gate))
        hidden = (0.5 * gate * (1.0 + wave) * upward).astype(BF16)
        part = part + nt(hidden, held[now, half, 2])

    @pl.when(step == 0)
    def _():
        branch_two[...] = part

    @pl.when(step > 0)
    def _():
        branch_two[...] += part

    @pl.when(step == pl.num_programs(0) - 1)
    def _():
        out[...] = middle[...] + rms(branch_two[...], gains[3:4, :])


def feed_back_kernel(
    choice, grad, branch_two, middle, branch, normed_two, gains, gate_in, up_in, *refs
):
    own, other = slots_of(refs[:16])
    send, keep, grad_middle, grad_branch, gain_grads = refs[16:21]
    incoming, incoming_t, rows_t, total, held, arrived = refs[21:]
    step = pl.program_id(0)
    now = stream(step, choice, own, other, held, arrived)

    @pl.when(step == 0)
    def _():
        values, gain = rms_back(grad[...], branch_two[...], gains[3:4, :])
        incoming[...] = values.astype(BF16)
        incoming_t[...] = values.T.astype(BF16)
        rows_t[...] = normed_two[...].T
        gain_grads[2:3, :] = gain
        gain_grads[3:4, :] = jnp.zeros_like(gain)

    part = 0.0
    for half in range(2):
        gate = gate_in[0, half].astype(F32)
        upward = up_in[0, half].astype(F32)
        square = gate * gate
        wave = jnp.tanh(GELU_A * gate * (1.0 + GELU_B * square))
        bell = 0.5 * (1.0 + wave)
        active = gate * bell
        slope = bell + 0.5 * gate * (1.0 - wave * wave) * (GELU_A * (1.0 + 3.0 * GELU_B * square))
        grad_hidden = nn(incoming[...], held[now, half, 2])
        grad_up = (grad_hidden * active).astype(BF16)
        grad_gate = (grad_hidden * upward * slope).astype(BF16)
        hidden = (active * upward).astype(BF16)
        grads = [
            nn(rows_t[...], grad_gate).astype(BF16),
            nn(rows_t[...], grad_up).astype(BF16),
            nn(incoming_t[...], hidden).astype(BF16),
        ]

        @pl.when(step < 2)
        def _(half=half, grads=grads):
            for number, value in enumerate(grads):
                send[0, half, number] = value

        @pl.when(step >= 2)
        def _(half=half, grads=grads):
            for number, value in enumerate(grads):
                keep[0, half, number] = value

        part = part + nt(grad_gate, held[now, half, 0]) + nt(grad_up, held[now, half, 1])

    @pl.when(step == 0)
    def _():
        total[...] = part

    @pl.when(step > 0)
    def _():
        total[...] += part

    @pl.when(step == pl.num_programs(0) - 1)
    def _():
        from_norm, gain = rms_back(total[...], middle[...], gains[2:3, :])
        gain_grads[1:2, :] = gain
        mid = grad[...] + from_norm
        grad_middle[...] = mid
        values, gain = rms_back(mid, branch[...], gains[1:2, :])
        gain_grads[0:1, :] = gain
        grad_branch[...] = values.astype(BF16)


def attend_back_kernel(
    choice, grad_branch, normed, heads, q, qraw, mixed, lse, own, prev, cosine, sine,
    seg_col, seg_own, seg_prev, qo_a, qo_b, qo_c, qo_d,
    send, keep, kv_own, kv_prev, grad_normed, head_grad, grad_t, rows_t, prev_sum, grad_q,
    held, arrived,
):
    step = pl.program_id(0)
    slots = [[qo_a], [qo_b], [qo_c], [qo_d]]
    now = stream(step, choice, slots, slots, held, arrived)

    @pl.when(step == 0)
    def _():
        grad_t[...] = grad_branch[...].T
        rows_t[...] = normed[...].T
        kv_own[...] = jnp.zeros_like(kv_own)
        prev_sum[...] = jnp.zeros_like(prev_sum)
        grad_normed[...] = jnp.zeros_like(grad_normed)
        head_grad[...] = jnp.zeros_like(head_grad)

    grad_mixed = nn(grad_branch[...], held[now, 0, :, HD:]).astype(BF16)
    lower = triangle()
    for block in range(2):
        rows, other, is_own = tiles(block)
        diagonal, rest = masks(block, lower, seg_col[...], seg_own[...], seg_prev[...])
        query = q[0, rows, :]
        incoming = grad_mixed[rows, :]
        far = own if is_own else prev
        far_sum = kv_own if is_own else prev_sum
        log_total = lse[0, rows, :]
        near_scores = jnp.where(
            lower, nt(query, own[rows, :HD]), nt(query, prev[rows, :HD])
        )
        near = jnp.exp(jnp.where(diagonal, near_scores, -1e30) - log_total)
        rest_p = jnp.exp(jnp.where(rest, nt(query, far[other, :HD]), -1e30) - log_total)
        near_grad = jnp.where(
            lower, nt(incoming, own[rows, HD:]), nt(incoming, prev[rows, HD:])
        )
        rest_grad = nt(incoming, far[other, HD:])
        inner = jnp.sum(near * near_grad, axis=-1, keepdims=True) + jnp.sum(
            rest_p * rest_grad, axis=-1, keepdims=True
        )
        near_score = near * (near_grad - inner)
        rest_score = (rest_p * (rest_grad - inner)).astype(BF16)
        score_own = jnp.where(lower, near_score, 0.0).astype(BF16)
        score_prev = jnp.where(lower, 0.0, near_score).astype(BF16)
        near_own = jnp.where(lower, near, 0.0).astype(BF16)
        near_prev = jnp.where(lower, 0.0, near).astype(BF16)
        rest_p = rest_p.astype(BF16)
        grad_q[rows, :] = 0.0625 * (
            nn(score_own, own[rows, :HD])
            + nn(score_prev, prev[rows, :HD])
            + nn(rest_score, far[other, :HD])
        )
        kv_own[rows, :HD] += tn(score_own, query)
        prev_sum[rows, :HD] += tn(score_prev, query)
        far_sum[other, :HD] += tn(rest_score, query)
        kv_own[rows, HD:] += tn(near_own, incoming)
        prev_sum[rows, HD:] += tn(near_prev, incoming)
        far_sum[other, HD:] += tn(rest_p, incoming)
    values, gain = rms_back(
        rot_back(grad_q[...], cosine[...], sine[...]), qraw[0], heads[0:1, :]
    )
    head_grad[0:1, :] += gain
    grad_raw = values.astype(BF16)
    grad_normed[...] += nt(grad_raw, held[now, 0, :, :HD])

    def store(place):
        place[0, :, :HD] = nn(rows_t[...], grad_raw).astype(BF16)
        place[0, :, HD:] = nn(grad_t[...], mixed[0]).astype(BF16)

    @pl.when(step < 2)
    def _():
        store(send)

    @pl.when(step >= 2)
    def _():
        store(keep)

    @pl.when(step == pl.num_programs(0) - 1)
    def _():
        kv_prev[...] = prev_sum[...].astype(BF16)


def finish_kernel(
    kv_own, kv_next, kraw, normed, kvw, heads, gains, x, grad_normed, grad_middle, cosine, sine,
    kv_grad, grad_x, gain_grad, head_grad,
):
    total = kv_own[...] + kv_next[...].astype(F32)
    values, gain = rms_back(
        rot_back(total[:, :HD], cosine[...], sine[...]), kraw[...], heads[1:2, :]
    )
    head_grad[...] = gain
    grad_key = values.astype(BF16)
    grad_value = total[:, HD:].astype(BF16)
    rows = normed[...]
    kv_grad[:, :HD] = tn(rows, grad_key).astype(BF16)
    kv_grad[:, HD:] = tn(rows, grad_value).astype(BF16)
    from_all = grad_normed[...] + nt(grad_key, kvw[:, :HD]) + nt(grad_value, kvw[:, HD : 2 * HD])
    from_norm, gain = rms_back(from_all, x[...], gains[0:1, :])
    gain_grad[...] = gain
    grad_x[...] = grad_middle[...] + from_norm


def whole(shape):
    zeros = (0,) * len(shape)
    return pl.BlockSpec(shape, lambda *at: zeros)


def anywhere(shape):
    return pl.BlockSpec(memory_space=pl.ANY)


def scalars(shape):
    return pl.BlockSpec(memory_space=pltpu.SMEM)


def slot(shape):
    zeros = (0,) * (len(shape) - 1)
    return pl.BlockSpec((1,) + tuple(shape[1:]), lambda at: (at,) + zeros)


def early(shape):
    zeros = (0,) * (len(shape) - 1)
    return pl.BlockSpec((1,) + tuple(shape[1:]), lambda at: (jnp.minimum(at, 1),) + zeros)


def late(shape):
    zeros = (0,) * (len(shape) - 1)
    return pl.BlockSpec((1,) + tuple(shape[1:]), lambda at: (jnp.maximum(at - 2, 0),) + zeros)


def run(kernel, grid, ins, outs, scratch=(), micros=2):
    arrays = [a for a, _ in ins]
    return pl.pallas_call(
        kernel,
        grid=grid,
        in_specs=[spec(a.shape) for a, spec in ins],
        out_specs=[spec(shape) for shape, _, spec in outs],
        out_shape=[jax.ShapeDtypeStruct(shape, kind) for shape, kind, _ in outs],
        scratch_shapes=list(scratch),
        compiler_params=pltpu.CompilerParams(vmem_limit_bytes=LIMIT),
        cost_estimate=pl.CostEstimate(
            flops=micros * 1153000000, bytes_accessed=1, transcendentals=0
        ),
    )(*arrays)


def qo_scratch(width):
    return [pltpu.VMEM((2, 1, width, 2 * HD), BF16), pltpu.SemaphoreType.DMA((2, 1))]


def ff_scratch(width, units):
    return [pltpu.VMEM((2, 2, 3, width, units), BF16), pltpu.SemaphoreType.DMA((2, 2))]


def forward_keys(x, small, common):
    cosine, sine = common[:2]
    kvw, gains, heads = small
    rows, width = x.shape
    normed, kraw, kv = run(
        prep_kernel, (1,),
        [(x, whole), (gains, whole), (heads, whole), (kvw, whole), (cosine, whole), (sine, whole)],
        [((rows, width), BF16, whole), ((rows, HD), F32, whole), ((rows, 2 * HD), BF16, whole)],
        micros=2,
    )
    return normed, kraw, kv


def halo_on(kv):
    return lax.ppermute(kv, "tensor", [(i, i + 1) for i in range(lax.axis_size("tensor") - 1)])


def forward_attend(x, keys, small, choice, qo, common):
    cosine, sine, seg_col, seg_own, seg_prev = common
    kvw, gains, heads = small
    normed, kraw, kv, prev = keys
    rows, width = x.shape
    slots = len(qo)
    return run(
        attend_kernel, (slots,),
        [(choice, scalars), (x, whole), (normed, whole), (gains, whole), (heads, whole),
         (kv, whole), (prev, whole), (cosine, whole), (sine, whole), (seg_col, whole),
         (seg_own, whole), (seg_prev, whole)] + [(part, anywhere) for part in qo],
        [((slots, rows, HD), F32, slot), ((slots, rows, HD), BF16, slot),
         ((slots, rows, HD), BF16, slot), ((slots, rows, 1), F32, slot),
         ((rows, width), F32, whole), ((rows, width), F32, whole), ((rows, width), BF16, whole)],
        qo_scratch(width),
        micros=14,
    )


def forward_feed(attended, small, choice, ff):
    gains = small[1]
    middle, normed_two = attended[5:]
    rows, width = middle.shape
    slots, units = len(ff) // 4, ff[0].shape[2]
    return run(
        feed_kernel, (slots,),
        [(choice, scalars), (normed_two, whole), (middle, whole), (gains, whole)]
        + [(part, anywhere) for part in ff],
        [((slots, 2, rows, units), BF16, slot), ((slots, 2, rows, units), BF16, slot),
         ((rows, width), F32, whole), ((rows, width), F32, whole)],
        ff_scratch(width, units),
        micros=12,
    )


def backward_feed(grad, branch, middle, normed_two, fed, small, choice, ff):
    gains = small[1]
    gate, upward, branch_two, _ = fed
    rows, width = middle.shape
    slots, units = len(ff) // 4, ff[0].shape[2]
    half = slots // 2
    return run(
        feed_back_kernel, (slots,),
        [(choice, scalars), (grad, whole), (branch_two, whole), (middle, whole), (branch, whole),
         (normed_two, whole), (gains, whole), (gate, slot), (upward, slot)]
        + [(part, anywhere) for part in ff],
        [((half, 2, 3, width, units), BF16, early), ((half, 2, 3, width, units), BF16, late),
         ((rows, width), F32, whole), ((rows, width), BF16, whole), ((4, width), F32, whole)],
        [pltpu.VMEM((rows, width), BF16), pltpu.VMEM((width, rows), BF16),
         pltpu.VMEM((width, rows), BF16), pltpu.VMEM((rows, width), F32)]
        + ff_scratch(width, units),
        micros=25,
    )


def backward_attend(grad_branch, keys, attended, small, choice, qo, common):
    cosine, sine, seg_col, seg_own, seg_prev = common
    heads = small[2]
    normed, kraw, kv, prev = keys
    qraw, q, mixed, lse = attended[:4]
    rows, width = normed.shape
    slots = len(qo)
    half = slots // 2
    return run(
        attend_back_kernel, (slots,),
        [(choice, scalars), (grad_branch, whole), (normed, whole), (heads, whole), (q, slot),
         (qraw, slot), (mixed, slot), (lse, slot), (kv, whole), (prev, whole), (cosine, whole),
         (sine, whole), (seg_col, whole), (seg_own, whole), (seg_prev, whole)]
        + [(part, anywhere) for part in qo],
        [((half, width, 2 * HD), BF16, early), ((half, width, 2 * HD), BF16, late),
         ((rows, 2 * HD), F32, whole), ((rows, 2 * HD), BF16, whole), ((rows, width), F32, whole),
         ((1, HD), F32, whole)],
        [pltpu.VMEM((width, rows), BF16), pltpu.VMEM((width, rows), BF16),
         pltpu.VMEM((rows, 2 * HD), F32), pltpu.VMEM((rows, HD), F32)] + qo_scratch(width),
        micros=17,
    )


def backward_keys(x, kv_own, kv_next, keys, small, grad_normed, grad_middle, common):
    cosine, sine = common[:2]
    kvw, gains, heads = small
    normed, kraw = keys[:2]
    rows, width = x.shape
    return run(
        finish_kernel, (1,),
        [(kv_own, whole), (kv_next, whole), (kraw, whole), (normed, whole), (kvw, whole),
         (heads, whole), (gains, whole), (x, whole), (grad_normed, whole), (grad_middle, whole),
         (cosine, whole), (sine, whole)],
        [((width, 2 * HD), BF16, whole), ((rows, width), F32, whole), ((1, width), F32, whole),
         ((1, HD), F32, whole)],
        micros=5,
    )


def halo_back(kv_prev):
    return lax.ppermute(
        kv_prev, "tensor", [(i + 1, i) for i in range(lax.axis_size("tensor") - 1)]
    )


def tensor_pairs(bit):
    return [(i, i ^ bit) for i in range(lax.axis_size("tensor"))]


def rows_over_dp(part, cuts):
    count = lax.axis_size("dp")
    lead, columns = part.shape[:-2], part.shape[-1]
    if count > 4:
        full = jnp.moveaxis(lax.all_gather(part, "dp", axis=0), 0, -3)
        return [
            full[..., start : start + rows, :].reshape(lead + (count * rows, columns))
            for start, rows in cuts
        ]
    pieces = [part] + [
        lax.ppermute(part, "dp", [(i, (i + shift) % count) for i in range(count)])
        for shift in range(1, count)
    ]
    place = lax.axis_index("dp").astype(jnp.int32).reshape(1)
    return run(
        functools.partial(assemble_kernel, cuts), (),
        [(place, scalars)] + [(piece, anywhere) for piece in pieces],
        [(lead + (count * rows, columns), part.dtype, anywhere) for _, rows in cuts],
        [pltpu.SemaphoreType.DMA((count, len(cuts)))],
    )


def across_tensor(part):
    return lax.ppermute(part, "tensor", tensor_pairs(2))


def beside_tensor(part):
    return lax.ppermute(part, "tensor", tensor_pairs(1))


def across_section(part):
    return lax.ppermute(part, "section", [(0, 1), (1, 0)])


def after(values, *others):
    return lax.optimization_barrier((values, others))[0]


def add(left, right):
    return (left.astype(F32) + right.astype(F32)).astype(BF16)


def summed_over_dp(full, layer=None):
    count = lax.axis_size("dp")
    if count > 4:
        return lax.psum_scatter(full, "dp", scatter_dimension=1, tiled=True).astype(F32)
    me = lax.axis_index("dp")
    rows = full.shape[1] // count
    sections = range(lax.axis_size("section")) if layer is None else (layer,)

    def rows_of(owner):
        return lax.dynamic_slice_in_dim(full, owner % count * rows, rows, 1)

    def shifted(shift):
        pairs = [
            (at * count + i, at * count + (i + shift) % count)
            for at in sections
            for i in range(count)
        ]
        return lax.ppermute(rows_of(me + shift), ("section", "dp"), pairs)

    total = rows_of(me).astype(F32)
    for piece in [shifted(shift) for shift in range(1, count)]:
        total += piece.astype(F32)
    return total


def to_section(part, layer):
    return add(part, lax.ppermute(part.astype(BF16), "section", [(1 - layer, layer)]))


def kept_sums(arrived, keep, half=None):
    if half is not None:
        arrived, keep = arrived[:, half], keep[:, half]
    return add(keep[1], arrived[1]), add(keep[0], arrived[0])


def pack_shared(kv_grad, gain_rows, head_rows):
    count = lax.axis_size("dp")
    width, columns = kv_grad.shape

    def shares(rows):
        parts = jnp.swapaxes(rows.reshape(rows.shape[0], count, -1), 0, 1)
        return jnp.pad(parts, ((0, 0), (0, 0), (0, columns - parts.shape[2])))

    small = jnp.concatenate([shares(gain_rows), shares(head_rows)], axis=1).astype(BF16)
    small = jnp.pad(small, ((0, 0), (0, 10), (0, 0)))
    return jnp.concatenate([kv_grad.reshape(count, -1, columns), small], axis=1).reshape(
        1, -1, columns
    )


def core_half(packed):
    count = lax.axis_size("dp")
    columns = packed.shape[-1]
    halves = packed.reshape(count, 2, -1, columns)
    mine = lax.axis_index("tensor") % 2

    def half(at):
        return lax.dynamic_index_in_dim(halves, at, 1, keepdims=False).reshape(1, -1, columns)

    return add(half(mine), beside_tensor(half(1 - mine)))


def body(
    section_input, cotangent, segments, query_weight, key_weight, value_weight, output_weight,
    gate_weight, up_weight, down_weight, norm_gains, head_gains,
):
    section = lax.axis_index("section")
    place = lax.axis_index("tensor")
    first = section == 0
    rows = section_input.shape[1]
    per_head = head_gains.shape[1]
    local = norm_gains.shape[1]

    gain_rows = norm_gains[0].T
    head_rows = jnp.pad(head_gains[0].T, ((0, 0), (0, local - per_head)))
    small = jnp.pad(jnp.concatenate([gain_rows, head_rows]), ((0, 10), (0, 2 * HD - local)))
    shared = jnp.concatenate(
        [
            jnp.concatenate([query_weight[0], output_weight[0]], axis=1),
            jnp.concatenate([key_weight[0], value_weight[0]], axis=1),
            small,
        ]
    )
    cuts = ((0, local), (local, local), (2 * local, 16))
    units = gate_weight.shape[2] // 2
    feeds = [
        jnp.stack([w[0, :, half * units : (half + 1) * units]
                   for w in (gate_weight, up_weight, down_weight)])
        for half in range(2)
    ]
    other = across_section(shared)
    own_segments = lax.dynamic_index_in_dim(segments, section, 0, keepdims=False)
    length = own_segments.shape[0]
    places = jnp.arange(length, dtype=jnp.int32)
    before = jnp.concatenate([own_segments[:1] - 1, own_segments[:-1]])
    starts = lax.cummax(jnp.where(own_segments != before, places, 0), axis=0)
    positions = lax.dynamic_slice_in_dim(places - starts, place * rows, rows, 0)
    inverse = jnp.exp(-jnp.log(10000.0) * jnp.arange(HALF, dtype=F32) / HALF)
    angle = positions.astype(F32)[:, None] * inverse[None, :]
    here = lax.dynamic_slice_in_dim(own_segments, place * rows, rows, 0)
    padded = jnp.concatenate([jnp.full((rows,), -1, jnp.int32), own_segments])
    prior = lax.dynamic_slice_in_dim(padded, place * rows, rows, 0)
    common = (jnp.cos(angle), jnp.sin(angle), here[:, None], here[None, :], prior[None, :])

    x0 = lax.dynamic_index_in_dim(section_input, section, 0, keepdims=False).astype(F32)
    grad = lax.dynamic_index_in_dim(cotangent, section, 0, keepdims=False).astype(F32)
    count = lax.axis_size("dp")

    def small_of(gathered):
        rows = gathered[2].reshape(count, 16, 2 * HD).astype(F32)
        gains = jnp.swapaxes(rows[:, :4, :local], 0, 1).reshape(4, count * local)
        heads = jnp.swapaxes(rows[:, 4:6, :per_head], 0, 1).reshape(2, HD)
        return gathered[1], gains, heads

    choices = [(section == layer).astype(jnp.int32).reshape(1) for layer in range(2)]
    shared_l = [jnp.where(first, shared, other), jnp.where(first, other, shared)]

    whole_cut = ((0, local),)
    gathered0 = rows_over_dp(shared_l[0], cuts)
    feed_in, qo_mine, kvw0, rows0, x0 = after((feeds[0], *gathered0, x0))
    qo_across = across_tensor(qo_mine)
    feed_a = rows_over_dp(feed_in, whole_cut)[0]
    small0 = small_of((qo_mine, kvw0, rows0))
    keys0 = forward_keys(x0, small0, common)
    feed_a, feed_in, qo_across, keys0 = after((feed_a, feeds[1], qo_across, keys0))
    other_a, mine_a = across_section(feed_a), across_tensor(feed_a)
    prev0 = halo_on(keys0[2])
    feed_b = rows_over_dp(feed_in, whole_cut)[0]
    qo0 = [beside_tensor(qo_mine), beside_tensor(qo_across), qo_mine, qo_across]
    other_a, mine_a, feed_b, shared1, qo0, prev0 = after(
        (other_a, mine_a, feed_b, shared_l[1], qo0, prev0)
    )
    keys0 = (*keys0, prev0)
    other_b, mine_b = across_section(feed_b), across_tensor(feed_b)
    gathered1 = rows_over_dp(shared1, cuts)
    beside_a = [beside_tensor(part) for part in (feed_a, mine_a, other_a)]
    attended0 = forward_attend(x0, keys0, small0, choices[0], qo0, common)
    other_a, other_b, mine_b, gathered1, beside_a, attended0 = after(
        (other_a, other_b, mine_b, gathered1, beside_a, attended0)
    )
    far_a, far_b = across_tensor(other_a), across_section(mine_b)
    beside_b = [beside_tensor(part) for part in (feed_b, mine_b, other_b)]
    small1 = small_of(gathered1)
    far_a, far_b, beside_b, small1, qo_mine1 = after(
        (far_a, far_b, beside_b, small1, gathered1[0])
    )
    beside_far = [beside_tensor(far_a), beside_tensor(far_b)]
    ff = [beside_a[0], beside_b[0], beside_a[1], beside_b[1], feed_a, feed_b, mine_a, mine_b,
          beside_a[2], beside_b[2], *beside_far, other_a, other_b, far_a, far_b]
    qo_across1 = across_tensor(qo_mine1)
    fed0 = forward_feed(attended0, small0, choices[0], ff)
    out0 = fed0[3]
    x1 = out0.astype(BF16).astype(F32)
    keys1 = forward_keys(x1, small1, common)
    keys1, qo_across1 = after((keys1, qo_across1))
    prev1 = halo_on(keys1[2])
    qo1 = [beside_tensor(qo_mine1), beside_tensor(qo_across1), qo_mine1, qo_across1]
    x1_low, prev1, qo1 = after((x1.astype(BF16), prev1, qo1))
    keys1 = (*keys1, prev1)
    down0 = lax.ppermute(x1_low, "section", [(1, 0)])
    attended1 = forward_attend(x1, keys1, small1, choices[1], qo1, common)
    attended1, down0 = after((attended1, down0))
    fed1 = forward_feed(attended1, small1, choices[1], ff)
    out1 = fed1[3]

    def packed(kv, gain, key, fed, at):
        return pack_shared(
            kv, jnp.concatenate([gain, fed[4][:3]]), jnp.concatenate([at[5], key])
        )

    def down(mine, arrived):
        full = add(mine, arrived)
        return summed_over_dp(full.reshape((-1,) + full.shape[-2:])).astype(BF16)

    up1 = lax.ppermute(out1.astype(BF16), "section", [(0, 1)])
    ff1 = backward_feed(grad, *attended1[4:], fed1, small1, choices[1], ff)
    ff1, up1 = after((ff1, up1))
    ff1_core = beside_tensor(ff1[0])
    at1 = backward_attend(ff1[3], keys1, attended1, small1, choices[1], qo1, common)
    at1, ff1_core = after((at1, ff1_core))
    next1 = halo_back(at1[3])
    qo1_core = beside_tensor(at1[0])
    sums1 = [kept_sums(ff1_core, ff1[1], half) for half in range(2)]
    next1, qo1_core, sums1 = after((next1, qo1_core, sums1))
    across1a = across_tensor(sums1[0][0])
    kv1, grad1, gain1, key1 = backward_keys(
        x1, at1[2], next1, keys1, small1, at1[4], ff1[2], common
    )
    grad1_low = grad1.astype(BF16)
    ff0 = backward_feed(
        grad1_low.astype(F32), *attended0[4:], fed0, small0, choices[0], ff
    )
    across1a, ff0, sums1 = after((across1a, ff0, sums1))
    ff0_core = beside_tensor(ff0[0])
    across1b = across_tensor(sums1[1][0])
    feed1a = down(sums1[0][1], across1a)
    at0 = backward_attend(ff0[3], keys0, attended0, small0, choices[0], qo0, common)
    at0, ff0_core, across1b, feed1a, qo1_core, grad1_low = after(
        (at0, ff0_core, across1b, feed1a, qo1_core, grad1_low)
    )
    next0 = halo_back(at0[3])
    qo0_core = beside_tensor(at0[0])
    sums0 = [kept_sums(ff0_core, ff0[1], half) for half in range(2)]
    across0a = across_tensor(sums0[0][0])
    feed1b = down(sums1[1][1], across1b)
    feed1a = to_section(feed1a, 1)
    kv0, grad0, gain0, key0 = backward_keys(
        x0, at0[2], next0, keys0, small0, at0[4], ff0[2], common
    )
    pair1 = kept_sums(qo1_core, at1[1])
    rest1 = core_half(packed(kv1, gain1, key1, ff1, at1))
    across0a, feed1b, sums0, kv0, pair1, rest1, qo0_core, grad1_low = after(
        (across0a, feed1b, sums0, kv0, pair1, rest1, qo0_core, grad1_low)
    )
    across0b = across_tensor(sums0[1][0])
    feed0a = down(sums0[0][1], across0a)
    feed1b = to_section(feed1b, 1)
    grad1_up = lax.ppermute(grad1_low, "section", [(0, 1)])
    grad0_down = lax.ppermute(grad0.astype(BF16), "section", [(1, 0)])
    pair0 = kept_sums(qo0_core, at0[1])
    rest0 = core_half(packed(kv0, gain0, key0, ff0, at0))
    across0b, feed0a, feed1b, grad1_up, grad0_down, pair0, rest0, rest1 = after(
        (across0b, feed0a, feed1b, grad1_up, grad0_down, pair0, rest0, rest1)
    )
    pairs_across = across_tensor(jnp.stack([pair0[0], pair1[0]]))
    rests = jnp.concatenate([rest0, rest1])
    feed0b = down(sums0[1][1], across0b)
    feed0a = to_section(feed0a, 0)
    pairs_across, feed0b, feed0a, rests = after((pairs_across, feed0b, feed0a, rests))
    pair_sums = down(jnp.stack([pair0[1], pair1[1]]), pairs_across)
    rests = summed_over_dp(rests).astype(BF16)
    feed0b = to_section(feed0b, 0)
    rests = add(rests, across_tensor(rests))
    owed = jnp.where(first, pair_sums[1], pair_sums[0])
    kept = jnp.where(first, pair_sums[0], pair_sums[1])
    pair = add(kept, across_section(owed)).astype(F32)[None]
    owed, kept = jnp.where(first, rests[1], rests[0]), jnp.where(first, rests[0], rests[1])
    rest = add(kept, across_section(owed))
    beside = beside_tensor(rest)
    even = place % 2 == 0
    rest = jnp.concatenate(
        [jnp.where(even, rest, beside), jnp.where(even, beside, rest)]
    ).astype(F32)
    feed0, feed1 = [feed0a, feed0b], [feed1a, feed1b]

    def placed(zero, from_zero, one, from_one):
        return jnp.stack(
            [
                jnp.where(first, zero, from_one.astype(F32)),
                jnp.where(first, from_zero.astype(F32), one),
            ]
        )[None]

    def owned(zero, one):
        return jnp.where(first, zero, one)

    halves = [owned(*both).astype(F32) for both in zip(feed0, feed1)]
    return (
        placed(out0, down0, out1, up1),
        placed(grad0, grad0_down, grad1, grad1_up),
        pair[:, :, :HD],
        rest[None, :local, :HD],
        rest[None, :local, HD:],
        pair[:, :, HD:],
        *[jnp.concatenate([halves[0][n], halves[1][n]], axis=1)[None] for n in range(3)],
        rest[local : local + 4, :local].T[None],
        rest[local + 4 : local + 6, :per_head].T[None],
    )


def solution(mesh):
    return jax.shard_map(
        body,
        mesh=mesh,
        in_specs=(
            P(None, ("dp", "tensor"), None),
            P(None, ("dp", "tensor"), None),
            P(None, "dp"),
            P("section", "dp", "tensor"),
            P("section", "dp", None),
            P("section", "dp", None),
            P("section", "dp", "tensor"),
            P("section", "dp", "tensor"),
            P("section", "dp", "tensor"),
            P("section", "dp", "tensor"),
            P("section", "dp", None),
            P("section", "dp", None),
        ),
        out_specs=(
            P("section", None, ("dp", "tensor"), None),
            P("section", None, ("dp", "tensor"), None),
            P("section", "dp", "tensor"),
            P("section", "dp", None),
            P("section", "dp", None),
            P("section", "dp", "tensor"),
            P("section", "dp", "tensor"),
            P("section", "dp", "tensor"),
            P("section", "dp", "tensor"),
            P("section", "dp", None),
            P("section", "dp", None),
        ),
        check_vma=False,
    )
```

```python
import functools

import jax
import jax.numpy as jnp
from jax import lax
from jax.experimental import pallas as pl
from jax.experimental.pallas import tpu as pltpu
from jax.sharding import PartitionSpec as P

HD = 256
HALF = HD // 2
WIN = 512
BLK = 256
EPS = 1e-06
F32 = jnp.float32
BF16 = jnp.bfloat16
LIMIT = 50 * 1024 * 1024


def nn(a, b):
    return lax.dot_general(a, b, (((1,), (0,)), ((), ())), preferred_element_type=F32)


def nt(a, b):
    return lax.dot_general(a, b, (((1,), (1,)), ((), ())), preferred_element_type=F32)


def tn(a, b):
    return lax.dot_general(a, b, (((0,), (0,)), ((), ())), preferred_element_type=F32)


def rms(values, gain):
    return values * lax.rsqrt(jnp.mean(values * values, axis=-1, keepdims=True) + EPS) * gain


def rms_back(grad, values, gain):
    scale = lax.rsqrt(jnp.mean(values * values, axis=-1, keepdims=True) + EPS)
    unit = values * scale
    scaled = grad * gain
    inner = jnp.mean(scaled * unit, axis=-1, keepdims=True)
    return scale * (scaled - unit * inner), jnp.sum(grad * unit, axis=0, keepdims=True)


def rot(values, cosine, sine):
    a, b = values[:, :HALF], values[:, HALF:]
    return jnp.concatenate([a * cosine - b * sine, b * cosine + a * sine], axis=-1)


def rot_back(grad, cosine, sine):
    a, b = grad[:, :HALF], grad[:, HALF:]
    return jnp.concatenate([a * cosine + b * sine, b * cosine - a * sine], axis=-1)


GELU_A = 0.7978845608028654
GELU_B = 0.044715


def triangle():
    row = lax.broadcasted_iota(jnp.int32, (BLK, BLK), 0)
    column = lax.broadcasted_iota(jnp.int32, (BLK, BLK), 1)
    return column <= row


def tiles(block):
    rows = slice(block * BLK, (block + 1) * BLK)
    other = slice((1 - block) * BLK, (2 - block) * BLK)
    return rows, other, block == 1


def masks(block, lower, seg_col, seg_own, seg_prev):
    rows, other, own = tiles(block)
    mine = seg_col[rows, :]
    diagonal = mine == jnp.where(lower, seg_own[:, rows], seg_prev[:, rows])
    rest = mine == (seg_own if own else seg_prev)[:, other]
    return diagonal, rest


def stream(step, choice, own, other, held, arrived):
    def fetch(index):
        for wanted, slots in ((1, own), (0, other)):

            @pl.when(choice[0] == wanted)
            def _(slots=slots):
                for part, ref in enumerate(slots[index]):
                    pltpu.make_async_copy(
                        ref, held.at[index % 2, part], arrived.at[index % 2, part]
                    ).start()

    @pl.when(step == 0)
    def _():
        fetch(0)

    for index in range(1, len(own)):

        @pl.when(step == index - 1)
        def _(index=index):
            fetch(index)

    now = lax.rem(step, 2)
    for part, ref in enumerate(own[0]):
        pltpu.make_async_copy(ref, held.at[now, part], arrived.at[now, part]).wait()
    return now


def assemble_kernel(cuts, place, *refs):
    count = (len(refs) - len(cuts) - 1)
    pieces, outs, done = refs[:count], refs[count:-1], refs[-1]
    copies = []
    for shift, piece in enumerate(pieces):
        owner = lax.rem(place[0] + count - shift, count)
        for cut, (start, rows) in enumerate(cuts):
            at = pl.ds(pl.multiple_of(owner * rows, rows), rows)
            lead = (slice(None),) * (len(piece.shape) - 2)
            copies.append(
                pltpu.make_async_copy(
                    piece.at[lead + (pl.ds(start, rows),)],
                    outs[cut].at[lead + (at,)],
                    done.at[shift, cut],
                )
            )
    for copy in copies:
        copy.start()
    for copy in copies:
        copy.wait()


def prep_kernel(x, gains, heads, kvw, cosine, sine, normed, kraw, kv):
    rows = rms(x[...].astype(F32), gains[0:1, :]).astype(BF16)
    normed[...] = rows
    raw = nn(rows, kvw[:, :HD])
    kraw[...] = raw
    kv[:, :HD] = rot(rms(raw, heads[1:2, :]), cosine[...], sine[...]).astype(BF16)
    kv[:, HD:] = nn(rows, kvw[:, HD : 2 * HD]).astype(BF16)


def attend_kernel(
    choice, x, normed, gains, heads, own, prev, cosine, sine, seg_col, seg_own, seg_prev,
    qo_a, qo_b, qo_c, qo_d, qraw, q, mixed, lse, branch, middle, normed_two, held, arrived,
):
    step = pl.program_id(0)
    slots = [[qo_a], [qo_b], [qo_c], [qo_d]]
    now = stream(step, choice, slots, slots, held, arrived)
    raw = nn(normed[...], held[now, 0, :, :HD])
    qraw[0] = raw
    turned = rot(rms(raw, heads[0:1, :]), cosine[...], sine[...]).astype(BF16)
    q[0] = turned * jnp.asarray(0.0625, BF16)
    lower = triangle()
    for block in range(2):
        rows, other, is_own = tiles(block)
        diagonal, rest = masks(block, lower, seg_col[...], seg_own[...], seg_prev[...])
        query = q[0, rows, :]
        far = own if is_own else prev
        near_scores = jnp.where(
            lower, nt(query, own[rows, :HD]), nt(query, prev[rows, :HD])
        )
        near_scores = jnp.where(diagonal, near_scores, -1e30)
        far_scores = jnp.where(rest, nt(query, far[other, :HD]), -1e30)
        largest = jnp.maximum(
            jnp.max(near_scores, axis=-1, keepdims=True),
            jnp.max(far_scores, axis=-1, keepdims=True),
        )
        near = jnp.exp(near_scores - largest)
        rest_p = jnp.exp(far_scores - largest)
        total = jnp.sum(near, axis=-1, keepdims=True) + jnp.sum(rest_p, axis=-1, keepdims=True)
        inverse = 1.0 / total
        near = near * inverse
        rest_p = (rest_p * inverse).astype(BF16)
        near_own = jnp.where(lower, near, 0.0).astype(BF16)
        near_prev = jnp.where(lower, 0.0, near).astype(BF16)
        mixed[0, rows, :] = (
            nn(near_own, own[rows, HD:]) + nn(near_prev, prev[rows, HD:]) + nn(rest_p, far[other, HD:])
        ).astype(BF16)
        lse[0, rows, :] = largest + jnp.log(total)
    part = nt(mixed[0], held[now, 0, :, HD:])

    @pl.when(step == 0)
    def _():
        branch[...] = part

    @pl.when(step > 0)
    def _():
        branch[...] += part

    @pl.when(step == pl.num_programs(0) - 1)
    def _():
        mid = x[...].astype(F32) + rms(branch[...], gains[1:2, :])
        middle[...] = mid
        normed_two[...] = rms(mid, gains[2:3, :]).astype(BF16)


def slots_of(refs):
    halves = [[refs[at], refs[at + 1]] for at in range(0, len(refs), 2)]
    return halves[: len(halves) // 2], halves[len(halves) // 2 :]


def feed_kernel(choice, normed_two, middle, gains, *refs):
    own, other = slots_of(refs[:16])
    gate_out, up_out, branch_two, out, out_low, held, arrived = refs[16:]
    step = pl.program_id(0)
    now = stream(step, choice, own, other, held, arrived)
    rows = normed_two[...]
    part = 0.0
    for half in range(2):
        gate = nn(rows, held[now, half, 0])
        upward = nn(rows, held[now, half, 1])
        gate_out[0, half] = gate.astype(BF16)
        up_out[0, half] = upward.astype(BF16)
        wave = jnp.tanh(GELU_A * (gate + GELU_B * gate * gate * gate))
        hidden = (0.5 * gate * (1.0 + wave) * upward).astype(BF16)
        part = part + nt(hidden, held[now, half, 2])

    @pl.when(step == 0)
    def _():
        branch_two[...] = part

    @pl.when(step > 0)
    def _():
        branch_two[...] += part

    @pl.when(step == pl.num_programs(0) - 1)
    def _():
        total = middle[...] + rms(branch_two[...], gains[3:4, :])
        out[...] = total
        out_low[...] = total.astype(BF16)


def feed_back_kernel(
    choice, grad, branch_two, middle, branch, normed_two, gains, gate_in, up_in, *refs
):
    own, other = slots_of(refs[:16])
    send, keep, grad_middle, grad_branch, gain_grads = refs[16:21]
    incoming, incoming_t, rows_t, total, held, arrived = refs[21:]
    step = pl.program_id(0)
    now = stream(step, choice, own, other, held, arrived)

    @pl.when(step == 0)
    def _():
        values, gain = rms_back(grad[...].astype(F32), branch_two[...], gains[3:4, :])
        incoming[...] = values.astype(BF16)
        incoming_t[...] = values.T.astype(BF16)
        rows_t[...] = normed_two[...].T
        gain_grads[2:3, :] = gain
        gain_grads[3:4, :] = jnp.zeros_like(gain)

    part = 0.0
    for half in range(2):
        gate = gate_in[0, half].astype(F32)
        upward = up_in[0, half].astype(F32)
        square = gate * gate
        wave = jnp.tanh(GELU_A * gate * (1.0 + GELU_B * square))
        bell = 0.5 * (1.0 + wave)
        active = gate * bell
        slope = bell + 0.5 * gate * (1.0 - wave * wave) * (GELU_A * (1.0 + 3.0 * GELU_B * square))
        grad_hidden = nn(incoming[...], held[now, half, 2])
        grad_up = (grad_hidden * active).astype(BF16)
        grad_gate = (grad_hidden * upward * slope).astype(BF16)
        hidden = (active * upward).astype(BF16)
        grads = [
            nn(rows_t[...], grad_gate).astype(BF16),
            nn(rows_t[...], grad_up).astype(BF16),
            nn(incoming_t[...], hidden).astype(BF16),
        ]

        @pl.when(step < 2)
        def _(half=half, grads=grads):
            for number, value in enumerate(grads):
                send[0, half, number] = value

        @pl.when(step >= 2)
        def _(half=half, grads=grads):
            for number, value in enumerate(grads):
                keep[0, half, number] = value

        part = part + nt(grad_gate, held[now, half, 0]) + nt(grad_up, held[now, half, 1])

    @pl.when(step == 0)
    def _():
        total[...] = part

    @pl.when(step > 0)
    def _():
        total[...] += part

    @pl.when(step == pl.num_programs(0) - 1)
    def _():
        from_norm, gain = rms_back(total[...], middle[...], gains[2:3, :])
        gain_grads[1:2, :] = gain
        mid = grad[...].astype(F32) + from_norm
        grad_middle[...] = mid
        values, gain = rms_back(mid, branch[...], gains[1:2, :])
        gain_grads[0:1, :] = gain
        grad_branch[...] = values.astype(BF16)


def attend_back_kernel(
    choice, grad_branch, normed, heads, q, qraw, mixed, lse, own, prev, cosine, sine,
    seg_col, seg_own, seg_prev, qo_a, qo_b, qo_c, qo_d,
    send, keep, kv_own, kv_prev, grad_normed, head_grad, grad_t, rows_t, prev_sum, grad_q,
    held, arrived,
):
    step = pl.program_id(0)
    slots = [[qo_a], [qo_b], [qo_c], [qo_d]]
    now = stream(step, choice, slots, slots, held, arrived)

    @pl.when(step == 0)
    def _():
        grad_t[...] = grad_branch[...].T
        rows_t[...] = normed[...].T
        kv_own[...] = jnp.zeros_like(kv_own)
        prev_sum[...] = jnp.zeros_like(prev_sum)
        grad_normed[...] = jnp.zeros_like(grad_normed)
        head_grad[...] = jnp.zeros_like(head_grad)

    grad_mixed = nn(grad_branch[...], held[now, 0, :, HD:]).astype(BF16)
    lower = triangle()
    for block in range(2):
        rows, other, is_own = tiles(block)
        diagonal, rest = masks(block, lower, seg_col[...], seg_own[...], seg_prev[...])
        query = q[0, rows, :]
        incoming = grad_mixed[rows, :]
        far = own if is_own else prev
        far_sum = kv_own if is_own else prev_sum
        log_total = lse[0, rows, :]
        near_scores = jnp.where(
            lower, nt(query, own[rows, :HD]), nt(query, prev[rows, :HD])
        )
        near = jnp.exp(jnp.where(diagonal, near_scores, -1e30) - log_total)
        rest_p = jnp.exp(jnp.where(rest, nt(query, far[other, :HD]), -1e30) - log_total)
        near_grad = jnp.where(
            lower, nt(incoming, own[rows, HD:]), nt(incoming, prev[rows, HD:])
        )
        rest_grad = nt(incoming, far[other, HD:])
        inner = jnp.sum(near * near_grad, axis=-1, keepdims=True) + jnp.sum(
            rest_p * rest_grad, axis=-1, keepdims=True
        )
        near_score = near * (near_grad - inner)
        rest_score = (rest_p * (rest_grad - inner)).astype(BF16)
        score_own = jnp.where(lower, near_score, 0.0).astype(BF16)
        score_prev = jnp.where(lower, 0.0, near_score).astype(BF16)
        near_own = jnp.where(lower, near, 0.0).astype(BF16)
        near_prev = jnp.where(lower, 0.0, near).astype(BF16)
        rest_p = rest_p.astype(BF16)
        grad_q[rows, :] = 0.0625 * (
            nn(score_own, own[rows, :HD])
            + nn(score_prev, prev[rows, :HD])
            + nn(rest_score, far[other, :HD])
        )
        kv_own[rows, :HD] += tn(score_own, query)
        prev_sum[rows, :HD] += tn(score_prev, query)
        far_sum[other, :HD] += tn(rest_score, query)
        kv_own[rows, HD:] += tn(near_own, incoming)
        prev_sum[rows, HD:] += tn(near_prev, incoming)
        far_sum[other, HD:] += tn(rest_p, incoming)
    values, gain = rms_back(
        rot_back(grad_q[...], cosine[...], sine[...]), qraw[0], heads[0:1, :]
    )
    head_grad[0:1, :] += gain
    grad_raw = values.astype(BF16)
    grad_normed[...] += nt(grad_raw, held[now, 0, :, :HD])

    def store(place):
        place[0, :, :HD] = nn(rows_t[...], grad_raw).astype(BF16)
        place[0, :, HD:] = nn(grad_t[...], mixed[0]).astype(BF16)

    @pl.when(step < 2)
    def _():
        store(send)

    @pl.when(step >= 2)
    def _():
        store(keep)

    @pl.when(step == pl.num_programs(0) - 1)
    def _():
        kv_prev[...] = prev_sum[...].astype(BF16)


def finish_kernel(
    kv_own, kv_next, kraw, normed, kvw, heads, gains, x, grad_normed, grad_middle, cosine, sine,
    kv_grad, grad_x, grad_low, gain_grad, head_grad,
):
    summed = kv_own[...] + kv_next[...].astype(F32)
    values, gain = rms_back(
        rot_back(summed[:, :HD], cosine[...], sine[...]), kraw[...], heads[1:2, :]
    )
    head_grad[...] = gain
    grad_key = values.astype(BF16)
    grad_value = summed[:, HD:].astype(BF16)
    rows = normed[...]
    kv_grad[:, :HD] = tn(rows, grad_key).astype(BF16)
    kv_grad[:, HD:] = tn(rows, grad_value).astype(BF16)
    from_all = grad_normed[...] + nt(grad_key, kvw[:, :HD]) + nt(grad_value, kvw[:, HD : 2 * HD])
    from_norm, gain = rms_back(from_all, x[...].astype(F32), gains[0:1, :])
    gain_grad[...] = gain
    total = grad_middle[...] + from_norm
    grad_x[...] = total
    grad_low[...] = total.astype(BF16)


def whole(shape):
    zeros = (0,) * len(shape)
    return pl.BlockSpec(shape, lambda *at: zeros)


def anywhere(shape):
    return pl.BlockSpec(memory_space=pl.ANY)


def fetched(shape):
    return pl.BlockSpec(memory_space=pltpu.HBM)


def scalars(shape):
    return pl.BlockSpec(memory_space=pltpu.SMEM)


def slot(shape):
    zeros = (0,) * (len(shape) - 1)
    return pl.BlockSpec((1,) + tuple(shape[1:]), lambda at: (at,) + zeros)


def early(shape):
    zeros = (0,) * (len(shape) - 1)
    return pl.BlockSpec((1,) + tuple(shape[1:]), lambda at: (jnp.minimum(at, 1),) + zeros)


def late(shape):
    zeros = (0,) * (len(shape) - 1)
    return pl.BlockSpec((1,) + tuple(shape[1:]), lambda at: (jnp.maximum(at - 2, 0),) + zeros)


def run(kernel, grid, ins, outs, scratch=(), micros=2):
    arrays = [a for a, _ in ins]
    return pl.pallas_call(
        kernel,
        grid=grid,
        in_specs=[spec(a.shape) for a, spec in ins],
        out_specs=[spec(shape) for shape, _, spec in outs],
        out_shape=[jax.ShapeDtypeStruct(shape, kind) for shape, kind, _ in outs],
        scratch_shapes=list(scratch),
        compiler_params=pltpu.CompilerParams(vmem_limit_bytes=LIMIT),
        cost_estimate=pl.CostEstimate(
            flops=micros * 1153000000, bytes_accessed=1, transcendentals=0
        ),
    )(*arrays)


def qo_scratch(width):
    return [pltpu.VMEM((2, 1, width, 2 * HD), BF16), pltpu.SemaphoreType.DMA((2, 1))]


def ff_scratch(width, units):
    return [pltpu.VMEM((2, 2, 3, width, units), BF16), pltpu.SemaphoreType.DMA((2, 2))]


def forward_keys(x, small, common):
    cosine, sine = common[:2]
    kvw, gains, heads = small
    rows, width = x.shape
    normed, kraw, kv = run(
        prep_kernel, (1,),
        [(x, whole), (gains, whole), (heads, whole), (kvw, whole), (cosine, whole), (sine, whole)],
        [((rows, width), BF16, whole), ((rows, HD), F32, whole), ((rows, 2 * HD), BF16, whole)],
        micros=2,
    )
    return normed, kraw, kv


def halo_on(kv):
    return lax.ppermute(kv, "tensor", [(i, i + 1) for i in range(lax.axis_size("tensor") - 1)])


def forward_attend(x, keys, small, choice, qo, common):
    cosine, sine, seg_col, seg_own, seg_prev = common
    kvw, gains, heads = small
    normed, kraw, kv, prev = keys
    rows, width = x.shape
    slots = len(qo)
    return run(
        attend_kernel, (slots,),
        [(choice, scalars), (x, whole), (normed, whole), (gains, whole), (heads, whole),
         (kv, whole), (prev, whole), (cosine, whole), (sine, whole), (seg_col, whole),
         (seg_own, whole), (seg_prev, whole)] + [(part, fetched) for part in qo],
        [((slots, rows, HD), F32, slot), ((slots, rows, HD), BF16, slot),
         ((slots, rows, HD), BF16, slot), ((slots, rows, 1), F32, slot),
         ((rows, width), F32, whole), ((rows, width), F32, whole), ((rows, width), BF16, whole)],
        qo_scratch(width),
        micros=14,
    )


def forward_feed(attended, small, choice, ff):
    gains = small[1]
    middle, normed_two = attended[5:]
    rows, width = middle.shape
    slots, units = len(ff) // 4, ff[0].shape[2]
    return run(
        feed_kernel, (slots,),
        [(choice, scalars), (normed_two, whole), (middle, whole), (gains, whole)]
        + [(part, fetched) for part in ff],
        [((slots, 2, rows, units), BF16, slot), ((slots, 2, rows, units), BF16, slot),
         ((rows, width), F32, whole), ((rows, width), F32, whole), ((rows, width), BF16, whole)],
        ff_scratch(width, units),
        micros=12,
    )


def backward_feed(grad, branch, middle, normed_two, fed, small, choice, ff):
    gains = small[1]
    gate, upward, branch_two = fed[:3]
    rows, width = middle.shape
    slots, units = len(ff) // 4, ff[0].shape[2]
    half = slots // 2
    return run(
        feed_back_kernel, (slots,),
        [(choice, scalars), (grad, whole), (branch_two, whole), (middle, whole), (branch, whole),
         (normed_two, whole), (gains, whole), (gate, slot), (upward, slot)]
        + [(part, fetched) for part in ff],
        [((half, 2, 3, width, units), BF16, early), ((half, 2, 3, width, units), BF16, late),
         ((rows, width), F32, whole), ((rows, width), BF16, whole), ((4, width), F32, whole)],
        [pltpu.VMEM((rows, width), BF16), pltpu.VMEM((width, rows), BF16),
         pltpu.VMEM((width, rows), BF16), pltpu.VMEM((rows, width), F32)]
        + ff_scratch(width, units),
        micros=25,
    )


def backward_attend(grad_branch, keys, attended, small, choice, qo, common):
    cosine, sine, seg_col, seg_own, seg_prev = common
    heads = small[2]
    normed, kraw, kv, prev = keys
    qraw, q, mixed, lse = attended[:4]
    rows, width = normed.shape
    slots = len(qo)
    half = slots // 2
    return run(
        attend_back_kernel, (slots,),
        [(choice, scalars), (grad_branch, whole), (normed, whole), (heads, whole), (q, slot),
         (qraw, slot), (mixed, slot), (lse, slot), (kv, whole), (prev, whole), (cosine, whole),
         (sine, whole), (seg_col, whole), (seg_own, whole), (seg_prev, whole)]
        + [(part, fetched) for part in qo],
        [((half, width, 2 * HD), BF16, early), ((half, width, 2 * HD), BF16, late),
         ((rows, 2 * HD), F32, whole), ((rows, 2 * HD), BF16, whole), ((rows, width), F32, whole),
         ((1, HD), F32, whole)],
        [pltpu.VMEM((width, rows), BF16), pltpu.VMEM((width, rows), BF16),
         pltpu.VMEM((rows, 2 * HD), F32), pltpu.VMEM((rows, HD), F32)] + qo_scratch(width),
        micros=17,
    )


def backward_keys(x, kv_own, kv_next, keys, small, grad_normed, grad_middle, common):
    cosine, sine = common[:2]
    kvw, gains, heads = small
    normed, kraw = keys[:2]
    rows, width = x.shape
    return run(
        finish_kernel, (1,),
        [(kv_own, whole), (kv_next, whole), (kraw, whole), (normed, whole), (kvw, whole),
         (heads, whole), (gains, whole), (x, whole), (grad_normed, whole), (grad_middle, whole),
         (cosine, whole), (sine, whole)],
        [((width, 2 * HD), BF16, whole), ((rows, width), F32, whole), ((rows, width), BF16, whole),
         ((1, width), F32, whole),
         ((1, HD), F32, whole)],
        micros=5,
    )


def halo_back(kv_prev):
    return lax.ppermute(
        kv_prev, "tensor", [(i + 1, i) for i in range(lax.axis_size("tensor") - 1)]
    )


def tensor_pairs(bit):
    return [(i, i ^ bit) for i in range(lax.axis_size("tensor"))]


def rows_over_dp(part, cuts):
    count = lax.axis_size("dp")
    lead, columns = part.shape[:-2], part.shape[-1]
    if count > 4:
        full = jnp.moveaxis(lax.all_gather(part, "dp", axis=0), 0, -3)
        return [
            full[..., start : start + rows, :].reshape(lead + (count * rows, columns))
            for start, rows in cuts
        ]
    pieces = [part] + [
        lax.ppermute(part, "dp", [(i, (i + shift) % count) for i in range(count)])
        for shift in range(1, count)
    ]
    place = lax.axis_index("dp").astype(jnp.int32).reshape(1)
    return run(
        functools.partial(assemble_kernel, cuts), (),
        [(place, scalars)] + [(piece, anywhere) for piece in pieces],
        [(lead + (count * rows, columns), part.dtype, anywhere) for _, rows in cuts],
        [pltpu.SemaphoreType.DMA((count, len(cuts)))],
    )


def across_tensor(part):
    return lax.ppermute(part, "tensor", tensor_pairs(2))


def beside_tensor(part):
    return lax.ppermute(part, "tensor", tensor_pairs(1))


def across_section(part):
    return lax.ppermute(part, "section", [(0, 1), (1, 0)])


def after(values, *others):
    return lax.optimization_barrier((values, others))[0]


def add(left, right):
    return (left.astype(F32) + right.astype(F32)).astype(BF16)


def summed_over_dp(parts):
    count = lax.axis_size("dp")
    if count > 4:
        return [
            lax.psum_scatter(part, "dp", scatter_dimension=1, tiled=True) for part in parts
        ]
    me = lax.axis_index("dp")
    shapes = [(part.shape[0], part.shape[1] // count, part.shape[2]) for part in parts]

    def share(owner):
        blocks = [
            lax.dynamic_slice_in_dim(part, owner % count * shape[1], shape[1], 1)
            for part, shape in zip(parts, shapes)
        ]
        return jnp.concatenate([block.reshape(-1, block.shape[2]) for block in blocks])

    total = share(me).astype(F32)
    pieces = [
        lax.ppermute(share(me + shift), "dp", [(i, (i + shift) % count) for i in range(count)])
        for shift in range(1, count)
    ]
    for piece in pieces:
        total += piece.astype(F32)
    total, sums, start = total.astype(BF16), [], 0
    for shape in shapes:
        size = shape[0] * shape[1]
        sums.append(total[start : start + size].reshape(shape))
        start += size
    return sums


def side_by_side(part):
    return jnp.concatenate([part[..., :HD], part[..., HD:]])


def joined(part):
    half = part.shape[0] // 2
    return jnp.concatenate([part[:half], part[half:]], axis=-1)


def kept_sums(arrived, keep, half=None):
    if half is not None:
        arrived, keep = arrived[:, half], keep[:, half]
    return add(keep[1], arrived[1]), add(keep[0], arrived[0])


def pack_shared(kv_grad, gain_rows, head_rows):
    count = lax.axis_size("dp")
    width, columns = kv_grad.shape

    def shares(rows):
        parts = jnp.swapaxes(rows.reshape(rows.shape[0], count, -1), 0, 1)
        return jnp.pad(parts, ((0, 0), (0, 0), (0, columns - parts.shape[2])))

    small = jnp.concatenate([shares(gain_rows), shares(head_rows)], axis=1).astype(BF16)
    small = jnp.pad(small, ((0, 0), (0, 10), (0, 0)))
    return jnp.concatenate([kv_grad.reshape(count, -1, columns), small], axis=1).reshape(
        1, -1, columns
    )


def core_half(packed):
    count = lax.axis_size("dp")
    columns = packed.shape[-1]
    halves = packed.reshape(count, 2, -1, columns)
    mine = lax.axis_index("tensor") % 2

    def half(at):
        return lax.dynamic_index_in_dim(halves, at, 1, keepdims=False).reshape(1, -1, columns)

    return add(half(mine), beside_tensor(half(1 - mine)))


def body(
    section_input, cotangent, segments, query_weight, key_weight, value_weight, output_weight,
    gate_weight, up_weight, down_weight, norm_gains, head_gains,
):
    section = lax.axis_index("section")
    place = lax.axis_index("tensor")
    first = section == 0
    rows = section_input.shape[1]
    per_head = head_gains.shape[1]
    local = norm_gains.shape[1]

    gain_rows = norm_gains[0].T
    head_rows = jnp.pad(head_gains[0].T, ((0, 0), (0, local - per_head)))
    small = jnp.pad(jnp.concatenate([gain_rows, head_rows]), ((0, 10), (0, 2 * HD - local)))
    shared = jnp.concatenate(
        [
            jnp.concatenate([query_weight[0], output_weight[0]], axis=1),
            lax.dynamic_slice_in_dim(
                jnp.concatenate([key_weight[0], value_weight[0]], axis=1),
                place % 2 * (local // 2), local // 2, 0,
            ),
            small,
        ]
    )
    cuts = ((0, local), (local, local // 2), (local + local // 2, 16))
    units = gate_weight.shape[2] // 2
    feeds = [
        jnp.stack([w[0, :, half * units : (half + 1) * units]
                   for w in (gate_weight, up_weight, down_weight)])
        for half in range(2)
    ]
    other = across_section(shared)
    own_segments = lax.dynamic_index_in_dim(segments, section, 0, keepdims=False)
    length = own_segments.shape[0]
    places = jnp.arange(length, dtype=jnp.int32)
    before = jnp.concatenate([own_segments[:1] - 1, own_segments[:-1]])
    starts = lax.cummax(jnp.where(own_segments != before, places, 0), axis=0)
    positions = lax.dynamic_slice_in_dim(places - starts, place * rows, rows, 0)
    inverse = jnp.exp(-jnp.log(10000.0) * jnp.arange(HALF, dtype=F32) / HALF)
    angle = positions.astype(F32)[:, None] * inverse[None, :]
    here = lax.dynamic_slice_in_dim(own_segments, place * rows, rows, 0)
    padded = jnp.concatenate([jnp.full((rows,), -1, jnp.int32), own_segments])
    prior = lax.dynamic_slice_in_dim(padded, place * rows, rows, 0)
    common = (jnp.cos(angle), jnp.sin(angle), here[:, None], here[None, :], prior[None, :])

    x0 = lax.dynamic_index_in_dim(section_input, section, 0, keepdims=False)
    grad = lax.dynamic_index_in_dim(cotangent, section, 0, keepdims=False)
    count = lax.axis_size("dp")

    def small_of(gathered):
        rows = gathered[2].reshape(count, 16, 2 * HD).astype(F32)
        gains = jnp.swapaxes(rows[:, :4, :local], 0, 1).reshape(4, count * local)
        heads = jnp.swapaxes(rows[:, 4:6, :per_head], 0, 1).reshape(2, HD)
        mine, other = gathered[1], beside_tensor(gathered[1])
        halves = [jnp.where(place % 2 == at, mine, other) for at in range(2)]
        halves = [half.reshape(count, 1, -1, 2 * HD) for half in halves]
        return jnp.concatenate(halves, axis=1).reshape(-1, 2 * HD), gains, heads

    choices = [(section == layer).astype(jnp.int32).reshape(1) for layer in range(2)]
    shared_l = [jnp.where(first, shared, other), jnp.where(first, other, shared)]

    whole_cut = ((0, local),)
    gathered0 = rows_over_dp(shared_l[0], cuts)
    feed_in, qo_mine, kvw0, rows0, x0 = after((feeds[0], *gathered0, x0))
    qo_across = across_tensor(qo_mine)
    feed_a = rows_over_dp(feed_in, whole_cut)[0]
    small0 = small_of((qo_mine, kvw0, rows0))
    feed_a, feed_in, qo_across, small0 = after((feed_a, feeds[1], qo_across, small0))
    keys0 = forward_keys(x0, small0, common)
    other_a, mine_a = across_section(feed_a), across_tensor(feed_a)
    feed_b = rows_over_dp(feed_in, whole_cut)[0]
    prev0 = halo_on(keys0[2])
    other_a, mine_a, feed_b = after((other_a, mine_a, feed_b))
    qo0 = [beside_tensor(qo_mine), beside_tensor(qo_across), qo_mine, qo_across]
    other_b, mine_b = across_section(feed_b), across_tensor(feed_b)
    keys0 = (*keys0, prev0)
    qo0, keys0 = after((qo0, keys0))
    beside_a = [beside_tensor(part) for part in (feed_a, mine_a, other_a)]
    attended0 = forward_attend(x0, keys0, small0, choices[0], qo0, common)
    other_a, other_b, mine_b, beside_a, attended0, shared1 = after(
        (other_a, other_b, mine_b, beside_a, attended0, shared_l[1])
    )
    far_a, far_b = across_tensor(other_a), across_section(mine_b)
    gathered1 = rows_over_dp(shared1, cuts)
    far_a, far_b, mine_b, other_b, gathered1 = after((far_a, far_b, mine_b, other_b, gathered1))
    beside_b = [beside_tensor(part) for part in (feed_b, mine_b, other_b)]
    beside_far = [beside_tensor(far_a), beside_tensor(far_b)]
    small1 = small_of(gathered1)
    qo_mine1, beside_b, beside_far = after((gathered1[0], beside_b, beside_far))
    ff = [beside_a[0], beside_b[0], beside_a[1], beside_b[1], feed_a, feed_b, mine_a, mine_b,
          beside_a[2], beside_b[2], *beside_far, other_a, other_b, far_a, far_b]
    qo_across1 = across_tensor(qo_mine1)
    fed0 = forward_feed(attended0, small0, choices[0], ff)
    out0, x1 = fed0[3:]
    keys1 = forward_keys(x1, small1, common)
    keys1, qo_across1 = after((keys1, qo_across1))
    prev1 = halo_on(keys1[2])
    qo1 = [beside_tensor(qo_mine1), beside_tensor(qo_across1), qo_mine1, qo_across1]
    x1, prev1, qo1 = after((x1, prev1, qo1))
    keys1 = (*keys1, prev1)
    attended1 = forward_attend(x1, keys1, small1, choices[1], qo1, common)
    fed1 = forward_feed(attended1, small1, choices[1], ff)
    out1, out1_low = fed1[3:]

    def packed(kv, gain, key, fed, at):
        return pack_shared(
            kv, jnp.concatenate([gain, fed[4][:3]]), jnp.concatenate([at[5], key])
        )

    out_got = across_section(jnp.where(first, out1_low, x1))
    ff1 = backward_feed(grad, *attended1[4:], fed1, small1, choices[1], ff)
    ff1, out_got = after((ff1, out_got))
    ff1_core = beside_tensor(ff1[0])
    at1 = backward_attend(ff1[3], keys1, attended1, small1, choices[1], qo1, common)
    at1, ff1_core = after((at1, ff1_core))
    next1 = halo_back(at1[3])
    qo1_core = beside_tensor(at1[0])
    sums1 = [kept_sums(ff1_core, ff1[1], half) for half in range(2)]
    next1, qo1_core, sums1 = after((next1, qo1_core, sums1))
    across1a = across_tensor(sums1[0][0])
    pair1 = kept_sums(qo1_core, at1[1])
    pair1_across = across_tensor(pair1[0])
    kv1, grad1, grad1_low, gain1, key1 = backward_keys(
        x1, at1[2], next1, keys1, small1, at1[4], ff1[2], common
    )
    rest1 = core_half(packed(kv1, gain1, key1, ff1, at1))[0]
    ff0 = backward_feed(grad1_low, *attended0[4:], fed0, small0, choices[0], ff)
    across1a, ff0, sums1, pair1, pair1_across, rest1 = after(
        (across1a, ff0, sums1, pair1, pair1_across, rest1)
    )
    ff0_core = beside_tensor(ff0[0])
    across1b, rest1_across = across_tensor(sums1[1][0]), across_tensor(rest1)
    at0 = backward_attend(ff0[3], keys0, attended0, small0, choices[0], qo0, common)
    at0, ff0_core, across1b, rest1, rest1_across = after(
        (at0, ff0_core, across1b, rest1, rest1_across)
    )
    next0 = halo_back(at0[3])
    qo0_core = beside_tensor(at0[0])
    sums0 = [kept_sums(ff0_core, ff0[1], half) for half in range(2)]
    across0a = across_tensor(sums0[0][0])
    kv0, grad0, grad0_low, gain0, key0 = backward_keys(
        x0, at0[2], next0, keys0, small0, at0[4], ff0[2], common
    )
    grad_got = across_section(jnp.where(first, grad1_low, grad0_low))
    pair0 = kept_sums(qo0_core, at0[1])
    rest0 = core_half(packed(kv0, gain0, key0, ff0, at0))[0]
    full1 = [add(sums1[0][1], across1a), add(sums1[1][1], across1b)]
    low1 = jnp.concatenate([add(pair1[1], pair1_across), add(rest1, rest1_across)])
    across0a, rest0, pair0, sums0, full1, low1, grad_got = after(
        (across0a, rest0, pair0, sums0, full1, low1, grad_got)
    )

    def swapped(zero, one):
        return add(jnp.where(first, zero, one), across_section(jnp.where(first, one, zero)))

    across0b = across_tensor(sums0[1][0])
    feed_a = swapped(add(sums0[0][1], across0a), full1[0])
    low0 = jnp.concatenate([pair0[0], rest0])
    across0b, feed_a, low0, sums0 = after((across0b, feed_a, low0, sums0))
    low0_across = across_tensor(low0)
    feed_b = swapped(add(sums0[1][1], across0b), full1[1])
    feed_a = summed_over_dp([feed_a])[0]
    low0_across, feed_a, feed_b = after((low0_across, feed_a, feed_b))
    low = swapped(add(jnp.concatenate([pair0[1], rest0]), low0_across), low1)
    feed_b = summed_over_dp([feed_b])[0]
    feed_b, low = after((feed_b, low))
    pair_rows = pair0[0].shape[0]
    pair, rest = summed_over_dp(
        [side_by_side(low[None, :pair_rows]), side_by_side(low[None, pair_rows:])]
    )
    pair, rest = joined(pair).astype(F32), joined(rest)[0]
    beside = beside_tensor(rest)
    even = place % 2 == 0
    rest = jnp.concatenate(
        [jnp.where(even, rest, beside), jnp.where(even, beside, rest)]
    ).astype(F32)
    feed = jnp.stack([feed_a, feed_b]).astype(F32)

    def placed(zero, one, got):
        got = got.astype(F32)
        return jnp.stack([jnp.where(first, zero, got), jnp.where(first, got, one)])[None]

    return (
        placed(out0, out1, out_got),
        placed(grad0, grad1, grad_got),
        pair[:, :, :HD],
        rest[None, :local, :HD],
        rest[None, :local, HD:],
        pair[:, :, HD:],
        *[jnp.concatenate([feed[0, n], feed[1, n]], axis=1)[None] for n in range(3)],
        rest[local : local + 4, :local].T[None],
        rest[local + 4 : local + 6, :per_head].T[None],
    )


def solution(mesh):
    return jax.shard_map(
        body,
        mesh=mesh,
        in_specs=(
            P(None, ("dp", "tensor"), None),
            P(None, ("dp", "tensor"), None),
            P(None, "dp"),
            P("section", "dp", "tensor"),
            P("section", "dp", None),
            P("section", "dp", None),
            P("section", "dp", "tensor"),
            P("section", "dp", "tensor"),
            P("section", "dp", "tensor"),
            P("section", "dp", "tensor"),
            P("section", "dp", None),
            P("section", "dp", None),
        ),
        out_specs=(
            P("section", None, ("dp", "tensor"), None),
            P("section", None, ("dp", "tensor"), None),
            P("section", "dp", "tensor"),
            P("section", "dp", None),
            P("section", "dp", None),
            P("section", "dp", "tensor"),
            P("section", "dp", "tensor"),
            P("section", "dp", "tensor"),
            P("section", "dp", "tensor"),
            P("section", "dp", None),
            P("section", "dp", None),
        ),
        check_vma=False,
    )
```

```python
import functools

import jax
import jax.numpy as jnp
from jax import lax
from jax.experimental import pallas as pl
from jax.experimental.pallas import tpu as pltpu
from jax.sharding import PartitionSpec as P

HD = 256
HALF = HD // 2
WIN = 512
BLK = 256
EPS = 1e-06
F32 = jnp.float32
BF16 = jnp.bfloat16
LIMIT = 50 * 1024 * 1024


def nn(a, b):
    return lax.dot_general(a, b, (((1,), (0,)), ((), ())), preferred_element_type=F32)


def nt(a, b):
    return lax.dot_general(a, b, (((1,), (1,)), ((), ())), preferred_element_type=F32)


def tn(a, b):
    return lax.dot_general(a, b, (((0,), (0,)), ((), ())), preferred_element_type=F32)


def rms(values, gain):
    return values * lax.rsqrt(jnp.mean(values * values, axis=-1, keepdims=True) + EPS) * gain


def rms_back(grad, values, gain):
    scale = lax.rsqrt(jnp.mean(values * values, axis=-1, keepdims=True) + EPS)
    unit = values * scale
    scaled = grad * gain
    inner = jnp.mean(scaled * unit, axis=-1, keepdims=True)
    return scale * (scaled - unit * inner), jnp.sum(grad * unit, axis=0, keepdims=True)


def rot(values, cosine, sine):
    a, b = values[:, :HALF], values[:, HALF:]
    return jnp.concatenate([a * cosine - b * sine, b * cosine + a * sine], axis=-1)


def rot_back(grad, cosine, sine):
    a, b = grad[:, :HALF], grad[:, HALF:]
    return jnp.concatenate([a * cosine + b * sine, b * cosine - a * sine], axis=-1)


GELU_A = 0.7978845608028654
GELU_B = 0.044715


def triangle():
    row = lax.broadcasted_iota(jnp.int32, (BLK, BLK), 0)
    column = lax.broadcasted_iota(jnp.int32, (BLK, BLK), 1)
    return column <= row


def tiles(block):
    rows = slice(block * BLK, (block + 1) * BLK)
    other = slice((1 - block) * BLK, (2 - block) * BLK)
    return rows, other, block == 1


def masks(block, lower, seg_col, seg_own, seg_prev):
    rows, other, own = tiles(block)
    mine = seg_col[rows, :]
    diagonal = mine == jnp.where(lower, seg_own[:, rows], seg_prev[:, rows])
    rest = mine == (seg_own if own else seg_prev)[:, other]
    return diagonal, rest


def stream(step, choice, own, other, held, arrived):
    def spot(index, part):
        if len(held.shape) == 4:
            return held.at[index, part]
        columns = held.shape[4] // 2
        return held.at[index, 0, :, :, pl.ds(part * columns, columns)]

    def fetch(index):
        for wanted, slots in ((1, own), (0, other)):

            @pl.when(choice[0] == wanted)
            def _(slots=slots):
                for part, ref in enumerate(slots[index]):
                    pltpu.make_async_copy(
                        ref, spot(index % 2, part), arrived.at[index % 2, part]
                    ).start()

    @pl.when(step == 0)
    def _():
        fetch(0)

    for index in range(1, len(own)):

        @pl.when(step == index - 1)
        def _(index=index):
            fetch(index)

    now = lax.rem(step, 2)
    for part, ref in enumerate(own[0]):
        pltpu.make_async_copy(ref, spot(now, part), arrived.at[now, part]).wait()
    return now


def assemble_kernel(cuts, place, *refs):
    count = (len(refs) - len(cuts) - 1)
    pieces, outs, done = refs[:count], refs[count:-1], refs[-1]
    copies = []
    for shift, piece in enumerate(pieces):
        owner = lax.rem(place[0] + count - shift, count)
        for cut, (start, rows) in enumerate(cuts):
            at = pl.ds(pl.multiple_of(owner * rows, rows), rows)
            lead = (slice(None),) * (len(piece.shape) - 2)
            copies.append(
                pltpu.make_async_copy(
                    piece.at[lead + (pl.ds(start, rows),)],
                    outs[cut].at[lead + (at,)],
                    done.at[shift, cut],
                )
            )
    for copy in copies:
        copy.start()
    for copy in copies:
        copy.wait()


def prep_kernel(x, gains, heads, kvw, cosine, sine, normed, kraw, kv):
    rows = rms(x[...].astype(F32), gains[0:1, :]).astype(BF16)
    normed[...] = rows
    raw = nn(rows, kvw[:, :HD])
    kraw[...] = raw
    kv[:, :HD] = rot(rms(raw, heads[1:2, :]), cosine[...], sine[...]).astype(BF16)
    kv[:, HD:] = nn(rows, kvw[:, HD : 2 * HD]).astype(BF16)


def flat(tile):
    return tile.reshape(-1, tile.shape[-1])


def tall(tile):
    return tile.reshape(2, -1, tile.shape[-1])


def attend_kernel(
    choice, x, normed, gains, heads, own, prev, cosine, sine, seg_col, seg_own, seg_prev,
    qo_a, qo_b, qo_c, qo_d, qraw, q, mixed, lse, branch, middle, normed_two, held, arrived,
):
    step = pl.program_id(0)
    slots = [[qo_a, qo_b], [qo_c, qo_d]]
    now = stream(step, choice, slots, slots, held, arrived)
    for head in range(2):
        raw = nn(normed[...], held[now, head, :, :HD])
        qraw[head] = raw
        turned = rot(rms(raw, heads[0:1, :]), cosine[...], sine[...]).astype(BF16)
        q[head] = turned * jnp.asarray(0.0625, BF16)
    lower = triangle()
    for block in range(2):
        rows, other, is_own = tiles(block)
        diagonal, rest = masks(block, lower, seg_col[...], seg_own[...], seg_prev[...])
        query = flat(q[:, rows, :])
        far = own if is_own else prev
        near_scores = jnp.where(
            lower, tall(nt(query, own[rows, :HD])), tall(nt(query, prev[rows, :HD]))
        )
        near_scores = jnp.where(diagonal, near_scores, -1e30)
        far_scores = jnp.where(rest, tall(nt(query, far[other, :HD])), -1e30)
        largest = jnp.maximum(
            jnp.max(near_scores, axis=-1, keepdims=True),
            jnp.max(far_scores, axis=-1, keepdims=True),
        )
        near = jnp.exp(near_scores - largest)
        rest_p = jnp.exp(far_scores - largest)
        total = jnp.sum(near, axis=-1, keepdims=True) + jnp.sum(rest_p, axis=-1, keepdims=True)
        inverse = 1.0 / total
        near = near * inverse
        rest_p = (rest_p * inverse).astype(BF16)
        near_own = jnp.where(lower, near, 0.0).astype(BF16)
        near_prev = jnp.where(lower, 0.0, near).astype(BF16)
        mixed[:, rows, :] = tall(
            nn(flat(near_own), own[rows, HD:])
            + nn(flat(near_prev), prev[rows, HD:])
            + nn(flat(rest_p), far[other, HD:])
        ).astype(BF16)
        lse[:, rows, :] = largest + jnp.log(total)
    part = nt(mixed[0], held[now, 0, :, HD:]) + nt(mixed[1], held[now, 1, :, HD:])

    @pl.when(step == 0)
    def _():
        branch[...] = part

    @pl.when(step > 0)
    def _():
        branch[...] += part

    @pl.when(step == pl.num_programs(0) - 1)
    def _():
        mid = x[...].astype(F32) + rms(branch[...], gains[1:2, :])
        middle[...] = mid
        normed_two[...] = rms(mid, gains[2:3, :]).astype(BF16)


def slots_of(refs):
    halves = [[refs[at], refs[at + 1]] for at in range(0, len(refs), 2)]
    return halves[: len(halves) // 2], halves[len(halves) // 2 :]


def feed_kernel(choice, normed_two, middle, gains, *refs):
    own, other = slots_of(refs[:16])
    gate_out, up_out, branch_two, out, out_low, held, arrived = refs[16:]
    step = pl.program_id(0)
    now = stream(step, choice, own, other, held, arrived)
    rows = normed_two[...]
    gate = nn(rows, held[now, 0, 0])
    upward = nn(rows, held[now, 0, 1])
    gate_out[0] = gate.astype(BF16)
    up_out[0] = upward.astype(BF16)
    wave = jnp.tanh(GELU_A * gate * (1.0 + GELU_B * gate * gate))
    hidden = (0.5 * gate * (1.0 + wave) * upward).astype(BF16)
    part = nt(hidden, held[now, 0, 2])

    @pl.when(step == 0)
    def _():
        branch_two[...] = part

    @pl.when(step > 0)
    def _():
        branch_two[...] += part

    @pl.when(step == pl.num_programs(0) - 1)
    def _():
        total = middle[...] + rms(branch_two[...], gains[3:4, :])
        out[...] = total
        out_low[...] = total.astype(BF16)


def feed_back_kernel(
    choice, grad, branch_two, middle, branch, normed_two, gains, gate_in, up_in, *refs
):
    own, other = slots_of(refs[:16])
    send, keep, grad_middle, grad_branch, gain_grads = refs[16:21]
    incoming, incoming_t, rows_t, total, held, arrived = refs[21:]
    step = pl.program_id(0)
    now = stream(step, choice, own, other, held, arrived)

    @pl.when(step == 0)
    def _():
        values, gain = rms_back(grad[...].astype(F32), branch_two[...], gains[3:4, :])
        incoming[...] = values.astype(BF16)
        incoming_t[...] = values.T.astype(BF16)
        rows_t[...] = normed_two[...].T
        gain_grads[2:3, :] = gain
        gain_grads[3:4, :] = jnp.zeros_like(gain)

    gate = gate_in[0].astype(F32)
    upward = up_in[0].astype(F32)
    square = gate * gate
    wave = jnp.tanh(GELU_A * gate * (1.0 + GELU_B * square))
    bell = 0.5 * (1.0 + wave)
    active = gate * bell
    slope = bell + gate * (1.0 - wave * wave) * (0.5 * GELU_A * (1.0 + 3.0 * GELU_B * square))
    grad_hidden = nn(incoming[...], held[now, 0, 2])
    grad_up = (grad_hidden * active).astype(BF16)
    grad_gate = (grad_hidden * upward * slope).astype(BF16)
    hidden = (active * upward).astype(BF16)
    columns = hidden.shape[1] // 2

    def store(place):
        for number, (left, right) in enumerate(
            ((rows_t, grad_gate), (rows_t, grad_up), (incoming_t, hidden))
        ):
            value = nn(left[...], right).astype(BF16)
            place[0, 0, number] = value[:, :columns]
            place[0, 1, number] = value[:, columns:]

    @pl.when(step < 2)
    def _():
        store(send)

    @pl.when(step >= 2)
    def _():
        store(keep)

    part = nt(grad_gate, held[now, 0, 0]) + nt(grad_up, held[now, 0, 1])

    @pl.when(step == 0)
    def _():
        total[...] = part

    @pl.when(step > 0)
    def _():
        total[...] += part

    @pl.when(step == pl.num_programs(0) - 1)
    def _():
        from_norm, gain = rms_back(total[...], middle[...], gains[2:3, :])
        gain_grads[1:2, :] = gain
        mid = grad[...].astype(F32) + from_norm
        grad_middle[...] = mid
        values, gain = rms_back(mid, branch[...], gains[1:2, :])
        gain_grads[0:1, :] = gain
        grad_branch[...] = values.astype(BF16)


def attend_back_kernel(
    choice, grad_branch, normed, heads, q, qraw, mixed, lse, own, prev, cosine, sine,
    seg_col, seg_own, seg_prev, qo_a, qo_b, qo_c, qo_d,
    send, keep, kv_own, kv_prev, grad_normed, head_grad, grad_t, rows_t, prev_sum, grad_q,
    held, arrived, mixed_g, raw_g,
):
    step = pl.program_id(0)
    slots = [[qo_a, qo_b], [qo_c, qo_d]]
    now = stream(step, choice, slots, slots, held, arrived)

    @pl.when(step == 0)
    def _():
        grad_t[...] = grad_branch[...].T
        rows_t[...] = normed[...].T
        kv_own[...] = jnp.zeros_like(kv_own)
        prev_sum[...] = jnp.zeros_like(prev_sum)
        grad_normed[...] = jnp.zeros_like(grad_normed)
        head_grad[...] = jnp.zeros_like(head_grad)

    for head in range(2):
        mixed_g[head] = nn(grad_branch[...], held[now, head, :, HD:]).astype(BF16)
    lower = triangle()
    for block in range(2):
        rows, other, is_own = tiles(block)
        diagonal, rest = masks(block, lower, seg_col[...], seg_own[...], seg_prev[...])
        query = flat(q[:, rows, :])
        incoming = flat(mixed_g[:, rows, :])
        far = own if is_own else prev
        far_sum = kv_own if is_own else prev_sum
        log_total = lse[:, rows, :]
        near_scores = jnp.where(
            lower, tall(nt(query, own[rows, :HD])), tall(nt(query, prev[rows, :HD]))
        )
        near = jnp.exp(jnp.where(diagonal, near_scores, -1e30) - log_total)
        rest_p = jnp.exp(jnp.where(rest, tall(nt(query, far[other, :HD])), -1e30) - log_total)
        near_grad = jnp.where(
            lower, tall(nt(incoming, own[rows, HD:])), tall(nt(incoming, prev[rows, HD:]))
        )
        rest_grad = tall(nt(incoming, far[other, HD:]))
        inner = jnp.sum(near * near_grad, axis=-1, keepdims=True) + jnp.sum(
            rest_p * rest_grad, axis=-1, keepdims=True
        )
        near_score = near * (near_grad - inner)
        rest_score = flat(rest_p * (rest_grad - inner)).astype(BF16)
        score_own = flat(jnp.where(lower, near_score, 0.0)).astype(BF16)
        score_prev = flat(jnp.where(lower, 0.0, near_score)).astype(BF16)
        near_own = flat(jnp.where(lower, near, 0.0)).astype(BF16)
        near_prev = flat(jnp.where(lower, 0.0, near)).astype(BF16)
        rest_p = flat(rest_p).astype(BF16)
        grad_q[:, rows, :] = tall(
            0.0625
            * (
                nn(score_own, own[rows, :HD])
                + nn(score_prev, prev[rows, :HD])
                + nn(rest_score, far[other, :HD])
            )
        )
        kv_own[rows, :HD] += tn(score_own, query)
        prev_sum[rows, :HD] += tn(score_prev, query)
        far_sum[other, :HD] += tn(rest_score, query)
        kv_own[rows, HD:] += tn(near_own, incoming)
        prev_sum[rows, HD:] += tn(near_prev, incoming)
        far_sum[other, HD:] += tn(rest_p, incoming)
    for head in range(2):
        values, gain = rms_back(
            rot_back(grad_q[head], cosine[...], sine[...]), qraw[head], heads[0:1, :]
        )
        head_grad[0:1, :] += gain
        raw_g[head] = values.astype(BF16)
        grad_normed[...] += nt(raw_g[head], held[now, head, :, :HD])

    def store(place):
        for head in range(2):
            place[head, :, :HD] = nn(rows_t[...], raw_g[head]).astype(BF16)
            place[head, :, HD:] = nn(grad_t[...], mixed[head]).astype(BF16)

    @pl.when(step == 0)
    def _():
        store(send)

    @pl.when(step == 1)
    def _():
        store(keep)

    @pl.when(step == pl.num_programs(0) - 1)
    def _():
        kv_prev[...] = prev_sum[...].astype(BF16)


def finish_kernel(
    kv_own, kv_next, kraw, normed, kvw, heads, gains, x, grad_normed, grad_middle, cosine, sine,
    kv_grad, grad_x, grad_low, gain_grad, head_grad,
):
    summed = kv_own[...] + kv_next[...].astype(F32)
    values, gain = rms_back(
        rot_back(summed[:, :HD], cosine[...], sine[...]), kraw[...], heads[1:2, :]
    )
    head_grad[...] = gain
    grad_key = values.astype(BF16)
    grad_value = summed[:, HD:].astype(BF16)
    rows = normed[...]
    kv_grad[:, :HD] = tn(rows, grad_key).astype(BF16)
    kv_grad[:, HD:] = tn(rows, grad_value).astype(BF16)
    from_all = grad_normed[...] + nt(grad_key, kvw[:, :HD]) + nt(grad_value, kvw[:, HD : 2 * HD])
    from_norm, gain = rms_back(from_all, x[...].astype(F32), gains[0:1, :])
    gain_grad[...] = gain
    total = grad_middle[...] + from_norm
    grad_x[...] = total
    grad_low[...] = total.astype(BF16)


def whole(shape):
    zeros = (0,) * len(shape)
    return pl.BlockSpec(shape, lambda *at: zeros)


def anywhere(shape):
    return pl.BlockSpec(memory_space=pl.ANY)


def fetched(shape):
    return pl.BlockSpec(memory_space=pltpu.HBM)


def scalars(shape):
    return pl.BlockSpec(memory_space=pltpu.SMEM)


def slot(shape):
    zeros = (0,) * (len(shape) - 1)
    return pl.BlockSpec((1,) + tuple(shape[1:]), lambda at: (at,) + zeros)


def pair(shape):
    zeros = (0,) * (len(shape) - 1)
    return pl.BlockSpec((2,) + tuple(shape[1:]), lambda at: (at,) + zeros)


def early(shape):
    zeros = (0,) * (len(shape) - 1)
    return pl.BlockSpec((1,) + tuple(shape[1:]), lambda at: (jnp.minimum(at, 1),) + zeros)


def late(shape):
    zeros = (0,) * (len(shape) - 1)
    return pl.BlockSpec((1,) + tuple(shape[1:]), lambda at: (jnp.maximum(at - 2, 0),) + zeros)


def run(kernel, grid, ins, outs, scratch=(), micros=2):
    arrays = [a for a, _ in ins]
    return pl.pallas_call(
        kernel,
        grid=grid,
        in_specs=[spec(a.shape) for a, spec in ins],
        out_specs=[spec(shape) for shape, _, spec in outs],
        out_shape=[jax.ShapeDtypeStruct(shape, kind) for shape, kind, _ in outs],
        scratch_shapes=list(scratch),
        compiler_params=pltpu.CompilerParams(vmem_limit_bytes=LIMIT),
        cost_estimate=pl.CostEstimate(
            flops=micros * 1153000000, bytes_accessed=1, transcendentals=0
        ),
    )(*arrays)


def qo_scratch(width):
    return [pltpu.VMEM((2, 2, width, 2 * HD), BF16), pltpu.SemaphoreType.DMA((2, 2))]


def ff_scratch(width, units):
    return [pltpu.VMEM((2, 1, 3, width, 2 * units), BF16), pltpu.SemaphoreType.DMA((2, 2))]


def forward_keys(x, small, common):
    cosine, sine = common[:2]
    kvw, gains, heads = small
    rows, width = x.shape
    normed, kraw, kv = run(
        prep_kernel, (1,),
        [(x, whole), (gains, whole), (heads, whole), (kvw, whole), (cosine, whole), (sine, whole)],
        [((rows, width), BF16, whole), ((rows, HD), F32, whole), ((rows, 2 * HD), BF16, whole)],
        micros=2,
    )
    return normed, kraw, kv


def halo_on(kv):
    return lax.ppermute(kv, "tensor", [(i, i + 1) for i in range(lax.axis_size("tensor") - 1)])


def forward_attend(x, keys, small, choice, qo, common):
    cosine, sine, seg_col, seg_own, seg_prev = common
    kvw, gains, heads = small
    normed, kraw, kv, prev = keys
    rows, width = x.shape
    slots = len(qo)
    return run(
        attend_kernel, (slots // 2,),
        [(choice, scalars), (x, whole), (normed, whole), (gains, whole), (heads, whole),
         (kv, whole), (prev, whole), (cosine, whole), (sine, whole), (seg_col, whole),
         (seg_own, whole), (seg_prev, whole)] + [(part, fetched) for part in qo],
        [((slots, rows, HD), F32, pair), ((slots, rows, HD), BF16, pair),
         ((slots, rows, HD), BF16, pair), ((slots, rows, 1), F32, pair),
         ((rows, width), F32, whole), ((rows, width), F32, whole), ((rows, width), BF16, whole)],
        qo_scratch(width),
        micros=14,
    )


def forward_feed(attended, small, choice, ff):
    gains = small[1]
    middle, normed_two = attended[5:]
    rows, width = middle.shape
    slots, units = len(ff) // 4, ff[0].shape[2]
    return run(
        feed_kernel, (slots,),
        [(choice, scalars), (normed_two, whole), (middle, whole), (gains, whole)]
        + [(part, fetched) for part in ff],
        [((slots, rows, 2 * units), BF16, slot), ((slots, rows, 2 * units), BF16, slot),
         ((rows, width), F32, whole), ((rows, width), F32, whole), ((rows, width), BF16, whole)],
        ff_scratch(width, units),
        micros=12,
    )


def backward_feed(grad, branch, middle, normed_two, fed, small, choice, ff):
    gains = small[1]
    gate, upward, branch_two = fed[:3]
    rows, width = middle.shape
    slots, units = len(ff) // 4, ff[0].shape[2]
    half = slots // 2
    return run(
        feed_back_kernel, (slots,),
        [(choice, scalars), (grad, whole), (branch_two, whole), (middle, whole), (branch, whole),
         (normed_two, whole), (gains, whole), (gate, slot), (upward, slot)]
        + [(part, fetched) for part in ff],
        [((half, 2, 3, width, units), BF16, early), ((half, 2, 3, width, units), BF16, late),
         ((rows, width), F32, whole), ((rows, width), BF16, whole), ((4, width), F32, whole)],
        [pltpu.VMEM((rows, width), BF16), pltpu.VMEM((width, rows), BF16),
         pltpu.VMEM((width, rows), BF16), pltpu.VMEM((rows, width), F32)]
        + ff_scratch(width, units),
        micros=25,
    )


def backward_attend(grad_branch, keys, attended, small, choice, qo, common):
    cosine, sine, seg_col, seg_own, seg_prev = common
    heads = small[2]
    normed, kraw, kv, prev = keys
    qraw, q, mixed, lse = attended[:4]
    rows, width = normed.shape
    slots = len(qo)
    half = slots // 2
    return run(
        attend_back_kernel, (slots // 2,),
        [(choice, scalars), (grad_branch, whole), (normed, whole), (heads, whole), (q, pair),
         (qraw, pair), (mixed, pair), (lse, pair), (kv, whole), (prev, whole), (cosine, whole),
         (sine, whole), (seg_col, whole), (seg_own, whole), (seg_prev, whole)]
        + [(part, fetched) for part in qo],
        [((half, width, 2 * HD), BF16, whole), ((half, width, 2 * HD), BF16, whole),
         ((rows, 2 * HD), F32, whole), ((rows, 2 * HD), BF16, whole), ((rows, width), F32, whole),
         ((1, HD), F32, whole)],
        [pltpu.VMEM((width, rows), BF16), pltpu.VMEM((width, rows), BF16),
         pltpu.VMEM((rows, 2 * HD), F32), pltpu.VMEM((2, rows, HD), F32)] + qo_scratch(width)
        + [pltpu.VMEM((2, rows, HD), BF16)] * 2,
        micros=17,
    )


def backward_keys(x, kv_own, kv_next, keys, small, grad_normed, grad_middle, common):
    cosine, sine = common[:2]
    kvw, gains, heads = small
    normed, kraw = keys[:2]
    rows, width = x.shape
    return run(
        finish_kernel, (1,),
        [(kv_own, whole), (kv_next, whole), (kraw, whole), (normed, whole), (kvw, whole),
         (heads, whole), (gains, whole), (x, whole), (grad_normed, whole), (grad_middle, whole),
         (cosine, whole), (sine, whole)],
        [((width, 2 * HD), BF16, whole), ((rows, width), F32, whole), ((rows, width), BF16, whole),
         ((1, width), F32, whole),
         ((1, HD), F32, whole)],
        micros=5,
    )


def halo_back(kv_prev):
    return lax.ppermute(
        kv_prev, "tensor", [(i + 1, i) for i in range(lax.axis_size("tensor") - 1)]
    )


def tensor_pairs(bit):
    return [(i, i ^ bit) for i in range(lax.axis_size("tensor"))]


def rows_over_dp(part, cuts):
    count = lax.axis_size("dp")
    lead, columns = part.shape[:-2], part.shape[-1]
    if count > 4:
        full = jnp.moveaxis(lax.all_gather(part, "dp", axis=0), 0, -3)
        return [
            full[..., start : start + rows, :].reshape(lead + (count * rows, columns))
            for start, rows in cuts
        ]
    pieces = [part] + [
        lax.ppermute(part, "dp", [(i, (i + shift) % count) for i in range(count)])
        for shift in range(1, count)
    ]
    place = lax.axis_index("dp").astype(jnp.int32).reshape(1)
    return run(
        functools.partial(assemble_kernel, cuts), (),
        [(place, scalars)] + [(piece, anywhere) for piece in pieces],
        [(lead + (count * rows, columns), part.dtype, anywhere) for _, rows in cuts],
        [pltpu.SemaphoreType.DMA((count, len(cuts)))],
    )


def across_tensor(part):
    return lax.ppermute(part, "tensor", tensor_pairs(2))


def beside_tensor(part):
    return lax.ppermute(part, "tensor", tensor_pairs(1))


def across_section(part):
    return lax.ppermute(part, "section", [(0, 1), (1, 0)])


def after(values, *others):
    return lax.optimization_barrier((values, others))[0]


def add(left, right):
    return (left.astype(F32) + right.astype(F32)).astype(BF16)


def summed_over_dp(parts):
    count = lax.axis_size("dp")
    if count > 4:
        return [
            lax.psum_scatter(part, "dp", scatter_dimension=1, tiled=True) for part in parts
        ]
    me = lax.axis_index("dp")
    shapes = [(part.shape[0], part.shape[1] // count, part.shape[2]) for part in parts]

    def share(owner):
        blocks = [
            lax.dynamic_slice_in_dim(part, owner % count * shape[1], shape[1], 1)
            for part, shape in zip(parts, shapes)
        ]
        return jnp.concatenate([block.reshape(-1, block.shape[2]) for block in blocks])

    total = share(me).astype(F32)
    pieces = [
        lax.ppermute(share(me + shift), "dp", [(i, (i + shift) % count) for i in range(count)])
        for shift in range(1, count)
    ]
    for piece in pieces:
        total += piece.astype(F32)
    total, sums, start = total.astype(BF16), [], 0
    for shape in shapes:
        size = shape[0] * shape[1]
        sums.append(total[start : start + size].reshape(shape))
        start += size
    return sums


def side_by_side(part):
    return jnp.concatenate([part[..., :HD], part[..., HD:]])


def joined(part):
    half = part.shape[0] // 2
    return jnp.concatenate([part[:half], part[half:]], axis=-1)


def kept_sums(arrived, keep, half=None):
    if half is not None:
        arrived, keep = arrived[:, half], keep[:, half]
    return add(keep[1], arrived[1]), add(keep[0], arrived[0])


def pack_shared(kv_grad, gain_rows, head_rows):
    count = lax.axis_size("dp")
    width, columns = kv_grad.shape

    def shares(rows):
        parts = jnp.swapaxes(rows.reshape(rows.shape[0], count, -1), 0, 1)
        return jnp.pad(parts, ((0, 0), (0, 0), (0, columns - parts.shape[2])))

    small = jnp.concatenate([shares(gain_rows), shares(head_rows)], axis=1).astype(BF16)
    small = jnp.pad(small, ((0, 0), (0, 10), (0, 0)))
    return jnp.concatenate([kv_grad.reshape(count, -1, columns), small], axis=1).reshape(
        1, -1, columns
    )


def core_half(packed):
    count = lax.axis_size("dp")
    columns = packed.shape[-1]
    halves = packed.reshape(count, 2, -1, columns)
    mine = lax.axis_index("tensor") % 2

    def half(at):
        return lax.dynamic_index_in_dim(halves, at, 1, keepdims=False).reshape(1, -1, columns)

    return add(half(mine), beside_tensor(half(1 - mine)))


def body(
    section_input, cotangent, segments, query_weight, key_weight, value_weight, output_weight,
    gate_weight, up_weight, down_weight, norm_gains, head_gains,
):
    section = lax.axis_index("section")
    place = lax.axis_index("tensor")
    first = section == 0
    rows = section_input.shape[1]
    per_head = head_gains.shape[1]
    local = norm_gains.shape[1]

    gain_rows = norm_gains[0].T
    head_rows = jnp.pad(head_gains[0].T, ((0, 0), (0, local - per_head)))
    small = jnp.pad(jnp.concatenate([gain_rows, head_rows]), ((0, 10), (0, 2 * HD - local)))
    shared = jnp.concatenate(
        [
            jnp.concatenate([query_weight[0], output_weight[0]], axis=1),
            lax.dynamic_slice_in_dim(
                jnp.concatenate([key_weight[0], value_weight[0]], axis=1),
                place % 2 * (local // 2), local // 2, 0,
            ),
            small,
        ]
    )
    cuts = ((0, local), (local, local // 2), (local + local // 2, 16))
    units = gate_weight.shape[2] // 2
    feeds = [
        jnp.stack([w[0, :, half * units : (half + 1) * units]
                   for w in (gate_weight, up_weight, down_weight)])
        for half in range(2)
    ]
    other = across_section(shared)
    own_segments = lax.dynamic_index_in_dim(segments, section, 0, keepdims=False)
    length = own_segments.shape[0]
    places = jnp.arange(length, dtype=jnp.int32)
    before = jnp.concatenate([own_segments[:1] - 1, own_segments[:-1]])
    starts = lax.cummax(jnp.where(own_segments != before, places, 0), axis=0)
    positions = lax.dynamic_slice_in_dim(places - starts, place * rows, rows, 0)
    inverse = jnp.exp(-jnp.log(10000.0) * jnp.arange(HALF, dtype=F32) / HALF)
    angle = positions.astype(F32)[:, None] * inverse[None, :]
    here = lax.dynamic_slice_in_dim(own_segments, place * rows, rows, 0)
    padded = jnp.concatenate([jnp.full((rows,), -1, jnp.int32), own_segments])
    prior = lax.dynamic_slice_in_dim(padded, place * rows, rows, 0)
    common = (jnp.cos(angle), jnp.sin(angle), here[:, None], here[None, :], prior[None, :])

    x0 = lax.dynamic_index_in_dim(section_input, section, 0, keepdims=False)
    grad = lax.dynamic_index_in_dim(cotangent, section, 0, keepdims=False)
    count = lax.axis_size("dp")

    def small_of(gathered):
        rows = gathered[2].reshape(count, 16, 2 * HD).astype(F32)
        gains = jnp.swapaxes(rows[:, :4, :local], 0, 1).reshape(4, count * local)
        heads = jnp.swapaxes(rows[:, 4:6, :per_head], 0, 1).reshape(2, HD)
        mine, other = gathered[1], beside_tensor(gathered[1])
        halves = [jnp.where(place % 2 == at, mine, other) for at in range(2)]
        halves = [half.reshape(count, 1, -1, 2 * HD) for half in halves]
        return jnp.concatenate(halves, axis=1).reshape(-1, 2 * HD), gains, heads

    choices = [(section == layer).astype(jnp.int32).reshape(1) for layer in range(2)]
    shared_l = [jnp.where(first, shared, other), jnp.where(first, other, shared)]

    whole_cut = ((0, local),)
    gathered0 = rows_over_dp(shared_l[0], cuts)
    feed_in, qo_mine, kvw0, rows0, x0 = after((feeds[0], *gathered0, x0))
    qo_across = across_tensor(qo_mine)
    feed_a = rows_over_dp(feed_in, whole_cut)[0]
    small0 = small_of((qo_mine, kvw0, rows0))
    feed_a, feed_in, qo_across, small0 = after((feed_a, feeds[1], qo_across, small0))
    keys0 = forward_keys(x0, small0, common)
    other_a, mine_a = across_section(feed_a), across_tensor(feed_a)
    feed_b = rows_over_dp(feed_in, whole_cut)[0]
    prev0 = halo_on(keys0[2])
    other_a, mine_a, feed_b = after((other_a, mine_a, feed_b))
    qo0 = [beside_tensor(qo_mine), beside_tensor(qo_across), qo_mine, qo_across]
    other_b, mine_b = across_section(feed_b), across_tensor(feed_b)
    keys0 = (*keys0, prev0)
    qo0, keys0 = after((qo0, keys0))
    beside_a = [beside_tensor(part) for part in (feed_a, mine_a, other_a)]
    attended0 = forward_attend(x0, keys0, small0, choices[0], qo0, common)
    other_a, other_b, mine_b, beside_a, attended0, shared1 = after(
        (other_a, other_b, mine_b, beside_a, attended0, shared_l[1])
    )
    far_a, far_b = across_tensor(other_a), across_section(mine_b)
    gathered1 = rows_over_dp(shared1, cuts)
    far_a, far_b, mine_b, other_b, gathered1 = after((far_a, far_b, mine_b, other_b, gathered1))
    beside_b = [beside_tensor(part) for part in (feed_b, mine_b, other_b)]
    beside_far = [beside_tensor(far_a), beside_tensor(far_b)]
    small1 = small_of(gathered1)
    qo_mine1, beside_b, beside_far = after((gathered1[0], beside_b, beside_far))
    ff = [beside_a[0], beside_b[0], beside_a[1], beside_b[1], feed_a, feed_b, mine_a, mine_b,
          beside_a[2], beside_b[2], *beside_far, other_a, other_b, far_a, far_b]
    qo_across1 = across_tensor(qo_mine1)
    fed0 = forward_feed(attended0, small0, choices[0], ff)
    out0, x1 = fed0[3:]
    keys1 = forward_keys(x1, small1, common)
    keys1, qo_across1 = after((keys1, qo_across1))
    prev1 = halo_on(keys1[2])
    qo1 = [beside_tensor(qo_mine1), beside_tensor(qo_across1), qo_mine1, qo_across1]
    x1, prev1, qo1 = after((x1, prev1, qo1))
    keys1 = (*keys1, prev1)
    attended1 = forward_attend(x1, keys1, small1, choices[1], qo1, common)
    fed1 = forward_feed(attended1, small1, choices[1], ff)
    out1, out1_low = fed1[3:]

    def packed(kv, gain, key, fed, at):
        return pack_shared(
            kv, jnp.concatenate([gain, fed[4][:3]]), jnp.concatenate([at[5], key])
        )

    out_got = across_section(jnp.where(first, out1_low, x1))
    ff1 = backward_feed(grad, *attended1[4:], fed1, small1, choices[1], ff)
    ff1, out_got = after((ff1, out_got))
    ff1_core = beside_tensor(ff1[0])
    at1 = backward_attend(ff1[3], keys1, attended1, small1, choices[1], qo1, common)
    at1, ff1_core = after((at1, ff1_core))
    next1 = halo_back(at1[3])
    qo1_core = beside_tensor(at1[0])
    sums1 = [kept_sums(ff1_core, ff1[1], half) for half in range(2)]
    next1, qo1_core, sums1 = after((next1, qo1_core, sums1))
    across1a = across_tensor(sums1[0][0])
    kv1, grad1, grad1_low, gain1, key1 = backward_keys(
        x1, at1[2], next1, keys1, small1, at1[4], ff1[2], common
    )
    ff0 = backward_feed(grad1_low, *attended0[4:], fed0, small0, choices[0], ff)
    across1a, ff0, sums1, qo1_core = after((across1a, ff0, sums1, qo1_core))
    ff0_core = beside_tensor(ff0[0])
    across1b = across_tensor(sums1[1][0])
    at0 = backward_attend(ff0[3], keys0, attended0, small0, choices[0], qo0, common)
    pair1 = kept_sums(qo1_core, at1[1])
    at0, ff0_core, across1b, pair1, kv1 = after((at0, ff0_core, across1b, pair1, kv1))
    pair1_across = across_tensor(pair1[0])
    rest1 = core_half(packed(kv1, gain1, key1, ff1, at1))[0]
    next0 = halo_back(at0[3])
    qo0_core = beside_tensor(at0[0])
    sums0 = [kept_sums(ff0_core, ff0[1], half) for half in range(2)]
    across0a = across_tensor(sums0[0][0])
    kv0, grad0, grad0_low, gain0, key0 = backward_keys(
        x0, at0[2], next0, keys0, small0, at0[4], ff0[2], common
    )
    grad_got = across_section(jnp.where(first, grad1_low, grad0_low))
    pair0 = kept_sums(qo0_core, at0[1])
    rest0 = core_half(packed(kv0, gain0, key0, ff0, at0))[0]
    full1 = [add(sums1[0][1], across1a), add(sums1[1][1], across1b)]
    pair1 = add(pair1[1], pair1_across)
    across0a, rest0, rest1, pair0, pair1, sums0, full1, grad_got = after(
        (across0a, rest0, rest1, pair0, pair1, sums0, full1, grad_got)
    )

    def swapped(zero, one):
        return add(jnp.where(first, zero, one), across_section(jnp.where(first, one, zero)))

    across0b = across_tensor(sums0[1][0])
    feed_a = swapped(add(sums0[0][1], across0a), full1[0])
    low0 = jnp.concatenate([pair0[0], rest0, rest1])
    across0b, feed_a, low0, sums0 = after((across0b, feed_a, low0, sums0))
    low0_across = across_tensor(low0)
    feed_b = swapped(add(sums0[1][1], across0b), full1[1])
    feed_a = summed_over_dp([feed_a])[0]
    low0_across, feed_a, feed_b = after((low0_across, feed_a, feed_b))
    size = low0.shape[0] - rest1.shape[0]
    low = swapped(
        add(jnp.concatenate([pair0[1], rest0]), low0_across[:size]),
        jnp.concatenate([pair1, add(rest1, low0_across[size:])]),
    )
    feed_b = summed_over_dp([feed_b])[0]
    feed_b, low = after((feed_b, low))
    pair_rows = pair0[0].shape[0]
    pair, rest = summed_over_dp(
        [side_by_side(low[None, :pair_rows]), side_by_side(low[None, pair_rows:])]
    )
    pair, rest = joined(pair).astype(F32), joined(rest)[0]
    beside = beside_tensor(rest)
    even = place % 2 == 0
    rest = jnp.concatenate(
        [jnp.where(even, rest, beside), jnp.where(even, beside, rest)]
    ).astype(F32)
    feed = jnp.stack([feed_a, feed_b]).astype(F32)

    def placed(zero, one, got):
        got = got.astype(F32)
        return jnp.stack([jnp.where(first, zero, got), jnp.where(first, got, one)])[None]

    return (
        placed(out0, out1, out_got),
        placed(grad0, grad1, grad_got),
        pair[:, :, :HD],
        rest[None, :local, :HD],
        rest[None, :local, HD:],
        pair[:, :, HD:],
        *[jnp.concatenate([feed[0, n], feed[1, n]], axis=1)[None] for n in range(3)],
        rest[local : local + 4, :local].T[None],
        rest[local + 4 : local + 6, :per_head].T[None],
    )


def solution(mesh):
    return jax.shard_map(
        body,
        mesh=mesh,
        in_specs=(
            P(None, ("dp", "tensor"), None),
            P(None, ("dp", "tensor"), None),
            P(None, "dp"),
            P("section", "dp", "tensor"),
            P("section", "dp", None),
            P("section", "dp", None),
            P("section", "dp", "tensor"),
            P("section", "dp", "tensor"),
            P("section", "dp", "tensor"),
            P("section", "dp", "tensor"),
            P("section", "dp", None),
            P("section", "dp", None),
        ),
        out_specs=(
            P("section", None, ("dp", "tensor"), None),
            P("section", None, ("dp", "tensor"), None),
            P("section", "dp", "tensor"),
            P("section", "dp", None),
            P("section", "dp", None),
            P("section", "dp", "tensor"),
            P("section", "dp", "tensor"),
            P("section", "dp", "tensor"),
            P("section", "dp", "tensor"),
            P("section", "dp", None),
            P("section", "dp", None),
        ),
        check_vma=False,
    )
```

```python
import functools

import jax
import jax.numpy as jnp
from jax import lax
from jax.experimental import pallas as pl
from jax.experimental.pallas import tpu as pltpu
from jax.sharding import PartitionSpec as P

HD = 256
HALF = HD // 2
WIN = 512
BLK = 256
EPS = 1e-06
F32 = jnp.float32
BF16 = jnp.bfloat16
LIMIT = 50 * 1024 * 1024


def nn(a, b):
    return lax.dot_general(a, b, (((1,), (0,)), ((), ())), preferred_element_type=F32)


def nt(a, b):
    return lax.dot_general(a, b, (((1,), (1,)), ((), ())), preferred_element_type=F32)


def tn(a, b):
    return lax.dot_general(a, b, (((0,), (0,)), ((), ())), preferred_element_type=F32)


def rms(values, gain):
    return values * lax.rsqrt(jnp.mean(values * values, axis=-1, keepdims=True) + EPS) * gain


def rms_back(grad, values, gain):
    scale = lax.rsqrt(jnp.mean(values * values, axis=-1, keepdims=True) + EPS)
    unit = values * scale
    scaled = grad * gain
    inner = jnp.mean(scaled * unit, axis=-1, keepdims=True)
    return scale * (scaled - unit * inner), jnp.sum(grad * unit, axis=0, keepdims=True)


def rot(values, cosine, sine):
    a, b = values[:, :HALF], values[:, HALF:]
    return jnp.concatenate([a * cosine - b * sine, b * cosine + a * sine], axis=-1)


def rot_back(grad, cosine, sine):
    a, b = grad[:, :HALF], grad[:, HALF:]
    return jnp.concatenate([a * cosine + b * sine, b * cosine - a * sine], axis=-1)


GELU_A = 0.7978845608028654
GELU_B = 0.044715


def triangle():
    row = lax.broadcasted_iota(jnp.int32, (BLK, BLK), 0)
    column = lax.broadcasted_iota(jnp.int32, (BLK, BLK), 1)
    return column <= row


def tiles(block):
    rows = slice(block * BLK, (block + 1) * BLK)
    other = slice((1 - block) * BLK, (2 - block) * BLK)
    return rows, other, block == 1


def masks(block, lower, seg_col, seg_own, seg_prev):
    rows, other, own = tiles(block)
    mine = seg_col[rows, :]
    diagonal = mine == jnp.where(lower, seg_own[:, rows], seg_prev[:, rows])
    rest = mine == (seg_own if own else seg_prev)[:, other]
    return diagonal, rest


def stream(step, choice, own, other, held, arrived):
    def spot(index, part):
        if len(held.shape) == 4:
            return held.at[index, part]
        columns = held.shape[4] // 2
        return held.at[index, 0, :, :, pl.ds(part * columns, columns)]

    def fetch(index):
        for wanted, slots in ((1, own), (0, other)):

            @pl.when(choice[0] == wanted)
            def _(slots=slots):
                for part, ref in enumerate(slots[index]):
                    pltpu.make_async_copy(
                        ref, spot(index % 2, part), arrived.at[index % 2, part]
                    ).start()

    @pl.when(step == 0)
    def _():
        fetch(0)

    for index in range(1, len(own)):

        @pl.when(step == index - 1)
        def _(index=index):
            fetch(index)

    now = lax.rem(step, 2)
    for part, ref in enumerate(own[0]):
        pltpu.make_async_copy(ref, spot(now, part), arrived.at[now, part]).wait()
    return now


def assemble_kernel(cuts, place, *refs):
    count = (len(refs) - len(cuts) - 1)
    pieces, outs, done = refs[:count], refs[count:-1], refs[-1]
    copies = []
    for shift, piece in enumerate(pieces):
        owner = lax.rem(place[0] + count - shift, count)
        for cut, (start, rows) in enumerate(cuts):
            at = pl.ds(pl.multiple_of(owner * rows, rows), rows)
            lead = (slice(None),) * (len(piece.shape) - 2)
            copies.append(
                pltpu.make_async_copy(
                    piece.at[lead + (pl.ds(start, rows),)],
                    outs[cut].at[lead + (at,)],
                    done.at[shift, cut],
                )
            )
    for copy in copies:
        copy.start()
    for copy in copies:
        copy.wait()


def prep_kernel(x, gains, heads, kvw, cosine, sine, normed, kraw, kv):
    rows = rms(x[...].astype(F32), gains[0:1, :]).astype(BF16)
    normed[...] = rows
    raw = nn(rows, kvw[:, :HD])
    kraw[...] = raw
    kv[:, :HD] = rot(rms(raw, heads[1:2, :]), cosine[...], sine[...]).astype(BF16)
    kv[:, HD:] = nn(rows, kvw[:, HD : 2 * HD]).astype(BF16)


def flat(tile):
    return tile.reshape(-1, tile.shape[-1])


def tall(tile):
    return tile.reshape(2, -1, tile.shape[-1])


def attend_kernel(
    choice, x, normed, gains, heads, own, prev, cosine, sine, seg_col, seg_own, seg_prev,
    qo_a, qo_b, qo_c, qo_d, qraw, q, mixed, lse, branch, middle, normed_two, held, arrived,
):
    step = pl.program_id(0)
    slots = [[qo_a, qo_b], [qo_c, qo_d]]
    now = stream(step, choice, slots, slots, held, arrived)
    for head in range(2):
        raw = nn(normed[...], held[now, head, :, :HD])
        qraw[head] = raw
        turned = rot(rms(raw, heads[0:1, :]), cosine[...], sine[...]).astype(BF16)
        q[head] = turned * jnp.asarray(0.0625, BF16)
    lower = triangle()
    for block in range(2):
        rows, other, is_own = tiles(block)
        diagonal, rest = masks(block, lower, seg_col[...], seg_own[...], seg_prev[...])
        query = flat(q[:, rows, :])
        far = own if is_own else prev
        near_scores = jnp.where(
            lower, tall(nt(query, own[rows, :HD])), tall(nt(query, prev[rows, :HD]))
        )
        near_scores = jnp.where(diagonal, near_scores, -1e30)
        far_scores = jnp.where(rest, tall(nt(query, far[other, :HD])), -1e30)
        largest = jnp.maximum(
            jnp.max(near_scores, axis=-1, keepdims=True),
            jnp.max(far_scores, axis=-1, keepdims=True),
        )
        near = jnp.exp(near_scores - largest)
        rest_p = jnp.exp(far_scores - largest)
        total = jnp.sum(near, axis=-1, keepdims=True) + jnp.sum(rest_p, axis=-1, keepdims=True)
        inverse = 1.0 / total
        near = near * inverse
        rest_p = (rest_p * inverse).astype(BF16)
        near_own = jnp.where(lower, near, 0.0).astype(BF16)
        near_prev = jnp.where(lower, 0.0, near).astype(BF16)
        mixed[:, rows, :] = tall(
            nn(flat(near_own), own[rows, HD:])
            + nn(flat(near_prev), prev[rows, HD:])
            + nn(flat(rest_p), far[other, HD:])
        ).astype(BF16)
        lse[:, rows, :] = largest + jnp.log(total)
    part = nt(mixed[0], held[now, 0, :, HD:]) + nt(mixed[1], held[now, 1, :, HD:])

    @pl.when(step == 0)
    def _():
        branch[...] = part

    @pl.when(step > 0)
    def _():
        branch[...] += part

    @pl.when(step == pl.num_programs(0) - 1)
    def _():
        mid = x[...].astype(F32) + rms(branch[...], gains[1:2, :])
        middle[...] = mid
        normed_two[...] = rms(mid, gains[2:3, :]).astype(BF16)


def slots_of(refs):
    halves = [[refs[at], refs[at + 1]] for at in range(0, len(refs), 2)]
    return halves[: len(halves) // 2], halves[len(halves) // 2 :]


def feed_kernel(choice, normed_two, middle, gains, *refs):
    own, other = slots_of(refs[:16])
    gate_out, up_out, branch_two, out, out_low, held, arrived = refs[16:]
    step = pl.program_id(0)
    now = stream(step, choice, own, other, held, arrived)
    rows = normed_two[...]
    gate = nn(rows, held[now, 0, 0])
    upward = nn(rows, held[now, 0, 1])
    gate_out[0] = gate.astype(BF16)
    up_out[0] = upward.astype(BF16)
    wave = jnp.tanh(GELU_A * gate * (1.0 + GELU_B * gate * gate))
    hidden = (0.5 * gate * (1.0 + wave) * upward).astype(BF16)
    part = nt(hidden, held[now, 0, 2])

    @pl.when(step == 0)
    def _():
        branch_two[...] = part

    @pl.when(step > 0)
    def _():
        branch_two[...] += part

    @pl.when(step == pl.num_programs(0) - 1)
    def _():
        total = middle[...] + rms(branch_two[...], gains[3:4, :])
        out[...] = total
        out_low[...] = total.astype(BF16)


def feed_back_kernel(
    choice, grad, branch_two, middle, branch, normed_two, gains, gate_in, up_in, *refs
):
    own, other = slots_of(refs[:16])
    send, keep, grad_middle, grad_branch, gain_grads = refs[16:21]
    incoming, incoming_t, rows_t, total, held, arrived = refs[21:]
    step = pl.program_id(0)
    now = stream(step, choice, own, other, held, arrived)

    @pl.when(step == 0)
    def _():
        values, gain = rms_back(grad[...].astype(F32), branch_two[...], gains[3:4, :])
        incoming[...] = values.astype(BF16)
        incoming_t[...] = values.T.astype(BF16)
        rows_t[...] = normed_two[...].T
        gain_grads[2:3, :] = gain
        gain_grads[3:4, :] = jnp.zeros_like(gain)

    gate = gate_in[0].astype(F32)
    upward = up_in[0].astype(F32)
    square = gate * gate
    wave = jnp.tanh(GELU_A * gate * (1.0 + GELU_B * square))
    bell = 0.5 * (1.0 + wave)
    active = gate * bell
    slope = bell + gate * (1.0 - wave * wave) * (0.5 * GELU_A * (1.0 + 3.0 * GELU_B * square))
    grad_hidden = nn(incoming[...], held[now, 0, 2])
    grad_up = (grad_hidden * active).astype(BF16)
    grad_gate = (grad_hidden * upward * slope).astype(BF16)
    hidden = (active * upward).astype(BF16)
    columns = hidden.shape[1] // 2

    def store(place):
        for number, (left, right) in enumerate(
            ((rows_t, grad_gate), (rows_t, grad_up), (incoming_t, hidden))
        ):
            value = nn(left[...], right).astype(BF16)
            place[0, 0, number] = value[:, :columns]
            place[0, 1, number] = value[:, columns:]

    @pl.when(step < 2)
    def _():
        store(send)

    @pl.when(step >= 2)
    def _():
        store(keep)

    part = nt(grad_gate, held[now, 0, 0]) + nt(grad_up, held[now, 0, 1])

    @pl.when(step == 0)
    def _():
        total[...] = part

    @pl.when(step > 0)
    def _():
        total[...] += part

    @pl.when(step == pl.num_programs(0) - 1)
    def _():
        from_norm, gain = rms_back(total[...], middle[...], gains[2:3, :])
        gain_grads[1:2, :] = gain
        mid = grad[...].astype(F32) + from_norm
        grad_middle[...] = mid
        values, gain = rms_back(mid, branch[...], gains[1:2, :])
        gain_grads[0:1, :] = gain
        grad_branch[...] = values.astype(BF16)


def attend_back_kernel(
    choice, grad_branch, normed, heads, q, qraw, mixed, lse, own, prev, cosine, sine,
    seg_col, seg_own, seg_prev, qo_a, qo_b, qo_c, qo_d,
    send, keep, kv_own, kv_prev, grad_normed, head_grad, grad_t, rows_t, prev_sum, grad_q,
    held, arrived, mixed_g, raw_g,
):
    step = pl.program_id(0)
    slots = [[qo_a, qo_b], [qo_c, qo_d]]
    now = stream(step, choice, slots, slots, held, arrived)

    @pl.when(step == 0)
    def _():
        grad_t[...] = grad_branch[...].T
        rows_t[...] = normed[...].T
        kv_own[...] = jnp.zeros_like(kv_own)
        prev_sum[...] = jnp.zeros_like(prev_sum)
        grad_normed[...] = jnp.zeros_like(grad_normed)
        head_grad[...] = jnp.zeros_like(head_grad)

    for head in range(2):
        mixed_g[head] = nn(grad_branch[...], held[now, head, :, HD:]).astype(BF16)
    lower = triangle()
    for block in range(2):
        rows, other, is_own = tiles(block)
        diagonal, rest = masks(block, lower, seg_col[...], seg_own[...], seg_prev[...])
        query = flat(q[:, rows, :])
        incoming = flat(mixed_g[:, rows, :])
        far = own if is_own else prev
        far_sum = kv_own if is_own else prev_sum
        log_total = lse[:, rows, :]
        near_scores = jnp.where(
            lower, tall(nt(query, own[rows, :HD])), tall(nt(query, prev[rows, :HD]))
        )
        near = jnp.exp(jnp.where(diagonal, near_scores, -1e30) - log_total)
        rest_p = jnp.exp(jnp.where(rest, tall(nt(query, far[other, :HD])), -1e30) - log_total)
        near_grad = jnp.where(
            lower, tall(nt(incoming, own[rows, HD:])), tall(nt(incoming, prev[rows, HD:]))
        )
        rest_grad = tall(nt(incoming, far[other, HD:]))
        inner = jnp.sum(near * near_grad, axis=-1, keepdims=True) + jnp.sum(
            rest_p * rest_grad, axis=-1, keepdims=True
        )
        near_score = near * (near_grad - inner)
        rest_score = flat(rest_p * (rest_grad - inner)).astype(BF16)
        score_own = flat(jnp.where(lower, near_score, 0.0)).astype(BF16)
        score_prev = flat(jnp.where(lower, 0.0, near_score)).astype(BF16)
        near_own = flat(jnp.where(lower, near, 0.0)).astype(BF16)
        near_prev = flat(jnp.where(lower, 0.0, near)).astype(BF16)
        rest_p = flat(rest_p).astype(BF16)
        grad_q[:, rows, :] = tall(
            0.0625
            * (
                nn(score_own, own[rows, :HD])
                + nn(score_prev, prev[rows, :HD])
                + nn(rest_score, far[other, :HD])
            )
        )
        kv_own[rows, :HD] += tn(score_own, query)
        prev_sum[rows, :HD] += tn(score_prev, query)
        far_sum[other, :HD] += tn(rest_score, query)
        kv_own[rows, HD:] += tn(near_own, incoming)
        prev_sum[rows, HD:] += tn(near_prev, incoming)
        far_sum[other, HD:] += tn(rest_p, incoming)
    for head in range(2):
        values, gain = rms_back(
            rot_back(grad_q[head], cosine[...], sine[...]), qraw[head], heads[0:1, :]
        )
        head_grad[0:1, :] += gain
        raw_g[head] = values.astype(BF16)
        grad_normed[...] += nt(raw_g[head], held[now, head, :, :HD])

    def store(place):
        for head in range(2):
            place[head, :, :HD] = nn(rows_t[...], raw_g[head]).astype(BF16)
            place[head, :, HD:] = nn(grad_t[...], mixed[head]).astype(BF16)

    @pl.when(step == 0)
    def _():
        store(send)

    @pl.when(step == 1)
    def _():
        store(keep)

    @pl.when(step == pl.num_programs(0) - 1)
    def _():
        kv_prev[...] = prev_sum[...].astype(BF16)


def finish_kernel(
    kv_own, kv_next, kraw, normed, kvw, heads, gains, x, grad_normed, grad_middle, cosine, sine,
    kv_grad, grad_x, grad_low, gain_grad, head_grad,
):
    summed = kv_own[...] + kv_next[...].astype(F32)
    values, gain = rms_back(
        rot_back(summed[:, :HD], cosine[...], sine[...]), kraw[...], heads[1:2, :]
    )
    head_grad[...] = gain
    grad_key = values.astype(BF16)
    grad_value = summed[:, HD:].astype(BF16)
    rows = normed[...]
    kv_grad[:, :HD] = tn(rows, grad_key).astype(BF16)
    kv_grad[:, HD:] = tn(rows, grad_value).astype(BF16)
    from_all = grad_normed[...] + nt(grad_key, kvw[:, :HD]) + nt(grad_value, kvw[:, HD : 2 * HD])
    from_norm, gain = rms_back(from_all, x[...].astype(F32), gains[0:1, :])
    gain_grad[...] = gain
    total = grad_middle[...] + from_norm
    grad_x[...] = total
    grad_low[...] = total.astype(BF16)


def whole(shape):
    zeros = (0,) * len(shape)
    return pl.BlockSpec(shape, lambda *at: zeros)


def anywhere(shape):
    return pl.BlockSpec(memory_space=pl.ANY)


def fetched(shape):
    return pl.BlockSpec(memory_space=pltpu.HBM)


def resident(shape):
    return pl.BlockSpec(memory_space=pltpu.VMEM)


def scalars(shape):
    return pl.BlockSpec(memory_space=pltpu.SMEM)


def slot(shape):
    zeros = (0,) * (len(shape) - 1)
    return pl.BlockSpec((1,) + tuple(shape[1:]), lambda at: (at,) + zeros)


def pair(shape):
    zeros = (0,) * (len(shape) - 1)
    return pl.BlockSpec((2,) + tuple(shape[1:]), lambda at: (at,) + zeros)


def early(shape):
    zeros = (0,) * (len(shape) - 1)
    return pl.BlockSpec((1,) + tuple(shape[1:]), lambda at: (jnp.minimum(at, 1),) + zeros)


def late(shape):
    zeros = (0,) * (len(shape) - 1)
    return pl.BlockSpec((1,) + tuple(shape[1:]), lambda at: (jnp.maximum(at - 2, 0),) + zeros)


def run(kernel, grid, ins, outs, scratch=(), micros=2):
    arrays = [a for a, _ in ins]
    return pl.pallas_call(
        kernel,
        grid=grid,
        in_specs=[spec(a.shape) for a, spec in ins],
        out_specs=[spec(shape) for shape, _, spec in outs],
        out_shape=[jax.ShapeDtypeStruct(shape, kind) for shape, kind, _ in outs],
        scratch_shapes=list(scratch),
        compiler_params=pltpu.CompilerParams(vmem_limit_bytes=LIMIT),
        cost_estimate=pl.CostEstimate(
            flops=micros * 1153000000, bytes_accessed=1, transcendentals=0
        ),
    )(*arrays)


def qo_scratch(width):
    return [pltpu.VMEM((2, 2, width, 2 * HD), BF16), pltpu.SemaphoreType.DMA((2, 2))]


def ff_scratch(width, units):
    return [pltpu.VMEM((2, 1, 3, width, 2 * units), BF16), pltpu.SemaphoreType.DMA((2, 2))]


def forward_keys(x, small, common):
    cosine, sine = common[:2]
    kvw, gains, heads = small
    rows, width = x.shape
    normed, kraw, kv = run(
        prep_kernel, (1,),
        [(x, whole), (gains, whole), (heads, whole), (kvw, whole), (cosine, whole), (sine, whole)],
        [((rows, width), BF16, whole), ((rows, HD), F32, whole), ((rows, 2 * HD), BF16, whole)],
        micros=2,
    )
    return normed, kraw, kv


def halo_on(kv):
    return lax.ppermute(kv, "tensor", [(i, i + 1) for i in range(lax.axis_size("tensor") - 1)])


def forward_attend(x, keys, small, choice, qo, common):
    cosine, sine, seg_col, seg_own, seg_prev = common
    kvw, gains, heads = small
    normed, kraw, kv, prev = keys
    rows, width = x.shape
    slots = len(qo)
    return run(
        attend_kernel, (slots // 2,),
        [(choice, scalars), (x, whole), (normed, whole), (gains, whole), (heads, whole),
         (kv, whole), (prev, whole), (cosine, whole), (sine, whole), (seg_col, whole),
         (seg_own, whole), (seg_prev, whole)] + [(part, fetched) for part in qo],
        [((slots, rows, HD), F32, pair), ((slots, rows, HD), BF16, pair),
         ((slots, rows, HD), BF16, pair), ((slots, rows, 1), F32, pair),
         ((rows, width), F32, whole), ((rows, width), F32, whole), ((rows, width), BF16, whole)],
        qo_scratch(width),
        micros=14,
    )


def forward_feed(attended, small, choice, ff):
    gains = small[1]
    middle, normed_two = attended[5:]
    rows, width = middle.shape
    slots, units = len(ff) // 4, ff[0].shape[2]
    return run(
        feed_kernel, (slots,),
        [(choice, scalars), (normed_two, whole), (middle, whole), (gains, whole)]
        + [(part, fetched) for part in ff],
        [((slots, rows, 2 * units), BF16, slot), ((slots, rows, 2 * units), BF16, slot),
         ((rows, width), F32, whole), ((rows, width), F32, whole), ((rows, width), BF16, whole)],
        ff_scratch(width, units),
        micros=12,
    )


def backward_feed(grad, branch, middle, normed_two, fed, small, choice, ff):
    gains = small[1]
    gate, upward, branch_two = fed[:3]
    rows, width = middle.shape
    slots, units = len(ff) // 4, ff[0].shape[2]
    half = slots // 2
    return run(
        feed_back_kernel, (slots,),
        [(choice, scalars), (grad, whole), (branch_two, whole), (middle, whole), (branch, whole),
         (normed_two, whole), (gains, whole), (gate, slot), (upward, slot)]
        + [(part, fetched) for part in ff],
        [((half, 2, 3, width, units), BF16, early), ((half, 2, 3, width, units), BF16, late),
         ((rows, width), F32, whole), ((rows, width), BF16, whole), ((4, width), F32, whole)],
        [pltpu.VMEM((rows, width), BF16), pltpu.VMEM((width, rows), BF16),
         pltpu.VMEM((width, rows), BF16), pltpu.VMEM((rows, width), F32)]
        + ff_scratch(width, units),
        micros=25,
    )


def backward_attend(grad_branch, keys, attended, small, choice, qo, common):
    cosine, sine, seg_col, seg_own, seg_prev = common
    heads = small[2]
    normed, kraw, kv, prev = keys
    qraw, q, mixed, lse = attended[:4]
    rows, width = normed.shape
    slots = len(qo)
    half = slots // 2
    return run(
        attend_back_kernel, (slots // 2,),
        [(choice, scalars), (grad_branch, whole), (normed, whole), (heads, whole), (q, pair),
         (qraw, pair), (mixed, pair), (lse, pair), (kv, whole), (prev, whole), (cosine, whole),
         (sine, whole), (seg_col, whole), (seg_own, whole), (seg_prev, whole)]
        + [(part, fetched) for part in qo],
        [((half, width, 2 * HD), BF16, whole), ((half, width, 2 * HD), BF16, whole),
         ((rows, 2 * HD), F32, whole), ((rows, 2 * HD), BF16, whole), ((rows, width), F32, whole),
         ((1, HD), F32, whole)],
        [pltpu.VMEM((width, rows), BF16), pltpu.VMEM((width, rows), BF16),
         pltpu.VMEM((rows, 2 * HD), F32), pltpu.VMEM((2, rows, HD), F32)] + qo_scratch(width)
        + [pltpu.VMEM((2, rows, HD), BF16)] * 2,
        micros=17,
    )


def backward_keys(x, kv_own, kv_next, keys, small, grad_normed, grad_middle, common):
    cosine, sine = common[:2]
    kvw, gains, heads = small
    normed, kraw = keys[:2]
    rows, width = x.shape
    return run(
        finish_kernel, (1,),
        [(kv_own, whole), (kv_next, whole), (kraw, whole), (normed, whole), (kvw, whole),
         (heads, whole), (gains, whole), (x, whole), (grad_normed, whole), (grad_middle, whole),
         (cosine, whole), (sine, whole)],
        [((width, 2 * HD), BF16, whole), ((rows, width), F32, whole), ((rows, width), BF16, whole),
         ((1, width), F32, whole),
         ((1, HD), F32, whole)],
        micros=5,
    )


def halo_back(kv_prev):
    return lax.ppermute(
        kv_prev, "tensor", [(i + 1, i) for i in range(lax.axis_size("tensor") - 1)]
    )


def tensor_pairs(bit):
    return [(i, i ^ bit) for i in range(lax.axis_size("tensor"))]


def rows_over_dp(part, cuts):
    count = lax.axis_size("dp")
    lead, columns = part.shape[:-2], part.shape[-1]
    if count > 4:
        full = jnp.moveaxis(lax.all_gather(part, "dp", axis=0), 0, -3)
        return [
            full[..., start : start + rows, :].reshape(lead + (count * rows, columns))
            for start, rows in cuts
        ]
    pieces = [part] + [
        lax.ppermute(part, "dp", [(i, (i + shift) % count) for i in range(count)])
        for shift in range(1, count)
    ]
    place = lax.axis_index("dp").astype(jnp.int32).reshape(1)
    return run(
        functools.partial(assemble_kernel, cuts), (),
        [(place, scalars)] + [(piece, resident) for piece in pieces],
        [(lead + (count * rows, columns), part.dtype, anywhere) for _, rows in cuts],
        [pltpu.SemaphoreType.DMA((count, len(cuts)))],
    )


def across_tensor(part):
    return lax.ppermute(part, "tensor", tensor_pairs(2))


def beside_tensor(part):
    return lax.ppermute(part, "tensor", tensor_pairs(1))


def across_section(part):
    return lax.ppermute(part, "section", [(0, 1), (1, 0)])


def after(values, *others):
    return lax.optimization_barrier((values, others))[0]


def add(left, right):
    return (left.astype(F32) + right.astype(F32)).astype(BF16)


def summed_over_dp(parts):
    count = lax.axis_size("dp")
    if count > 4:
        return [
            lax.psum_scatter(part, "dp", scatter_dimension=1, tiled=True) for part in parts
        ]
    me = lax.axis_index("dp")
    shapes = [(part.shape[0], part.shape[1] // count, part.shape[2]) for part in parts]

    def share(owner):
        blocks = [
            lax.dynamic_slice_in_dim(part, owner % count * shape[1], shape[1], 1)
            for part, shape in zip(parts, shapes)
        ]
        return jnp.concatenate([block.reshape(-1, block.shape[2]) for block in blocks])

    total = share(me).astype(F32)
    pieces = [
        lax.ppermute(share(me + shift), "dp", [(i, (i + shift) % count) for i in range(count)])
        for shift in range(1, count)
    ]
    for piece in pieces:
        total += piece.astype(F32)
    total, sums, start = total.astype(BF16), [], 0
    for shape in shapes:
        size = shape[0] * shape[1]
        sums.append(total[start : start + size].reshape(shape))
        start += size
    return sums


def side_by_side(part):
    return jnp.concatenate([part[..., :HD], part[..., HD:]])


def joined(part):
    half = part.shape[0] // 2
    return jnp.concatenate([part[:half], part[half:]], axis=-1)


def kept_sums(arrived, keep, half=None):
    if half is not None:
        arrived, keep = arrived[:, half], keep[:, half]
    return add(keep[1], arrived[1]), add(keep[0], arrived[0])


def pack_shared(kv_grad, gain_rows, head_rows):
    count = lax.axis_size("dp")
    width, columns = kv_grad.shape

    def shares(rows):
        parts = jnp.swapaxes(rows.reshape(rows.shape[0], count, -1), 0, 1)
        return jnp.pad(parts, ((0, 0), (0, 0), (0, columns - parts.shape[2])))

    small = jnp.concatenate([shares(gain_rows), shares(head_rows)], axis=1).astype(BF16)
    small = jnp.pad(small, ((0, 0), (0, 10), (0, 0)))
    return jnp.concatenate([kv_grad.reshape(count, -1, columns), small], axis=1).reshape(
        1, -1, columns
    )


def core_half(packed):
    count = lax.axis_size("dp")
    columns = packed.shape[-1]
    halves = packed.reshape(count, 2, -1, columns)
    mine = lax.axis_index("tensor") % 2

    def half(at):
        return lax.dynamic_index_in_dim(halves, at, 1, keepdims=False).reshape(1, -1, columns)

    return add(half(mine), beside_tensor(half(1 - mine)))


def body(
    section_input, cotangent, segments, query_weight, key_weight, value_weight, output_weight,
    gate_weight, up_weight, down_weight, norm_gains, head_gains,
):
    section = lax.axis_index("section")
    place = lax.axis_index("tensor")
    first = section == 0
    rows = section_input.shape[1]
    per_head = head_gains.shape[1]
    local = norm_gains.shape[1]

    gain_rows = norm_gains[0].T
    head_rows = jnp.pad(head_gains[0].T, ((0, 0), (0, local - per_head)))
    small = jnp.pad(jnp.concatenate([gain_rows, head_rows]), ((0, 10), (0, 2 * HD - local)))
    shared = jnp.concatenate(
        [
            jnp.concatenate([query_weight[0], output_weight[0]], axis=1),
            lax.dynamic_slice_in_dim(
                jnp.concatenate([key_weight[0], value_weight[0]], axis=1),
                place % 2 * (local // 2), local // 2, 0,
            ),
            small,
        ]
    )
    cuts = ((0, local), (local, local // 2), (local + local // 2, 16))
    units = gate_weight.shape[2] // 2
    feeds = [
        jnp.stack([w[0, :, half * units : (half + 1) * units]
                   for w in (gate_weight, up_weight, down_weight)])
        for half in range(2)
    ]
    other = across_section(shared)
    own_segments = lax.dynamic_index_in_dim(segments, section, 0, keepdims=False)
    length = own_segments.shape[0]
    places = jnp.arange(length, dtype=jnp.int32)
    before = jnp.concatenate([own_segments[:1] - 1, own_segments[:-1]])
    starts = lax.cummax(jnp.where(own_segments != before, places, 0), axis=0)
    inverse = jnp.exp(-jnp.log(10000.0) * jnp.arange(HALF, dtype=F32) / HALF)

    def tables(block):
        positions = lax.dynamic_slice_in_dim(places - starts, block * rows, rows, 0)
        angle = positions.astype(F32)[:, None] * inverse[None, :]
        return jnp.cos(angle), jnp.sin(angle)

    tables_before = tables(jnp.maximum(place - 1, 0))
    here = lax.dynamic_slice_in_dim(own_segments, place * rows, rows, 0)
    padded = jnp.concatenate([jnp.full((rows,), -1, jnp.int32), own_segments])
    prior = lax.dynamic_slice_in_dim(padded, place * rows, rows, 0)
    common = (*tables(place), here[:, None], here[None, :], prior[None, :])

    x0 = lax.dynamic_index_in_dim(section_input, section, 0, keepdims=False)
    x_before = halo_on(x0)
    grad = lax.dynamic_index_in_dim(cotangent, section, 0, keepdims=False)
    count = lax.axis_size("dp")

    def small_of(gathered):
        rows = gathered[2].reshape(count, 16, 2 * HD).astype(F32)
        gains = jnp.swapaxes(rows[:, :4, :local], 0, 1).reshape(4, count * local)
        heads = jnp.swapaxes(rows[:, 4:6, :per_head], 0, 1).reshape(2, HD)
        mine, other = gathered[1], beside_tensor(gathered[1])
        halves = [jnp.where(place % 2 == at, mine, other) for at in range(2)]
        halves = [half.reshape(count, 1, -1, 2 * HD) for half in halves]
        return jnp.concatenate(halves, axis=1).reshape(-1, 2 * HD), gains, heads

    choices = [(section == layer).astype(jnp.int32).reshape(1) for layer in range(2)]
    shared_l = [jnp.where(first, shared, other), jnp.where(first, other, shared)]

    whole_cut = ((0, local),)
    gathered0 = rows_over_dp(shared_l[0], cuts)
    feed_in, qo_mine, kvw0, rows0, x0, x_before = after((feeds[0], *gathered0, x0, x_before))
    qo_across = across_tensor(qo_mine)
    feed_a = rows_over_dp(feed_in, whole_cut)[0]
    small0 = small_of((qo_mine, kvw0, rows0))
    other_a, mine_a = across_section(feed_a), across_tensor(feed_a)
    feed_in, qo_across, small0 = after((feeds[1], qo_across, small0), feed_a)
    keys0 = forward_keys(x0, small0, common)
    prev0 = forward_keys(x_before, small0, tables_before)[2]
    feed_b = rows_over_dp(feed_in, whole_cut)[0]
    other_a, mine_a, feed_b, qo_mine, qo_across, keys0, prev0 = after(
        (other_a, mine_a, feed_b, qo_mine, qo_across, keys0, prev0)
    )
    qo0 = [beside_tensor(qo_mine), beside_tensor(qo_across), qo_mine, qo_across]
    other_b, mine_b = across_section(feed_b), across_tensor(feed_b)
    keys0 = (*keys0, prev0)
    beside_a = [beside_tensor(part) for part in (feed_a, mine_a, other_a)]
    attended0 = forward_attend(x0, keys0, small0, choices[0], qo0, common)
    other_a, other_b, mine_b, beside_a, attended0, shared1 = after(
        (other_a, other_b, mine_b, beside_a, attended0, shared_l[1])
    )
    far_a, far_b = across_tensor(other_a), across_section(mine_b)
    gathered1 = rows_over_dp(shared1, cuts)
    far_a, far_b, mine_b, other_b, gathered1 = after((far_a, far_b, mine_b, other_b, gathered1))
    beside_b = [beside_tensor(part) for part in (feed_b, mine_b, other_b)]
    beside_far = [beside_tensor(far_a), beside_tensor(far_b)]
    small1 = small_of(gathered1)
    qo_mine1, beside_b, beside_far = after((gathered1[0], beside_b, beside_far))
    ff = [beside_a[0], beside_b[0], beside_a[1], beside_b[1], feed_a, feed_b, mine_a, mine_b,
          beside_a[2], beside_b[2], *beside_far, other_a, other_b, far_a, far_b]
    qo_across1 = across_tensor(qo_mine1)
    fed0 = forward_feed(attended0, small0, choices[0], ff)
    out0, x1 = fed0[3:]
    keys1 = forward_keys(x1, small1, common)
    keys1, qo_across1 = after((keys1, qo_across1))
    prev1 = halo_on(keys1[2])
    qo1 = [beside_tensor(qo_mine1), beside_tensor(qo_across1), qo_mine1, qo_across1]
    x1, prev1, qo1 = after((x1, prev1, qo1))
    keys1 = (*keys1, prev1)
    attended1 = forward_attend(x1, keys1, small1, choices[1], qo1, common)
    fed1 = forward_feed(attended1, small1, choices[1], ff)
    out1, out1_low = fed1[3:]

    def packed(kv, gain, key, fed, at):
        return pack_shared(
            kv, jnp.concatenate([gain, fed[4][:3]]), jnp.concatenate([at[5], key])
        )

    out_got = across_section(jnp.where(first, out1_low, x1))
    ff1 = backward_feed(grad, *attended1[4:], fed1, small1, choices[1], ff)
    ff1, out_got = after((ff1, out_got))
    ff1_core = beside_tensor(ff1[0])
    at1 = backward_attend(ff1[3], keys1, attended1, small1, choices[1], qo1, common)
    at1, ff1_core = after((at1, ff1_core))
    next1 = halo_back(at1[3])
    qo1_core = beside_tensor(at1[0])
    sums1 = [kept_sums(ff1_core, ff1[1], half) for half in range(2)]
    next1, sums1 = after((next1, sums1))
    across1a = across_tensor(sums1[0][0])
    kv1, grad1, grad1_low, gain1, key1 = backward_keys(
        x1, at1[2], next1, keys1, small1, at1[4], ff1[2], common
    )
    ff0 = backward_feed(grad1_low, *attended0[4:], fed0, small0, choices[0], ff)
    across1a, ff0, sums1, qo1_core = after((across1a, ff0, sums1, qo1_core))
    ff0_core = beside_tensor(ff0[0])
    across1b = across_tensor(sums1[1][0])
    at0 = backward_attend(ff0[3], keys0, attended0, small0, choices[0], qo0, common)
    pair1 = kept_sums(qo1_core, at1[1])
    at0, ff0_core, across1b, pair1, kv1 = after((at0, ff0_core, across1b, pair1, kv1))
    pair1_across = across_tensor(pair1[0])
    rest1 = core_half(packed(kv1, gain1, key1, ff1, at1))[0]
    next0 = halo_back(at0[3])
    qo0_core = beside_tensor(at0[0])
    sums0 = [kept_sums(ff0_core, ff0[1], half) for half in range(2)]
    across0a = across_tensor(sums0[0][0])
    kv0, grad0, grad0_low, gain0, key0 = backward_keys(
        x0, at0[2], next0, keys0, small0, at0[4], ff0[2], common
    )
    grad_got = across_section(jnp.where(first, grad1_low, grad0_low))
    pair0 = kept_sums(qo0_core, at0[1])
    rest0 = core_half(packed(kv0, gain0, key0, ff0, at0))[0]
    full1 = [add(sums1[0][1], across1a), add(sums1[1][1], across1b)]
    pair1 = add(pair1[1], pair1_across)
    across0a, rest0, rest1, pair0, pair1, sums0, full1, grad_got = after(
        (across0a, rest0, rest1, pair0, pair1, sums0, full1, grad_got)
    )

    def swapped(zero, one):
        return add(jnp.where(first, zero, one), across_section(jnp.where(first, one, zero)))

    across0b = across_tensor(sums0[1][0])
    feed_a = swapped(add(sums0[0][1], across0a), full1[0])
    low0 = jnp.concatenate([pair0[0], rest0, rest1])
    across0b, feed_a, low0, sums0 = after((across0b, feed_a, low0, sums0))
    low0_across = across_tensor(low0)
    feed_b = swapped(add(sums0[1][1], across0b), full1[1])
    feed_a = summed_over_dp([feed_a])[0]
    low0_across, feed_a, feed_b = after((low0_across, feed_a, feed_b))
    size = low0.shape[0] - rest1.shape[0]
    low = swapped(
        add(jnp.concatenate([pair0[1], rest0]), low0_across[:size]),
        jnp.concatenate([pair1, add(rest1, low0_across[size:])]),
    )
    feed_b = summed_over_dp([feed_b])[0]
    feed_b, low = after((feed_b, low))
    pair_rows = pair0[0].shape[0]
    pair, rest = summed_over_dp(
        [side_by_side(low[None, :pair_rows]), side_by_side(low[None, pair_rows:])]
    )
    pair, rest = joined(pair).astype(F32), joined(rest)[0]
    beside = beside_tensor(rest)
    even = place % 2 == 0
    rest = jnp.concatenate(
        [jnp.where(even, rest, beside), jnp.where(even, beside, rest)]
    ).astype(F32)
    feed = jnp.stack([feed_a, feed_b]).astype(F32)

    def placed(zero, one, got):
        got = got.astype(F32)
        return jnp.stack([jnp.where(first, zero, got), jnp.where(first, got, one)])[None]

    return (
        placed(out0, out1, out_got),
        placed(grad0, grad1, grad_got),
        pair[:, :, :HD],
        rest[None, :local, :HD],
        rest[None, :local, HD:],
        pair[:, :, HD:],
        *[jnp.concatenate([feed[0, n], feed[1, n]], axis=1)[None] for n in range(3)],
        rest[local : local + 4, :local].T[None],
        rest[local + 4 : local + 6, :per_head].T[None],
    )


def solution(mesh):
    return jax.shard_map(
        body,
        mesh=mesh,
        in_specs=(
            P(None, ("dp", "tensor"), None),
            P(None, ("dp", "tensor"), None),
            P(None, "dp"),
            P("section", "dp", "tensor"),
            P("section", "dp", None),
            P("section", "dp", None),
            P("section", "dp", "tensor"),
            P("section", "dp", "tensor"),
            P("section", "dp", "tensor"),
            P("section", "dp", "tensor"),
            P("section", "dp", None),
            P("section", "dp", None),
        ),
        out_specs=(
            P("section", None, ("dp", "tensor"), None),
            P("section", None, ("dp", "tensor"), None),
            P("section", "dp", "tensor"),
            P("section", "dp", None),
            P("section", "dp", None),
            P("section", "dp", "tensor"),
            P("section", "dp", "tensor"),
            P("section", "dp", "tensor"),
            P("section", "dp", "tensor"),
            P("section", "dp", None),
            P("section", "dp", None),
        ),
        check_vma=False,
    )
```

```python
import functools

import jax
import jax.numpy as jnp
from jax import lax
from jax.experimental import pallas as pl
from jax.experimental.pallas import tpu as pltpu
from jax.sharding import PartitionSpec as P

HD = 256
HALF = HD // 2
WIN = 512
BLK = 256
EPS = 1e-06
F32 = jnp.float32
BF16 = jnp.bfloat16
LIMIT = 50 * 1024 * 1024


def nn(a, b):
    return lax.dot_general(a, b, (((1,), (0,)), ((), ())), preferred_element_type=F32)


def nt(a, b):
    return lax.dot_general(a, b, (((1,), (1,)), ((), ())), preferred_element_type=F32)


def tn(a, b):
    return lax.dot_general(a, b, (((0,), (0,)), ((), ())), preferred_element_type=F32)


def rms(values, gain):
    return values * lax.rsqrt(jnp.mean(values * values, axis=-1, keepdims=True) + EPS) * gain


def rms_back(grad, values, gain):
    scale = lax.rsqrt(jnp.mean(values * values, axis=-1, keepdims=True) + EPS)
    unit = values * scale
    scaled = grad * gain
    inner = jnp.mean(scaled * unit, axis=-1, keepdims=True)
    return scale * (scaled - unit * inner), jnp.sum(grad * unit, axis=0, keepdims=True)


def rot(values, cosine, sine):
    a, b = values[:, :HALF], values[:, HALF:]
    return jnp.concatenate([a * cosine - b * sine, b * cosine + a * sine], axis=-1)


def rot_back(grad, cosine, sine):
    a, b = grad[:, :HALF], grad[:, HALF:]
    return jnp.concatenate([a * cosine + b * sine, b * cosine - a * sine], axis=-1)


GELU_A = 0.7978845608028654
GELU_B = 0.044715


def triangle():
    row = lax.broadcasted_iota(jnp.int32, (BLK, BLK), 0)
    column = lax.broadcasted_iota(jnp.int32, (BLK, BLK), 1)
    return column <= row


def tiles(block):
    rows = slice(block * BLK, (block + 1) * BLK)
    other = slice((1 - block) * BLK, (2 - block) * BLK)
    return rows, other, block == 1


def masks(block, lower, seg_col, seg_own, seg_prev):
    rows, other, own = tiles(block)
    mine = seg_col[rows, :]
    diagonal = mine == jnp.where(lower, seg_own[:, rows], seg_prev[:, rows])
    rest = mine == (seg_own if own else seg_prev)[:, other]
    return diagonal, rest


def stream(step, choice, own, other, held, arrived):
    def spot(index, part):
        if len(held.shape) == 4:
            return held.at[index, part]
        columns = held.shape[4] // 2
        return held.at[index, 0, :, :, pl.ds(part * columns, columns)]

    def fetch(index):
        for wanted, slots in ((1, own), (0, other)):

            @pl.when(choice[0] == wanted)
            def _(slots=slots):
                for part, ref in enumerate(slots[index]):
                    pltpu.make_async_copy(
                        ref, spot(index % 2, part), arrived.at[index % 2, part]
                    ).start()

    @pl.when(step == 0)
    def _():
        fetch(0)

    for index in range(1, len(own)):

        @pl.when(step == index - 1)
        def _(index=index):
            fetch(index)

    now = lax.rem(step, 2)
    for part, ref in enumerate(own[0]):
        pltpu.make_async_copy(ref, spot(now, part), arrived.at[now, part]).wait()
    return now


def assemble_kernel(cuts, place, *refs):
    count = (len(refs) - len(cuts) - 1)
    pieces, outs, done = refs[:count], refs[count:-1], refs[-1]
    copies = []
    for shift, piece in enumerate(pieces):
        owner = lax.rem(place[0] + count - shift, count)
        for cut, (start, rows) in enumerate(cuts):
            at = pl.ds(pl.multiple_of(owner * rows, rows), rows)
            lead = (slice(None),) * (len(piece.shape) - 2)
            copies.append(
                pltpu.make_async_copy(
                    piece.at[lead + (pl.ds(start, rows),)],
                    outs[cut].at[lead + (at,)],
                    done.at[shift, cut],
                )
            )
    for copy in copies:
        copy.start()
    for copy in copies:
        copy.wait()


def prep_kernel(x, gains, heads, kvw, cosine, sine, normed, kraw, kv):
    rows = rms(x[...].astype(F32), gains[0:1, :]).astype(BF16)
    normed[...] = rows
    raw = nn(rows, kvw[:, :HD])
    kraw[...] = raw
    kv[:, :HD] = rot(rms(raw, heads[1:2, :]), cosine[...], sine[...]).astype(BF16)
    kv[:, HD:] = nn(rows, kvw[:, HD : 2 * HD]).astype(BF16)


def flat(tile):
    return tile.reshape(-1, tile.shape[-1])


def tall(tile):
    return tile.reshape(2, -1, tile.shape[-1])


def attend_kernel(
    choice, x, normed, gains, heads, own, prev, cosine, sine, seg_col, seg_own, seg_prev,
    qo_a, qo_b, qo_c, qo_d, qraw, q, mixed, lse, branch, middle, normed_two, held, arrived,
):
    step = pl.program_id(0)
    slots = [[qo_a, qo_b], [qo_c, qo_d]]
    now = stream(step, choice, slots, slots, held, arrived)
    for head in range(2):
        raw = nn(normed[...], held[now, head, :, :HD])
        qraw[head] = raw
        turned = rot(rms(raw, heads[0:1, :]), cosine[...], sine[...]).astype(BF16)
        q[head] = turned * jnp.asarray(0.0625, BF16)
    lower = triangle()
    for block in range(2):
        rows, other, is_own = tiles(block)
        diagonal, rest = masks(block, lower, seg_col[...], seg_own[...], seg_prev[...])
        query = flat(q[:, rows, :])
        far = own if is_own else prev
        near_scores = jnp.where(
            lower, tall(nt(query, own[rows, :HD])), tall(nt(query, prev[rows, :HD]))
        )
        near_scores = jnp.where(diagonal, near_scores, -1e30)
        far_scores = jnp.where(rest, tall(nt(query, far[other, :HD])), -1e30)
        largest = jnp.maximum(
            jnp.max(near_scores, axis=-1, keepdims=True),
            jnp.max(far_scores, axis=-1, keepdims=True),
        )
        near = jnp.exp(near_scores - largest)
        rest_p = jnp.exp(far_scores - largest)
        total = jnp.sum(near, axis=-1, keepdims=True) + jnp.sum(rest_p, axis=-1, keepdims=True)
        inverse = 1.0 / total
        near = near * inverse
        rest_p = (rest_p * inverse).astype(BF16)
        near_own = jnp.where(lower, near, 0.0).astype(BF16)
        near_prev = jnp.where(lower, 0.0, near).astype(BF16)
        mixed[:, rows, :] = tall(
            nn(flat(near_own), own[rows, HD:])
            + nn(flat(near_prev), prev[rows, HD:])
            + nn(flat(rest_p), far[other, HD:])
        ).astype(BF16)
        lse[:, rows, :] = largest + jnp.log(total)
    part = nt(mixed[0], held[now, 0, :, HD:]) + nt(mixed[1], held[now, 1, :, HD:])

    @pl.when(step == 0)
    def _():
        branch[...] = part

    @pl.when(step > 0)
    def _():
        branch[...] += part

    @pl.when(step == pl.num_programs(0) - 1)
    def _():
        mid = x[...].astype(F32) + rms(branch[...], gains[1:2, :])
        middle[...] = mid
        normed_two[...] = rms(mid, gains[2:3, :]).astype(BF16)


def slots_of(refs):
    halves = [[refs[at], refs[at + 1]] for at in range(0, len(refs), 2)]
    return halves[: len(halves) // 2], halves[len(halves) // 2 :]


def feed_kernel(choice, normed_two, middle, gains, *refs):
    own, other = slots_of(refs[:16])
    gate_out, up_out, branch_two, out, out_low, held, arrived = refs[16:]
    step = pl.program_id(0)
    now = stream(step, choice, own, other, held, arrived)
    rows = normed_two[...]
    gate = nn(rows, held[now, 0, 0])
    upward = nn(rows, held[now, 0, 1])
    gate_out[0] = gate.astype(BF16)
    up_out[0] = upward.astype(BF16)
    wave = jnp.tanh(GELU_A * gate * (1.0 + GELU_B * gate * gate))
    hidden = (0.5 * gate * (1.0 + wave) * upward).astype(BF16)
    part = nt(hidden, held[now, 0, 2])

    @pl.when(step == 0)
    def _():
        branch_two[...] = part

    @pl.when(step > 0)
    def _():
        branch_two[...] += part

    @pl.when(step == pl.num_programs(0) - 1)
    def _():
        total = middle[...] + rms(branch_two[...], gains[3:4, :])
        out[...] = total
        out_low[...] = total.astype(BF16)


def feed_back_kernel(
    choice, grad, branch_two, middle, branch, normed_two, gains, gate_in, up_in, *refs
):
    own, other = slots_of(refs[:16])
    send, keep, grad_middle, grad_branch, gain_grads = refs[16:21]
    incoming, incoming_t, rows_t, total, held, arrived = refs[21:]
    step = pl.program_id(0)
    now = stream(step, choice, own, other, held, arrived)

    @pl.when(step == 0)
    def _():
        values, gain = rms_back(grad[...].astype(F32), branch_two[...], gains[3:4, :])
        incoming[...] = values.astype(BF16)
        incoming_t[...] = values.T.astype(BF16)
        rows_t[...] = normed_two[...].T
        gain_grads[2:3, :] = gain
        gain_grads[3:4, :] = jnp.zeros_like(gain)

    gate = gate_in[0].astype(F32)
    upward = up_in[0].astype(F32)
    square = gate * gate
    wave = jnp.tanh(GELU_A * gate * (1.0 + GELU_B * square))
    bell = 0.5 * (1.0 + wave)
    active = gate * bell
    slope = bell + gate * (1.0 - wave * wave) * (0.5 * GELU_A * (1.0 + 3.0 * GELU_B * square))
    grad_hidden = nn(incoming[...], held[now, 0, 2])
    grad_up = (grad_hidden * active).astype(BF16)
    grad_gate = (grad_hidden * upward * slope).astype(BF16)
    hidden = (active * upward).astype(BF16)
    columns = hidden.shape[1] // 2

    def store(place):
        for number, (left, right) in enumerate(
            ((rows_t, grad_gate), (rows_t, grad_up), (incoming_t, hidden))
        ):
            value = nn(left[...], right).astype(BF16)
            place[0, 0, number] = value[:, :columns]
            place[0, 1, number] = value[:, columns:]

    @pl.when(step < 2)
    def _():
        store(send)

    @pl.when(step >= 2)
    def _():
        store(keep)

    part = nt(grad_gate, held[now, 0, 0]) + nt(grad_up, held[now, 0, 1])

    @pl.when(step == 0)
    def _():
        total[...] = part

    @pl.when(step > 0)
    def _():
        total[...] += part

    @pl.when(step == pl.num_programs(0) - 1)
    def _():
        from_norm, gain = rms_back(total[...], middle[...], gains[2:3, :])
        gain_grads[1:2, :] = gain
        mid = grad[...].astype(F32) + from_norm
        grad_middle[...] = mid
        values, gain = rms_back(mid, branch[...], gains[1:2, :])
        gain_grads[0:1, :] = gain
        grad_branch[...] = values.astype(BF16)


def attend_back_kernel(
    choice, grad_branch, normed, heads, q, qraw, mixed, lse, own, prev, cosine, sine,
    seg_col, seg_own, seg_prev, qo_a, qo_b, qo_c, qo_d,
    send, keep, kv_own, kv_prev, grad_normed, head_grad, grad_t, rows_t, prev_sum, grad_q,
    held, arrived, mixed_g, raw_g,
):
    step = pl.program_id(0)
    slots = [[qo_a, qo_b], [qo_c, qo_d]]
    now = stream(step, choice, slots, slots, held, arrived)

    @pl.when(step == 0)
    def _():
        grad_t[...] = grad_branch[...].T
        rows_t[...] = normed[...].T
        kv_own[...] = jnp.zeros_like(kv_own)
        prev_sum[...] = jnp.zeros_like(prev_sum)
        grad_normed[...] = jnp.zeros_like(grad_normed)
        head_grad[...] = jnp.zeros_like(head_grad)

    for head in range(2):
        mixed_g[head] = nn(grad_branch[...], held[now, head, :, HD:]).astype(BF16)
    lower = triangle()
    for block in range(2):
        rows, other, is_own = tiles(block)
        diagonal, rest = masks(block, lower, seg_col[...], seg_own[...], seg_prev[...])
        query = flat(q[:, rows, :])
        incoming = flat(mixed_g[:, rows, :])
        far = own if is_own else prev
        far_sum = kv_own if is_own else prev_sum
        log_total = lse[:, rows, :]
        near_scores = jnp.where(
            lower, tall(nt(query, own[rows, :HD])), tall(nt(query, prev[rows, :HD]))
        )
        near = jnp.exp(jnp.where(diagonal, near_scores, -1e30) - log_total)
        rest_p = jnp.exp(jnp.where(rest, tall(nt(query, far[other, :HD])), -1e30) - log_total)
        near_grad = jnp.where(
            lower, tall(nt(incoming, own[rows, HD:])), tall(nt(incoming, prev[rows, HD:]))
        )
        rest_grad = tall(nt(incoming, far[other, HD:]))
        inner = jnp.sum(near * near_grad, axis=-1, keepdims=True) + jnp.sum(
            rest_p * rest_grad, axis=-1, keepdims=True
        )
        near_score = near * (near_grad - inner)
        rest_score = flat(rest_p * (rest_grad - inner)).astype(BF16)
        score_own = flat(jnp.where(lower, near_score, 0.0)).astype(BF16)
        score_prev = flat(jnp.where(lower, 0.0, near_score)).astype(BF16)
        near_own = flat(jnp.where(lower, near, 0.0)).astype(BF16)
        near_prev = flat(jnp.where(lower, 0.0, near)).astype(BF16)
        rest_p = flat(rest_p).astype(BF16)
        grad_q[:, rows, :] = tall(
            0.0625
            * (
                nn(score_own, own[rows, :HD])
                + nn(score_prev, prev[rows, :HD])
                + nn(rest_score, far[other, :HD])
            )
        )
        kv_own[rows, :HD] += tn(score_own, query)
        prev_sum[rows, :HD] += tn(score_prev, query)
        far_sum[other, :HD] += tn(rest_score, query)
        kv_own[rows, HD:] += tn(near_own, incoming)
        prev_sum[rows, HD:] += tn(near_prev, incoming)
        far_sum[other, HD:] += tn(rest_p, incoming)
    for head in range(2):
        values, gain = rms_back(
            rot_back(grad_q[head], cosine[...], sine[...]), qraw[head], heads[0:1, :]
        )
        head_grad[0:1, :] += gain
        raw_g[head] = values.astype(BF16)
        grad_normed[...] += nt(raw_g[head], held[now, head, :, :HD])

    def store(place):
        for head in range(2):
            place[head, :, :HD] = nn(rows_t[...], raw_g[head]).astype(BF16)
            place[head, :, HD:] = nn(grad_t[...], mixed[head]).astype(BF16)

    @pl.when(step == 0)
    def _():
        store(send)

    @pl.when(step == 1)
    def _():
        store(keep)

    @pl.when(step == pl.num_programs(0) - 1)
    def _():
        kv_prev[...] = prev_sum[...].astype(BF16)


def finish_kernel(
    kv_own, kv_next, kraw, normed, kvw, heads, gains, x, grad_normed, grad_middle, cosine, sine,
    kv_grad, grad_x, grad_low, gain_grad, head_grad,
):
    summed = kv_own[...] + kv_next[...].astype(F32)
    values, gain = rms_back(
        rot_back(summed[:, :HD], cosine[...], sine[...]), kraw[...], heads[1:2, :]
    )
    head_grad[...] = gain
    grad_key = values.astype(BF16)
    grad_value = summed[:, HD:].astype(BF16)
    rows = normed[...]
    kv_grad[:, :HD] = tn(rows, grad_key).astype(BF16)
    kv_grad[:, HD:] = tn(rows, grad_value).astype(BF16)
    from_all = grad_normed[...] + nt(grad_key, kvw[:, :HD]) + nt(grad_value, kvw[:, HD : 2 * HD])
    from_norm, gain = rms_back(from_all, x[...].astype(F32), gains[0:1, :])
    gain_grad[...] = gain
    total = grad_middle[...] + from_norm
    grad_x[...] = total
    grad_low[...] = total.astype(BF16)


def whole(shape):
    zeros = (0,) * len(shape)
    return pl.BlockSpec(shape, lambda *at: zeros)


def anywhere(shape):
    return pl.BlockSpec(memory_space=pl.ANY)


def fetched(shape):
    return pl.BlockSpec(memory_space=pltpu.HBM)


def resident(shape):
    return pl.BlockSpec(memory_space=pltpu.VMEM)


def scalars(shape):
    return pl.BlockSpec(memory_space=pltpu.SMEM)


def slot(shape):
    zeros = (0,) * (len(shape) - 1)
    return pl.BlockSpec((1,) + tuple(shape[1:]), lambda at: (at,) + zeros)


def pair(shape):
    zeros = (0,) * (len(shape) - 1)
    return pl.BlockSpec((2,) + tuple(shape[1:]), lambda at: (at,) + zeros)


def early(shape):
    zeros = (0,) * (len(shape) - 1)
    return pl.BlockSpec((1,) + tuple(shape[1:]), lambda at: (jnp.minimum(at, 1),) + zeros)


def late(shape):
    zeros = (0,) * (len(shape) - 1)
    return pl.BlockSpec((1,) + tuple(shape[1:]), lambda at: (jnp.maximum(at - 2, 0),) + zeros)


def run(kernel, grid, ins, outs, scratch=(), micros=2):
    arrays = [a for a, _ in ins]
    return pl.pallas_call(
        kernel,
        grid=grid,
        in_specs=[spec(a.shape) for a, spec in ins],
        out_specs=[spec(shape) for shape, _, spec in outs],
        out_shape=[jax.ShapeDtypeStruct(shape, kind) for shape, kind, _ in outs],
        scratch_shapes=list(scratch),
        compiler_params=pltpu.CompilerParams(vmem_limit_bytes=LIMIT),
        cost_estimate=pl.CostEstimate(
            flops=micros * 1153000000, bytes_accessed=1, transcendentals=0
        ),
    )(*arrays)


def qo_scratch(width):
    return [pltpu.VMEM((2, 2, width, 2 * HD), BF16), pltpu.SemaphoreType.DMA((2, 2))]


def ff_scratch(width, units):
    return [pltpu.VMEM((2, 1, 3, width, 2 * units), BF16), pltpu.SemaphoreType.DMA((2, 2))]


def forward_keys(x, small, common):
    cosine, sine = common[:2]
    kvw, gains, heads = small
    rows, width = x.shape
    normed, kraw, kv = run(
        prep_kernel, (1,),
        [(x, whole), (gains, whole), (heads, whole), (kvw, whole), (cosine, whole), (sine, whole)],
        [((rows, width), BF16, whole), ((rows, HD), F32, whole), ((rows, 2 * HD), BF16, whole)],
        micros=2,
    )
    return normed, kraw, kv


def halo_on(kv):
    return lax.ppermute(kv, "tensor", [(i, i + 1) for i in range(lax.axis_size("tensor") - 1)])


def forward_attend(x, keys, small, choice, qo, common):
    cosine, sine, seg_col, seg_own, seg_prev = common
    kvw, gains, heads = small
    normed, kraw, kv, prev = keys
    rows, width = x.shape
    slots = len(qo)
    return run(
        attend_kernel, (slots // 2,),
        [(choice, scalars), (x, whole), (normed, whole), (gains, whole), (heads, whole),
         (kv, whole), (prev, whole), (cosine, whole), (sine, whole), (seg_col, whole),
         (seg_own, whole), (seg_prev, whole)] + [(part, fetched) for part in qo],
        [((slots, rows, HD), F32, pair), ((slots, rows, HD), BF16, pair),
         ((slots, rows, HD), BF16, pair), ((slots, rows, 1), F32, pair),
         ((rows, width), F32, whole), ((rows, width), F32, whole), ((rows, width), BF16, whole)],
        qo_scratch(width),
        micros=14,
    )


def forward_feed(attended, small, choice, ff):
    gains = small[1]
    middle, normed_two = attended[5:]
    rows, width = middle.shape
    slots, units = len(ff) // 4, ff[0].shape[2]
    return run(
        feed_kernel, (slots,),
        [(choice, scalars), (normed_two, whole), (middle, whole), (gains, whole)]
        + [(part, fetched) for part in ff],
        [((slots, rows, 2 * units), BF16, slot), ((slots, rows, 2 * units), BF16, slot),
         ((rows, width), F32, whole), ((rows, width), F32, whole), ((rows, width), BF16, whole)],
        ff_scratch(width, units),
        micros=12,
    )


def backward_feed(grad, branch, middle, normed_two, fed, small, choice, ff):
    gains = small[1]
    gate, upward, branch_two = fed[:3]
    rows, width = middle.shape
    slots, units = len(ff) // 4, ff[0].shape[2]
    half = slots // 2
    return run(
        feed_back_kernel, (slots,),
        [(choice, scalars), (grad, whole), (branch_two, whole), (middle, whole), (branch, whole),
         (normed_two, whole), (gains, whole), (gate, slot), (upward, slot)]
        + [(part, fetched) for part in ff],
        [((half, 2, 3, width, units), BF16, early), ((half, 2, 3, width, units), BF16, late),
         ((rows, width), F32, whole), ((rows, width), BF16, whole), ((4, width), F32, whole)],
        [pltpu.VMEM((rows, width), BF16), pltpu.VMEM((width, rows), BF16),
         pltpu.VMEM((width, rows), BF16), pltpu.VMEM((rows, width), F32)]
        + ff_scratch(width, units),
        micros=25,
    )


def backward_attend(grad_branch, keys, attended, small, choice, qo, common):
    cosine, sine, seg_col, seg_own, seg_prev = common
    heads = small[2]
    normed, kraw, kv, prev = keys
    qraw, q, mixed, lse = attended[:4]
    rows, width = normed.shape
    slots = len(qo)
    half = slots // 2
    return run(
        attend_back_kernel, (slots // 2,),
        [(choice, scalars), (grad_branch, whole), (normed, whole), (heads, whole), (q, pair),
         (qraw, pair), (mixed, pair), (lse, pair), (kv, whole), (prev, whole), (cosine, whole),
         (sine, whole), (seg_col, whole), (seg_own, whole), (seg_prev, whole)]
        + [(part, fetched) for part in qo],
        [((half, width, 2 * HD), BF16, whole), ((half, width, 2 * HD), BF16, whole),
         ((rows, 2 * HD), F32, whole), ((rows, 2 * HD), BF16, whole), ((rows, width), F32, whole),
         ((1, HD), F32, whole)],
        [pltpu.VMEM((width, rows), BF16), pltpu.VMEM((width, rows), BF16),
         pltpu.VMEM((rows, 2 * HD), F32), pltpu.VMEM((2, rows, HD), F32)] + qo_scratch(width)
        + [pltpu.VMEM((2, rows, HD), BF16)] * 2,
        micros=17,
    )


def backward_keys(x, kv_own, kv_next, keys, small, grad_normed, grad_middle, common):
    cosine, sine = common[:2]
    kvw, gains, heads = small
    normed, kraw = keys[:2]
    rows, width = x.shape
    return run(
        finish_kernel, (1,),
        [(kv_own, whole), (kv_next, whole), (kraw, whole), (normed, whole), (kvw, whole),
         (heads, whole), (gains, whole), (x, whole), (grad_normed, whole), (grad_middle, whole),
         (cosine, whole), (sine, whole)],
        [((width, 2 * HD), BF16, whole), ((rows, width), F32, whole), ((rows, width), BF16, whole),
         ((1, width), F32, whole),
         ((1, HD), F32, whole)],
        micros=5,
    )


def halo_back(kv_prev):
    return lax.ppermute(
        kv_prev, "tensor", [(i + 1, i) for i in range(lax.axis_size("tensor") - 1)]
    )


def tensor_pairs(bit):
    return [(i, i ^ bit) for i in range(lax.axis_size("tensor"))]


def rows_over_dp(part, cuts):
    count = lax.axis_size("dp")
    lead, columns = part.shape[:-2], part.shape[-1]
    if count > 4:
        full = jnp.moveaxis(lax.all_gather(part, "dp", axis=0), 0, -3)
        return [
            full[..., start : start + rows, :].reshape(lead + (count * rows, columns))
            for start, rows in cuts
        ]
    pieces = [part] + [
        lax.ppermute(part, "dp", [(i, (i + shift) % count) for i in range(count)])
        for shift in range(1, count)
    ]
    place = lax.axis_index("dp").astype(jnp.int32).reshape(1)
    return run(
        functools.partial(assemble_kernel, cuts), (),
        [(place, scalars)] + [(piece, resident) for piece in pieces],
        [(lead + (count * rows, columns), part.dtype, anywhere) for _, rows in cuts],
        [pltpu.SemaphoreType.DMA((count, len(cuts)))],
    )


def across_tensor(part):
    return lax.ppermute(part, "tensor", tensor_pairs(2))


def beside_tensor(part):
    return lax.ppermute(part, "tensor", tensor_pairs(1))


def across_section(part):
    return lax.ppermute(part, "section", [(0, 1), (1, 0)])


def after(values, *others):
    return lax.optimization_barrier((values, others))[0]


def add(left, right):
    return (left.astype(F32) + right.astype(F32)).astype(BF16)


def summed_over_dp(parts):
    count = lax.axis_size("dp")
    if count > 4:
        return [
            lax.psum_scatter(part, "dp", scatter_dimension=1, tiled=True) for part in parts
        ]
    me = lax.axis_index("dp")
    shapes = [(part.shape[0], part.shape[1] // count, part.shape[2]) for part in parts]

    def share(owner):
        blocks = [
            lax.dynamic_slice_in_dim(part, owner % count * shape[1], shape[1], 1)
            for part, shape in zip(parts, shapes)
        ]
        return jnp.concatenate([block.reshape(-1, block.shape[2]) for block in blocks])

    total = share(me).astype(F32)
    pieces = [
        lax.ppermute(share(me + shift), "dp", [(i, (i + shift) % count) for i in range(count)])
        for shift in range(1, count)
    ]
    for piece in pieces:
        total += piece.astype(F32)
    total, sums, start = total.astype(BF16), [], 0
    for shape in shapes:
        size = shape[0] * shape[1]
        sums.append(total[start : start + size].reshape(shape))
        start += size
    return sums


def side_by_side(part):
    return jnp.concatenate([part[..., :HD], part[..., HD:]])


def joined(part):
    half = part.shape[0] // 2
    return jnp.concatenate([part[:half], part[half:]], axis=-1)


def kept_sums(arrived, keep, half=None):
    if half is not None:
        arrived, keep = arrived[:, half], keep[:, half]
    return add(keep[1], arrived[1]), add(keep[0], arrived[0])


def pack_shared(kv_grad, gain_rows, head_rows):
    count = lax.axis_size("dp")
    width, columns = kv_grad.shape

    def shares(rows):
        parts = jnp.swapaxes(rows.reshape(rows.shape[0], count, -1), 0, 1)
        return jnp.pad(parts, ((0, 0), (0, 0), (0, columns - parts.shape[2])))

    small = jnp.concatenate([shares(gain_rows), shares(head_rows)], axis=1).astype(BF16)
    small = jnp.pad(small, ((0, 0), (0, 10), (0, 0)))
    return jnp.concatenate([kv_grad.reshape(count, -1, columns), small], axis=1).reshape(
        1, -1, columns
    )


def core_half(packed):
    count = lax.axis_size("dp")
    columns = packed.shape[-1]
    halves = packed.reshape(count, 2, -1, columns)
    mine = lax.axis_index("tensor") % 2

    def half(at):
        return lax.dynamic_index_in_dim(halves, at, 1, keepdims=False).reshape(1, -1, columns)

    return add(half(mine), beside_tensor(half(1 - mine)))


def body(
    section_input, cotangent, segments, query_weight, key_weight, value_weight, output_weight,
    gate_weight, up_weight, down_weight, norm_gains, head_gains,
):
    section = lax.axis_index("section")
    place = lax.axis_index("tensor")
    first = section == 0
    rows = section_input.shape[1]
    per_head = head_gains.shape[1]
    local = norm_gains.shape[1]

    gain_rows = norm_gains[0].T
    head_rows = jnp.pad(head_gains[0].T, ((0, 0), (0, local - per_head)))
    small = jnp.pad(jnp.concatenate([gain_rows, head_rows]), ((0, 10), (0, 2 * HD - local)))
    shared = jnp.concatenate(
        [
            jnp.concatenate([query_weight[0], output_weight[0]], axis=1),
            lax.dynamic_slice_in_dim(
                jnp.concatenate([key_weight[0], value_weight[0]], axis=1),
                place % 2 * (local // 2), local // 2, 0,
            ),
            small,
        ]
    )
    cuts = ((0, local), (local, local // 2), (local + local // 2, 16))
    units = gate_weight.shape[2] // 2
    feeds = [
        jnp.stack([w[0, :, half * units : (half + 1) * units]
                   for w in (gate_weight, up_weight, down_weight)])
        for half in range(2)
    ]
    other = across_section(shared)
    own_segments = lax.dynamic_index_in_dim(segments, section, 0, keepdims=False)
    length = own_segments.shape[0]
    places = jnp.arange(length, dtype=jnp.int32)
    before = jnp.concatenate([own_segments[:1] - 1, own_segments[:-1]])
    starts = lax.cummax(jnp.where(own_segments != before, places, 0), axis=0)
    inverse = jnp.exp(-jnp.log(10000.0) * jnp.arange(HALF, dtype=F32) / HALF)

    def tables(block):
        positions = lax.dynamic_slice_in_dim(places - starts, block * rows, rows, 0)
        angle = positions.astype(F32)[:, None] * inverse[None, :]
        return jnp.cos(angle), jnp.sin(angle)

    tables_before = tables(jnp.maximum(place - 1, 0))
    here = lax.dynamic_slice_in_dim(own_segments, place * rows, rows, 0)
    padded = jnp.concatenate([jnp.full((rows,), -1, jnp.int32), own_segments])
    prior = lax.dynamic_slice_in_dim(padded, place * rows, rows, 0)
    common = (*tables(place), here[:, None], here[None, :], prior[None, :])

    x0 = lax.dynamic_index_in_dim(section_input, section, 0, keepdims=False)
    x_before = halo_on(x0)
    grad = lax.dynamic_index_in_dim(cotangent, section, 0, keepdims=False)
    count = lax.axis_size("dp")

    def small_of(gathered):
        rows = gathered[2].reshape(count, 16, 2 * HD).astype(F32)
        gains = jnp.swapaxes(rows[:, :4, :local], 0, 1).reshape(4, count * local)
        heads = jnp.swapaxes(rows[:, 4:6, :per_head], 0, 1).reshape(2, HD)
        mine, other = gathered[1], beside_tensor(gathered[1])
        halves = [jnp.where(place % 2 == at, mine, other) for at in range(2)]
        halves = [half.reshape(count, 1, -1, 2 * HD) for half in halves]
        return jnp.concatenate(halves, axis=1).reshape(-1, 2 * HD), gains, heads

    choices = [(section == layer).astype(jnp.int32).reshape(1) for layer in range(2)]
    shared_l = [jnp.where(first, shared, other), jnp.where(first, other, shared)]

    whole_cut = ((0, local),)
    gathered0 = rows_over_dp(shared_l[0], cuts)
    feed_in, qo_mine, kvw0, rows0, x0, x_before = after((feeds[0], *gathered0, x0, x_before))
    qo_across = across_tensor(qo_mine)
    feed_a = rows_over_dp(feed_in, whole_cut)[0]
    small0 = small_of((qo_mine, kvw0, rows0))
    other_a, mine_a = across_section(feed_a), across_tensor(feed_a)
    feed_in, qo_across, small0 = after((feeds[1], qo_across, small0), feed_a)
    keys0 = forward_keys(x0, small0, common)
    prev0 = forward_keys(x_before, small0, tables_before)[2]
    feed_b = rows_over_dp(feed_in, whole_cut)[0]
    other_a, mine_a, feed_b, qo_mine, qo_across, keys0, prev0 = after(
        (other_a, mine_a, feed_b, qo_mine, qo_across, keys0, prev0)
    )
    qo0 = [beside_tensor(qo_mine), beside_tensor(qo_across), qo_mine, qo_across]
    other_b, mine_b = across_section(feed_b), across_tensor(feed_b)
    keys0 = (*keys0, prev0)
    beside_a = [beside_tensor(part) for part in (feed_a, mine_a, other_a)]
    attended0 = forward_attend(x0, keys0, small0, choices[0], qo0, common)
    other_a, other_b, mine_b, beside_a, attended0, shared1 = after(
        (other_a, other_b, mine_b, beside_a, attended0, shared_l[1])
    )
    far_a, far_b = across_tensor(other_a), across_section(mine_b)
    gathered1 = rows_over_dp(shared1, cuts)
    far_a, far_b, mine_b, other_b, gathered1 = after((far_a, far_b, mine_b, other_b, gathered1))
    beside_b = [beside_tensor(part) for part in (feed_b, mine_b, other_b)]
    beside_far = [beside_tensor(far_a), beside_tensor(far_b)]
    small1 = small_of(gathered1)
    qo_mine1, beside_b, beside_far = after((gathered1[0], beside_b, beside_far))
    ff = [beside_a[0], beside_b[0], beside_a[1], beside_b[1], feed_a, feed_b, mine_a, mine_b,
          beside_a[2], beside_b[2], *beside_far, other_a, other_b, far_a, far_b]
    qo_across1 = across_tensor(qo_mine1)
    fed0 = forward_feed(attended0, small0, choices[0], ff)
    out0, x1 = fed0[3:]
    keys1 = forward_keys(x1, small1, common)
    keys1, qo_across1 = after((keys1, qo_across1))
    prev1 = halo_on(keys1[2])
    qo1 = [beside_tensor(qo_mine1), beside_tensor(qo_across1), qo_mine1, qo_across1]
    x1, prev1, qo1 = after((x1, prev1, qo1))
    keys1 = (*keys1, prev1)
    attended1 = forward_attend(x1, keys1, small1, choices[1], qo1, common)
    fed1 = forward_feed(attended1, small1, choices[1], ff)
    out1, out1_low = fed1[3:]

    def packed(kv, gain, key, fed, at):
        return pack_shared(
            kv, jnp.concatenate([gain, fed[4][:3]]), jnp.concatenate([at[5], key])
        )

    out_got = across_section(jnp.where(first, out1_low, x1))
    ff1 = backward_feed(grad, *attended1[4:], fed1, small1, choices[1], ff)
    ff1, out_got = after((ff1, out_got))
    ff1_core = beside_tensor(ff1[0])
    at1 = backward_attend(ff1[3], keys1, attended1, small1, choices[1], qo1, common)
    at1, ff1_core = after((at1, ff1_core))
    next1 = halo_back(at1[3])
    qo1_core = beside_tensor(at1[0])
    sums1 = [kept_sums(ff1_core, ff1[1], half) for half in range(2)]
    next1, sums1 = after((next1, sums1))
    across1a = across_tensor(sums1[0][0])
    kv1, grad1, grad1_low, gain1, key1 = backward_keys(
        x1, at1[2], next1, keys1, small1, at1[4], ff1[2], common
    )
    ff0 = backward_feed(grad1_low, *attended0[4:], fed0, small0, choices[0], ff)
    across1a, ff0, sums1, qo1_core = after((across1a, ff0, sums1, qo1_core))
    ff0_core = beside_tensor(ff0[0])
    across1b = across_tensor(sums1[1][0])
    at0 = backward_attend(ff0[3], keys0, attended0, small0, choices[0], qo0, common)
    pair1 = kept_sums(qo1_core, at1[1])
    at0, ff0_core, across1b, pair1, kv1 = after((at0, ff0_core, across1b, pair1, kv1))
    rest1 = core_half(packed(kv1, gain1, key1, ff1, at1))[0]
    next0 = halo_back(at0[3])
    qo0_core = beside_tensor(at0[0])
    sums0 = [kept_sums(ff0_core, ff0[1], 0), kept_sums(after(ff0_core, next0), ff0[1], 1)]
    across0a = across_tensor(sums0[0][0])
    pair1_across = across_tensor(after(pair1[0], sums0[0]))
    kv0, grad0, grad0_low, gain0, key0 = backward_keys(
        x0, at0[2], next0, keys0, small0, at0[4], ff0[2], common
    )
    grad_got = across_section(jnp.where(first, grad1_low, grad0_low))
    pair0 = kept_sums(qo0_core, at0[1])
    rest0 = core_half(packed(kv0, gain0, key0, ff0, at0))[0]
    full1 = [add(sums1[0][1], across1a), add(sums1[1][1], across1b)]
    pair1 = add(pair1[1], pair1_across)
    across0a, rest0, rest1, pair0, sums0, full1, grad_got = after(
        (across0a, rest0, rest1, pair0, sums0, full1, grad_got)
    )

    def swapped(zero, one):
        return add(jnp.where(first, zero, one), across_section(jnp.where(first, one, zero)))

    across0b = across_tensor(sums0[1][0])
    feed_a = swapped(add(sums0[0][1], across0a), full1[0])
    low0 = jnp.concatenate([pair0[0], rest0, rest1])
    across0b, feed_a, low0, sums0 = after((across0b, feed_a, low0, sums0))
    low0_across = across_tensor(low0)
    feed_b = swapped(add(sums0[1][1], across0b), full1[1])
    feed_a = summed_over_dp([feed_a])[0]
    low0_across, feed_a, feed_b = after((low0_across, feed_a, feed_b))
    size = low0.shape[0] - rest1.shape[0]
    low = swapped(
        add(jnp.concatenate([pair0[1], rest0]), low0_across[:size]),
        jnp.concatenate([pair1, add(rest1, low0_across[size:])]),
    )
    feed_b = summed_over_dp([feed_b])[0]
    feed_b, low = after((feed_b, low))
    pair_rows = pair0[0].shape[0]
    pair, rest = summed_over_dp(
        [side_by_side(low[None, :pair_rows]), side_by_side(low[None, pair_rows:])]
    )
    pair, rest = joined(pair).astype(F32), joined(rest)[0]
    beside = beside_tensor(rest)
    even = place % 2 == 0
    rest = jnp.concatenate(
        [jnp.where(even, rest, beside), jnp.where(even, beside, rest)]
    ).astype(F32)
    feed = jnp.stack([feed_a, feed_b]).astype(F32)

    def placed(zero, one, got):
        got = got.astype(F32)
        return jnp.stack([jnp.where(first, zero, got), jnp.where(first, got, one)])[None]

    return (
        placed(out0, out1, out_got),
        placed(grad0, grad1, grad_got),
        pair[:, :, :HD],
        rest[None, :local, :HD],
        rest[None, :local, HD:],
        pair[:, :, HD:],
        *[jnp.concatenate([feed[0, n], feed[1, n]], axis=1)[None] for n in range(3)],
        rest[local : local + 4, :local].T[None],
        rest[local + 4 : local + 6, :per_head].T[None],
    )


def solution(mesh):
    return jax.shard_map(
        body,
        mesh=mesh,
        in_specs=(
            P(None, ("dp", "tensor"), None),
            P(None, ("dp", "tensor"), None),
            P(None, "dp"),
            P("section", "dp", "tensor"),
            P("section", "dp", None),
            P("section", "dp", None),
            P("section", "dp", "tensor"),
            P("section", "dp", "tensor"),
            P("section", "dp", "tensor"),
            P("section", "dp", "tensor"),
            P("section", "dp", None),
            P("section", "dp", None),
        ),
        out_specs=(
            P("section", None, ("dp", "tensor"), None),
            P("section", None, ("dp", "tensor"), None),
            P("section", "dp", "tensor"),
            P("section", "dp", None),
            P("section", "dp", None),
            P("section", "dp", "tensor"),
            P("section", "dp", "tensor"),
            P("section", "dp", "tensor"),
            P("section", "dp", "tensor"),
            P("section", "dp", None),
            P("section", "dp", None),
        ),
        check_vma=False,
    )
```
